512 devices in a mesh: cfg: 2 (over core), band: 16 (over z_hi, x), seq: 16 (over y, z_lo).
Axes of the slice: x: 4, y: 4, z: 16 (z_hi: 4, z_lo: 4; z = z_hi * 4 + z_lo), core: 2. Of those that a mesh axis runs over, the one named last changes fastest.
Arguments:
- query: bfloat16 [2, 8192, 4096], P('cfg', 'seq', 'band'), may hold values from -8 to 8
- keys: bfloat16 [2, 8192, 4096], P('cfg', 'seq', 'band'), may hold values from -8 to 8
- values: bfloat16 [2, 8192, 4096], P('cfg', 'seq', 'band'), may hold values from -6 to 6
- lengths: int32 [1], replicated, may hold values from 6144 to 8192
- timestep: int32 [1], replicated, may hold values from 0 to 49
- latent: float32 [16, 32, 64, 16], P('seq', 'band'), may hold values from -6 to 6
- head_weight: bfloat16 [4096, 64], replicated, may hold values from -0.59765625 to 0.59765625
- conv_weight: bfloat16 [3, 3, 3, 16, 384], replicated, may hold values from -0.3125 to 0.3125
- conv_bias: float32 [384], replicated, may hold values from -4 to 4
- gain: float32 [384], replicated, may hold values from 0.1 to 1.9
Outputs:
- velocity: float32 [16, 32, 64, 16], P('seq', 'band', 'cfg')
- decoded: bfloat16 [16, 32, 64, 384], P('seq', 'band', 'cfg')
The draws below stay inside these ranges and needn't reach their ends.
All inputs are finite; a program needn't handle non-finite values.
Results may differ from the reference program's by a relative error of at most 0.017.
Values may be sent and summed in bfloat16 or wider, within the bound.
No kernel may reach another device: no remote copies, remote signals or barrier semaphores. Data moves between devices by JAX's collectives and lax.ppermute only.
A program may use at most 64 MiB of HBM per device.

```python
import math
import jax
import jax.numpy as jnp
from jax import lax

HEADS = 32
DH = 128
LCH = 16
VCH = 384
TC = 32
STEPS = 50
HD = 4096
PCH = 64
TROWS = 16
FRAMES = 16
SEQ_LEN = 8192
LROWS = 32
W = 64


def draw_query(key, part):
    key = jax.random.fold_in(key, 1)
    shape = (2, SEQ_LEN, HEADS * DH)
    base = jnp.clip(1.414 * jax.random.normal(key, shape, jnp.float32), -8.0, 8.0)
    return base.astype(jnp.bfloat16)


def draw_keys(key, part):
    key = jax.random.fold_in(key, 2)
    shape = (2, SEQ_LEN, HEADS * DH)
    base = jnp.clip(1.414 * jax.random.normal(key, shape, jnp.float32), -8.0, 8.0)
    return base.astype(jnp.bfloat16)


def block_levels(rng, shape, cuts, smallest, largest):
    factor_of = 1.0
    for dim, shards_of in cuts:
        heights = jax.random.uniform(jax.random.fold_in(jax.random.fold_in(rng, 6), dim), (shards_of,), jnp.float32, smallest / len(cuts), largest / len(cuts))
        factor_of = factor_of * jnp.repeat(jnp.exp(heights), shape[dim] // shards_of).reshape((-1,) + (1,) * (len(shape) - 1 - dim))
    return factor_of


def bell_draw(own_key, extent, scale, limit, cuts=(), kind=jnp.bfloat16):
    drawn = scale * jax.random.normal(own_key, extent, jnp.float32)
    if cuts:
        drawn = drawn * block_levels(own_key, extent, cuts, -0.22, 0.18)
    return jnp.clip(drawn, -limit, limit).astype(kind)


def setup_inputs(seed: int = 0) -> dict:
    key_list = jax.random.split(jax.random.key(seed), 11)
    query = draw_query(jax.random.fold_in(key_list[10], 71), 0)
    keys = draw_keys(jax.random.fold_in(key_list[10], 71), 0)
    values = bell_draw(key_list[2], (2, SEQ_LEN, HD), 1.0, 6.0, ((0, 2), (1, 16), (2, 16)))
    lengths = jax.random.randint(key_list[3], (1,), SEQ_LEN * 3 // 4, SEQ_LEN + 1).astype(jnp.int32)
    timestep = jax.random.randint(key_list[4], (1,), 0, STEPS).astype(jnp.int32)
    latent = bell_draw(key_list[5], (FRAMES, LROWS, W, LCH), 1.0, 6.0, ((0, 16), (1, 16)), jnp.float32)
    head_weight = bell_draw(key_list[6], (HD, PCH), 0.1, 0.59765625)
    conv_weight = bell_draw(key_list[7], (3, 3, 3, LCH, VCH), (27 * LCH) ** -0.5, 0.3125)
    conv_bias = bell_draw(key_list[8], (VCH,), 1.0, 4.0, (), jnp.float32)
    gain = jnp.clip(1.0 + 0.18 * jax.random.normal(key_list[9], (VCH,), jnp.float32), 0.1, 1.9)
    return dict(query=query, keys=keys, values=values, lengths=lengths, timestep=timestep, latent=latent, head_weight=head_weight, conv_weight=conv_weight, conv_bias=conv_bias, gain=gain)


GUIDE = 5.0
SHIFT_FACTOR = 5.0
NEG_FILL = -1e+30
EPSILON = 1e-06

def noise_level(timestep, total_steps):
    frac = 1.0 - timestep.astype(jnp.float32) / total_steps
    return SHIFT_FACTOR * frac / (1.0 + (SHIFT_FACTOR - 1.0) * frac)

def attend_rows(query, keys, values, length, head_size):
    scores = jnp.dot(query.astype(jnp.float32), jnp.transpose(keys.astype(jnp.float32))) / math.sqrt(head_size)
    valid = lax.broadcasted_iota(jnp.int32, (1, keys.shape[0]), 1) < length
    scores = jnp.where(valid, scores, NEG_FILL)
    top = lax.optimization_barrier(jnp.max(scores, axis=1, keepdims=True))
    weights = jnp.where(valid, jnp.exp(scores - top), 0.0)
    denom = lax.optimization_barrier(jnp.sum(weights, axis=1, keepdims=True))
    probs = weights.astype(jnp.bfloat16)
    mixed = jnp.dot(probs.astype(jnp.float32), values.astype(jnp.float32))
    return (mixed / denom).astype(jnp.bfloat16)

def decode_cells(window, frames, conv_weight, conv_bias, gain):
    rows = window.shape[1] - 2
    cols = window.shape[2] - 2
    chans = window.shape[3]
    slices = [window[a:a + frames, b:b + rows, c:c + cols, :] for a in range(3) for b in range(3) for c in range(3)]
    patches = jnp.concatenate(slices, 3).reshape(-1, 27 * chans)
    features = jnp.dot(patches, conv_weight.reshape(27 * chans, -1), preferred_element_type=jnp.float32) + conv_bias
    scaled = features * lax.rsqrt(lax.optimization_barrier(jnp.mean(features * features, axis=1, keepdims=True)) + EPSILON) * gain
    return jax.nn.silu(scaled).astype(jnp.bfloat16).reshape(frames, rows, cols, -1)

def reference(query, keys, values, lengths, timestep, latent, head_weight, conv_weight, conv_bias, gain):
    passes, seq_len, width = query.shape
    block = math.gcd(seq_len, 1024)
    nblocks = seq_len // block
    count = passes * HEADS * nblocks
    length = lengths[0]

    def one_block(index):
        pass_index = index // (HEADS * nblocks)
        head = index // nblocks % HEADS
        qblock = index % nblocks
        zero = jnp.zeros((), jnp.int32)
        qrows = lax.dynamic_slice(query, (pass_index, qblock * block, head * DH), (1, block, DH))[0]
        krows = lax.dynamic_slice(keys, (pass_index, zero, head * DH), (1, seq_len, DH))[0]
        vrows = lax.dynamic_slice(values, (pass_index, zero, head * DH), (1, seq_len, DH))[0]
        return attend_rows(qrows, krows, vrows, length, DH)
    outs = lax.map(one_block, jnp.arange(count, dtype=jnp.int32))
    attention = outs.reshape(passes, HEADS, nblocks, block, DH).transpose(0, 2, 3, 1, 4).reshape(-1, HEADS * DH)
    prediction = jnp.dot(attention, head_weight, preferred_element_type=jnp.float32)
    predicted = prediction.reshape(passes, FRAMES, TROWS, TC, 2, 2, LCH).transpose(0, 1, 2, 4, 3, 5, 6)
    predicted = predicted.reshape(passes, FRAMES, LROWS, W, LCH)
    velocity = predicted[1] + GUIDE * (predicted[0] - predicted[1])
    sigma = noise_level(timestep[0], STEPS)
    decoder_in = (latent - sigma * velocity).astype(jnp.bfloat16)
    window = jnp.pad(decoder_in, ((2, 0), (1, 1), (1, 1), (0, 0)))
    decoded = decode_cells(window, FRAMES, conv_weight, conv_bias, gain)
    return (velocity, decoded)
```

```python
import math

import jax
import jax.numpy as jnp
from jax import lax
from jax.experimental import pallas as pl
from jax.experimental.pallas import tpu as pltpu
from jax.sharding import Mesh
from jax.sharding import PartitionSpec as P

DH = 128
STEPS = 50
GUIDE = 5.0
SHIFT_FACTOR = 5.0
NEG_FILL = -1e30
EPSILON = 1e-06
SIDE = 4
TOK = 512
ROWS, TCOLS = 16, 32
CUT = 24
LOG2_SCALE = math.log2(math.e) / math.sqrt(DH)

VMEM = pl.BlockSpec(memory_space=pltpu.VMEM)
SMEM = pl.BlockSpec(memory_space=pltpu.SMEM)


def noise_level(timestep, total_steps):
    frac = 1.0 - timestep.astype(jnp.float32) / total_steps
    return SHIFT_FACTOR * frac / (1.0 + (SHIFT_FACTOR - 1.0) * frac)


def ring(steps):
    return [(i, (i + steps) % SIDE) for i in range(SIDE)]


def crossed(mask):
    return [(i, i ^ mask) for i in range(SIDE)]


def moved(steps):
    count = SIDE * SIDE
    return [(i, i + steps) for i in range(count) if 0 <= i + steps < count]


def attention_kernel(count_ref, slot_ref, *refs):
    q_refs, kv_refs = refs[0:4], refs[4:8]
    lse_ref, top_ref, acc_ref = refs[8:11]
    qs, ks, vs, denom = refs[11:]
    for j in range(4):
        qs[j] = q_refs[j][...]
        ks[j] = kv_refs[j][:, : 2 * DH]
        for h in range(2):
            vs[j, h] = jnp.transpose(kv_refs[j][:, (2 + h) * DH : (3 + h) * DH])

    def query_block(j, _):
        out = slot_ref[j]
        top_ref[out] = jnp.full((2, TOK), NEG_FILL, jnp.float32)
        denom[...] = jnp.zeros((2, TOK), jnp.float32)
        acc_ref[out] = jnp.zeros((2, DH, TOK), jnp.float32)

        def update(b, masked):
            for h in range(2):
                scores = lax.dot_general(
                    ks[b, :, h * DH : (h + 1) * DH],
                    qs[j, :, h * DH : (h + 1) * DH],
                    (((1,), (1,)), ((), ())),
                    preferred_element_type=jnp.float32,
                )
                if masked:
                    valid = lax.broadcasted_iota(jnp.int32, (TOK, TOK), 0) < count_ref[b]
                    scores = jnp.where(valid, scores, NEG_FILL)
                old = top_ref[out, h : h + 1]
                new = jnp.maximum(old, jnp.max(scores, axis=0, keepdims=True))
                weights = jnp.exp2((scores - new) * LOG2_SCALE)
                if masked:
                    weights = jnp.where(valid, weights, 0.0)
                factor = jnp.exp2((old - new) * LOG2_SCALE)
                top_ref[out, h : h + 1] = new
                denom[h : h + 1] = denom[h : h + 1] * factor + jnp.sum(
                    weights, axis=0, keepdims=True
                )
                acc_ref[out, h] = acc_ref[out, h] * factor + jnp.dot(
                    vs[b, h], weights.astype(jnp.bfloat16), preferred_element_type=jnp.float32
                )

        def key_block(b, _):
            count = count_ref[b]

            @pl.when(count >= TOK)
            def _():
                update(b, False)

            @pl.when((count > 0) & (count < TOK))
            def _():
                update(b, True)

            return 0

        lax.fori_loop(0, 4, key_block, 0)
        stat = top_ref[out] * LOG2_SCALE + jnp.log2(denom[...])
        for copy in range(4):
            lse_ref[copy, out] = stat
        return 0

    lax.fori_loop(0, 4, query_block, 0)


def attend(counts, slots, queries, key_values):
    f32 = jnp.float32
    return pl.pallas_call(
        attention_kernel,
        out_shape=(
            jax.ShapeDtypeStruct((4, 4, 2, TOK), f32),
            jax.ShapeDtypeStruct((4, 2, TOK), f32),
            jax.ShapeDtypeStruct((4, 2, DH, TOK), f32),
        ),
        in_specs=[SMEM, SMEM] + [VMEM] * 8,
        out_specs=(VMEM,) * 3,
        scratch_shapes=[
            pltpu.VMEM((4, TOK, 2 * DH), jnp.bfloat16),
            pltpu.VMEM((4, TOK, 2 * DH), jnp.bfloat16),
            pltpu.VMEM((4, 2, DH, TOK), jnp.bfloat16),
            pltpu.VMEM((2, TOK), f32),
        ],
        compiler_params=pltpu.CompilerParams(vmem_limit_bytes=40 * 2**20),
    )(counts, slots, *queries, *key_values)


def project_kernel(scale_ref, lse_ref, top_ref, acc_ref, weight_ref, out_ref):
    lane = lax.broadcasted_iota(jnp.int32, (ROWS, TCOLS, 128), 2)
    blank = jnp.zeros((1, TCOLS, 128), jnp.float32)
    for j in range(4):
        stats = [lse_ref[z, j] for z in range(4)]
        peak = jnp.maximum(jnp.maximum(stats[0], stats[1]), jnp.maximum(stats[2], stats[3]))
        total = sum(jnp.exp2(stat - peak) for stat in stats)
        factor = jnp.exp2(top_ref[j] * LOG2_SCALE - peak) / total * scale_ref[0]
        mixed = jnp.concatenate(
            [(acc_ref[j, h] * factor[h : h + 1]).astype(jnp.bfloat16) for h in range(2)], 0
        )
        values = lax.dot_general(
            mixed, weight_ref[...], (((0,), (0,)), ((), ())), preferred_element_type=jnp.float32
        ).reshape(ROWS, TCOLS, 128)
        above = jnp.concatenate([blank, values[:-1]], 0)
        below = jnp.concatenate([values[1:], blank], 0)
        window = jnp.where(lane < 32, above, jnp.where(lane < 96, values, below))
        for row in range(ROWS):
            for half in range(2):
                cut = window[row, half * 8 : half * 8 + CUT]
                out_ref[half * 4 + row % 4, row // 4 * 4 + j] = cut.astype(jnp.bfloat16)


def project(scale, lse, top, acc, weight):
    return pl.pallas_call(
        project_kernel,
        out_shape=jax.ShapeDtypeStruct((8, 16, CUT, 128), jnp.bfloat16),
        in_specs=[SMEM] + [VMEM] * 4,
        out_specs=VMEM,
        compiler_params=pltpu.CompilerParams(vmem_limit_bytes=32 * 2**20),
    )(scale, lse, top, acc, weight)


def decode_kernel(half_ref, own_ref, last_ref, older_ref, even_ref, odd_ref, bias_ref, gain_ref, out_ref):
    left = half_ref[0] == 0
    blank = jnp.zeros((1, 128), jnp.float32)
    even, odd = [], []
    for ref in (older_ref, last_ref, own_ref):
        block = ref[...].astype(jnp.float32)
        here = jnp.where(left, block[0:16], block[8:24])
        before = jnp.where(left, jnp.concatenate([blank, block[0:15]], 0), block[7:23])
        after = jnp.where(left, block[1:17], jnp.concatenate([block[9:24], blank], 0))
        rows = [
            jnp.concatenate([x, pltpu.roll(x, 96, 1)], 0).astype(jnp.bfloat16)
            for x in (before, here, after)
        ]
        even += rows[0:2]
        odd += rows[1:3]
    finished = []
    for parts, weight_ref in ((even, even_ref), (odd, odd_ref)):
        features = (
            jnp.dot(
                jnp.concatenate(parts, 1), weight_ref[...], preferred_element_type=jnp.float32
            )
            + bias_ref[...]
        )
        power = jnp.mean(features * features, axis=1, keepdims=True)
        scaled = features * lax.rsqrt(power + EPSILON) * gain_ref[...]
        finished.append((scaled / (1.0 + jnp.exp(-scaled))).astype(jnp.bfloat16))
    target = lax.broadcasted_iota(jnp.int32, (32, 32), 0)
    source = lax.broadcasted_iota(jnp.int32, (32, 32), 1)
    order = ((target & 1) * 16 + (target >> 1) == source).astype(jnp.float32).astype(jnp.bfloat16)
    for row in range(2):
        both = jnp.concatenate([x[row * 16 : row * 16 + 16] for x in finished], 0)
        out_ref[row] = jnp.dot(order, both, preferred_element_type=jnp.float32).astype(jnp.bfloat16)


def decode(half, own, last, older, even, odd, bias, gain):
    chans = bias.shape[1]
    return pl.pallas_call(
        decode_kernel,
        out_shape=jax.ShapeDtypeStruct((2, 32, chans), jnp.bfloat16),
        in_specs=[SMEM] + [VMEM] * 7,
        out_specs=VMEM,
        compiler_params=pltpu.CompilerParams(vmem_limit_bytes=32 * 2**20),
    )(half, own, last, older, even, odd, bias, gain)


def conv_matrices(conv_weight):
    taps, _, _, chans, outs = conv_weight.shape
    padded = jnp.pad(conv_weight, ((0, 0), (0, 1), (0, 0), (0, 0), (0, 0)))
    blank = jnp.zeros((taps, 4, 1, chans, outs), conv_weight.dtype)
    both = []
    for parts in ([blank, padded], [padded, blank]):
        spread = jnp.concatenate(parts, 2).reshape(taps, 4, 2, 2, chans, outs)
        both.append(spread.transpose(0, 2, 1, 3, 4, 5).reshape(taps * 16 * chans, outs))
    return both


def local(
    query, keys, values, lengths, timestep, latent, head_weight, conv_weight, conv_bias, gain
):
    cfg, zh, x = lax.axis_index("cfg"), lax.axis_index("zh"), lax.axis_index("x")
    y, zl = lax.axis_index("y"), lax.axis_index("zl")
    seq, band = ("y", "zl"), ("zh", "x")

    own = jnp.concatenate([keys[0], values[0]], 1)
    key_values = [own] + [lax.ppermute(own, "y", ring(d)) for d in (1, 3, 2)]
    queries = [query[0]] + [lax.ppermute(query[0], "zl", crossed(m)) for m in (1, 2, 3)]
    block = jnp.stack([((y - d) % SIDE) * SIDE + zl for d in (0, 1, 3, 2)])
    counts = jnp.clip(lengths[0] - block * TOK, 0, TOK).astype(jnp.int32)
    slots = jnp.stack([zl ^ m for m in range(4)]).astype(jnp.int32)

    rows = latent[0]
    above = lax.ppermute(rows[1:2], band, moved(1))
    below = lax.ppermute(rows[0:1], band, moved(-1))
    grid = jnp.concatenate([above, rows, below], 0).reshape(4, TCOLS, 2, -1)
    grid = grid.transpose(1, 0, 2, 3).reshape(TCOLS, 128)
    latent_window = lax.dynamic_slice_in_dim(grid, cfg * 8, CUT, 0)
    even, odd = conv_matrices(conv_weight)
    part = lax.dynamic_slice_in_dim(head_weight, (zh * SIDE + x) * 2 * DH, 2 * DH, 0)
    weight = jnp.concatenate([part[:, 32:], part, part[:, :32]], 1)
    scale = jnp.where(cfg == 0, GUIDE, 1.0 - GUIDE).astype(jnp.float32).reshape(1)

    lse, top, acc = attend(counts, slots, queries, key_values)
    lse = lax.all_to_all(lse, "zl", 0, 0, tiled=True)
    shares = project(scale, lse, top, acc, weight)
    shares = lax.all_to_all(shares, ("cfg", "x"), 0, 0, tiled=True)
    shares = jnp.sum(shares.astype(jnp.float32), 0).astype(jnp.bfloat16)
    shares = lax.all_to_all(shares, ("zh", "zl"), 0, 0, tiled=True)
    window = jnp.sum(shares.astype(jnp.float32), 0)

    sigma = noise_level(timestep[0], STEPS)
    current = (latent_window - sigma * window).astype(jnp.bfloat16)
    last = lax.ppermute(current, seq, moved(1))
    older = lax.ppermute(current, seq, moved(2))
    mine = lax.dynamic_slice_in_dim(window, cfg * 8, TCOLS // 2, 0)[:, 32:96]
    velocity = mine.reshape(TCOLS // 2, 2, 2, -1).transpose(1, 0, 2, 3).reshape(1, 2, TCOLS, -1)
    decoded = decode(
        cfg.astype(jnp.int32).reshape(1),
        current,
        last,
        older,
        even,
        odd,
        conv_bias.reshape(1, -1),
        gain.reshape(1, -1),
    )
    return (velocity, decoded[None])


def solution(mesh):
    split = Mesh(
        mesh.devices.reshape(2, SIDE, SIDE, SIDE, SIDE), ("cfg", "zh", "x", "y", "zl")
    )
    seq, band = ("y", "zl"), ("zh", "x")
    tokens = P("cfg", seq, band)
    return jax.shard_map(
        local,
        mesh=split,
        in_specs=(
            tokens,
            tokens,
            tokens,
            P(),
            P(),
            P(seq, band, None, None),
            P(),
            P(),
            P(),
            P(),
        ),
        out_specs=(P(seq, band, "cfg", None), P(seq, band, "cfg", None)),
        check_vma=False,
    )
```

```python
import functools
import math

import jax
import jax.numpy as jnp
from jax import lax
from jax.experimental import pallas as pl
from jax.experimental.pallas import tpu as pltpu
from jax.sharding import Mesh
from jax.sharding import PartitionSpec as P

DH = 128
STEPS = 50
GUIDE = 5.0
SHIFT_FACTOR = 5.0
NEG_FILL = -1e30
EPSILON = 1e-06
SIDE = 4
TOK = 512
ROWS, TCOLS = 16, 32
CUT = 24
LOG2_SCALE = math.log2(math.e) / math.sqrt(DH)

VMEM = pl.BlockSpec(memory_space=pltpu.VMEM)
SMEM = pl.BlockSpec(memory_space=pltpu.SMEM)
ANY = pl.BlockSpec(memory_space=pl.ANY)


def noise_level(timestep, total_steps):
    frac = 1.0 - timestep.astype(jnp.float32) / total_steps
    return SHIFT_FACTOR * frac / (1.0 + (SHIFT_FACTOR - 1.0) * frac)


def ring(steps):
    return [(i, (i + steps) % SIDE) for i in range(SIDE)]


def crossed(mask):
    return [(i, i ^ mask) for i in range(SIDE)]


def moved(steps):
    count = SIDE * SIDE
    return [(i, i + steps) for i in range(count) if 0 <= i + steps < count]


def attention_kernel(count_ref, slot_ref, *refs, parts, nq, nk, nx, last):
    refs = list(refs)
    if not parts and nx:
        carried_ref = refs.pop(nq + nk)
        refs.pop(nq + nk + 3)[...] = carried_ref[...]
        nx = 0
    q_refs, kv_refs = refs[:nq], refs[nq : nq + nk]
    states = [refs[nq + nk + 3 * i : nq + nk + 3 * i + 3] for i in range(len(parts))]
    at = nq + nk + 3 * len(parts) + nx
    if last:
        lse_ref, top_ref, acc_ref = refs[at : at + 3]
        qs, kvs, vs, scores, sems, denom = refs[at + 3 :]
    else:
        top_ref, denom, acc_ref = refs[at : at + 3]
        qs, kvs, vs, scores, sems = refs[at + 3 :]
    copies = [pltpu.make_async_copy(q_refs[j], qs.at[j], sems.at[j]) for j in range(nq)]
    copies += [pltpu.make_async_copy(kv_refs[b], kvs.at[b], sems.at[nq + b]) for b in range(nk)]
    for copy in copies:
        copy.start()
    if not parts:
        for j in range(nq):
            top_ref[j] = jnp.full((2, TOK), NEG_FILL, jnp.float32)
            denom[j] = jnp.zeros((2, TOK), jnp.float32)
            acc_ref[j] = jnp.zeros((2, DH, TOK), jnp.float32)
    j = 0
    for size, (top_in, denom_in, acc_in) in zip(parts, states):
        for i in range(size):
            out = slot_ref[j] if last else j
            top_ref[out] = top_in[i]
            denom[out] = denom_in[i]
            acc_ref[out] = acc_in[i]
            j += 1
    for copy in copies:
        copy.wait()
    for b in range(nk):
        for h in range(2):
            vs[b, h, :DH] = jnp.transpose(kvs[b, :, (2 + h) * DH : (3 + h) * DH])
            vs[b, h, DH:] = jnp.ones((16, TOK), jnp.bfloat16)

    def scored(j, b, h):
        return lax.dot_general(
            kvs[b, :, h * DH : (h + 1) * DH],
            qs[j, :, h * DH : (h + 1) * DH],
            (((1,), (1,)), ((), ())),
            preferred_element_type=jnp.float32,
        )

    def folded(out, b, h, score, masked):
        if masked:
            valid = lax.broadcasted_iota(jnp.int32, (TOK, TOK), 0) < count_ref[b]
            score = jnp.where(valid, score, NEG_FILL)
        old = top_ref[out, h : h + 1]
        new = jnp.maximum(old, jnp.max(score, axis=0, keepdims=True))
        weights = jnp.exp2((score - new) * LOG2_SCALE)
        if masked:
            weights = jnp.where(valid, weights, 0.0)
        factor = jnp.exp2((old - new) * LOG2_SCALE)
        top_ref[out, h : h + 1] = new
        mixed = jnp.dot(vs[b, h], weights.astype(jnp.bfloat16), preferred_element_type=jnp.float32)
        denom[out, h : h + 1] = denom[out, h : h + 1] * factor + mixed[DH : DH + 1]
        acc_ref[out, h] = acc_ref[out, h] * factor + mixed[:DH]

    def step(t, _):
        j, b = lax.div(t, nk), lax.rem(t, nk)
        later = jnp.minimum(t + 1, nq * nk - 1)
        next_j, next_b = lax.div(later, nk), lax.rem(later, nk)
        out = slot_ref[j] if last else j
        count = count_ref[b]

        def update(masked):
            scores[1] = scored(j, b, 1)
            folded(out, b, 0, scores[0], masked)
            scores[0] = scored(next_j, next_b, 0)
            folded(out, b, 1, scores[1], masked)

        @pl.when(count >= TOK)
        def _():
            update(False)

        @pl.when((count > 0) & (count < TOK))
        def _():
            update(True)

        @pl.when(count <= 0)
        def _():
            scores[0] = scored(next_j, next_b, 0)

        return 0

    scores[0] = scored(0, 0, 0)
    lax.fori_loop(0, nq * nk, step, 0)
    if last:
        for out in range(nq):
            stat = top_ref[out] * LOG2_SCALE + jnp.log2(denom[out])
            for copy in range(4):
                lse_ref[copy, out] = stat


def attend(counts, slots, queries, key_values, states=(), extras=(), last=False):
    f32, bf16 = jnp.float32, jnp.bfloat16
    nq, nk = len(queries), len(key_values)
    parts = tuple(state[0].shape[0] for state in states)
    stat = jax.ShapeDtypeStruct((nq, 2, TOK), f32)
    acc = jax.ShapeDtypeStruct((nq, 2, DH, TOK), f32)
    first = jax.ShapeDtypeStruct((4, nq, 2, TOK), f32) if last else stat
    carried = () if parts else tuple(jax.ShapeDtypeStruct(x.shape, x.dtype) for x in extras)
    scratch = [
        pltpu.VMEM((nq, TOK, 2 * DH), bf16),
        pltpu.VMEM((nk, TOK, 4 * DH), bf16),
        pltpu.VMEM((nk, 2, DH + 16, TOK), bf16),
        pltpu.VMEM((2, TOK, TOK), f32),
        pltpu.SemaphoreType.DMA((nq + nk,)),
    ]
    if last:
        scratch.append(pltpu.VMEM((nq, 2, TOK), f32))
    work = nq * nk * 2 * TOK * TOK
    return pl.pallas_call(
        functools.partial(
            attention_kernel, parts=parts, nq=nq, nk=nk, nx=len(extras), last=last
        ),
        out_shape=(first, stat, acc) + carried,
        in_specs=[SMEM, SMEM]
        + [ANY] * (nq + nk)
        + [VMEM] * (3 * len(parts))
        + [ANY if parts else VMEM] * len(extras),
        out_specs=(VMEM,) * (3 + len(carried)),
        scratch_shapes=scratch,
        compiler_params=pltpu.CompilerParams(vmem_limit_bytes=20 * 2**20),
        cost_estimate=pl.CostEstimate(
            flops=work * DH * 4, transcendentals=work, bytes_accessed=(nq + 2 * nk) * TOK * 4 * DH
        ),
    )(counts, slots, *queries, *key_values, *(x for state in states for x in state), *extras)


def project_kernel(scale_ref, lse_ref, top_ref, acc_ref, weight_ref, out_ref):
    lane = lax.broadcasted_iota(jnp.int32, (ROWS, TCOLS, 128), 2)
    blank = jnp.zeros((1, TCOLS, 128), jnp.float32)
    for j in range(4):
        stats = [lse_ref[z, j] for z in range(4)]
        peak = jnp.maximum(jnp.maximum(stats[0], stats[1]), jnp.maximum(stats[2], stats[3]))
        total = sum(jnp.exp2(stat - peak) for stat in stats)
        factor = jnp.exp2(top_ref[j] * LOG2_SCALE - peak) / total * scale_ref[0]
        mixed = jnp.concatenate(
            [(acc_ref[j, h] * factor[h : h + 1]).astype(jnp.bfloat16) for h in range(2)], 0
        )
        values = lax.dot_general(
            mixed, weight_ref[...], (((0,), (0,)), ((), ())), preferred_element_type=jnp.float32
        ).reshape(ROWS, TCOLS, 128)
        above = jnp.concatenate([blank, values[:-1]], 0)
        below = jnp.concatenate([values[1:], blank], 0)
        window = jnp.where(lane < 32, above, jnp.where(lane < 96, values, below))
        for row in range(ROWS):
            for half in range(2):
                cut = window[row, half * 8 : half * 8 + CUT]
                out_ref[half * 4 + row % 4, row // 4 * 4 + j] = cut.astype(jnp.bfloat16)


def project(scale, lse, top, acc, weight):
    return pl.pallas_call(
        project_kernel,
        out_shape=jax.ShapeDtypeStruct((8, 16, CUT, 128), jnp.bfloat16),
        in_specs=[SMEM] + [VMEM] * 4,
        out_specs=VMEM,
        compiler_params=pltpu.CompilerParams(vmem_limit_bytes=32 * 2**20),
    )(scale, lse, top, acc, weight)


def added_kernel(shares_ref, out_ref):
    total = shares_ref[0].astype(jnp.float32)
    for source in range(1, shares_ref.shape[0]):
        total += shares_ref[source].astype(jnp.float32)
    out_ref[...] = total.astype(jnp.bfloat16)


def added(shares):
    return pl.pallas_call(
        added_kernel,
        out_shape=jax.ShapeDtypeStruct(shares.shape[1:], shares.dtype),
        in_specs=[VMEM],
        out_specs=VMEM,
    )(shares)


def denoised_kernel(sigma_ref, shares_ref, latent_ref, current_ref, window_ref):
    total = shares_ref[0].astype(jnp.float32)
    for source in range(1, shares_ref.shape[0]):
        total += shares_ref[source].astype(jnp.float32)
    window_ref[...] = total
    current_ref[...] = (latent_ref[...] - sigma_ref[0] * total).astype(jnp.bfloat16)


def denoised(sigma, shares, latent):
    return pl.pallas_call(
        denoised_kernel,
        out_shape=(
            jax.ShapeDtypeStruct(latent.shape, jnp.bfloat16),
            jax.ShapeDtypeStruct(latent.shape, jnp.float32),
        ),
        in_specs=[SMEM, VMEM, VMEM],
        out_specs=(VMEM, VMEM),
    )(sigma, shares, latent)


def decode_kernel(half_ref, own_ref, last_ref, older_ref, even_ref, odd_ref, bias_ref, gain_ref, out_ref):
    left = half_ref[0] == 0
    blank = jnp.zeros((1, 128), jnp.float32)
    even, odd = [], []
    for ref in (older_ref, last_ref, own_ref):
        block = ref[...].astype(jnp.float32)
        here = jnp.where(left, block[0:16], block[8:24])
        before = jnp.where(left, jnp.concatenate([blank, block[0:15]], 0), block[7:23])
        after = jnp.where(left, block[1:17], jnp.concatenate([block[9:24], blank], 0))
        rows = [
            jnp.concatenate([x, pltpu.roll(x, 96, 1)], 0).astype(jnp.bfloat16)
            for x in (before, here, after)
        ]
        even += rows[0:2]
        odd += rows[1:3]
    finished = []
    for parts, weight_ref in ((even, even_ref), (odd, odd_ref)):
        features = (
            jnp.dot(
                jnp.concatenate(parts, 1), weight_ref[...], preferred_element_type=jnp.float32
            )
            + bias_ref[...]
        )
        power = jnp.mean(features * features, axis=1, keepdims=True)
        scaled = features * lax.rsqrt(power + EPSILON) * gain_ref[...]
        finished.append((scaled / (1.0 + jnp.exp(-scaled))).astype(jnp.bfloat16))
    target = lax.broadcasted_iota(jnp.int32, (32, 32), 0)
    source = lax.broadcasted_iota(jnp.int32, (32, 32), 1)
    order = ((target & 1) * 16 + (target >> 1) == source).astype(jnp.float32).astype(jnp.bfloat16)
    for row in range(2):
        both = jnp.concatenate([x[row * 16 : row * 16 + 16] for x in finished], 0)
        out_ref[row] = jnp.dot(order, both, preferred_element_type=jnp.float32).astype(jnp.bfloat16)


def decode(half, own, last, older, even, odd, bias, gain):
    chans = bias.shape[1]
    return pl.pallas_call(
        decode_kernel,
        out_shape=jax.ShapeDtypeStruct((2, 32, chans), jnp.bfloat16),
        in_specs=[SMEM] + [VMEM] * 7,
        out_specs=VMEM,
        compiler_params=pltpu.CompilerParams(vmem_limit_bytes=32 * 2**20),
    )(half, own, last, older, even, odd, bias, gain)


def conv_matrices(conv_weight):
    taps, _, _, chans, outs = conv_weight.shape
    padded = jnp.pad(conv_weight, ((0, 0), (0, 1), (0, 0), (0, 0), (0, 0)))
    blank = jnp.zeros((taps, 4, 1, chans, outs), conv_weight.dtype)
    both = []
    for parts in ([blank, padded], [padded, blank]):
        spread = jnp.concatenate(parts, 2).reshape(taps, 4, 2, 2, chans, outs)
        both.append(spread.transpose(0, 2, 1, 3, 4, 5).reshape(taps * 16 * chans, outs))
    return both


def local(
    query, keys, values, lengths, timestep, latent, head_weight, conv_weight, conv_bias, gain
):
    cfg, zh, x = lax.axis_index("cfg"), lax.axis_index("zh"), lax.axis_index("x")
    y, zl = lax.axis_index("y"), lax.axis_index("zl")
    seq, band = ("y", "zl"), ("zh", "x")

    own = jnp.concatenate([keys[0], values[0]], 1)
    key_values = [own] + [lax.ppermute(own, "y", ring(d)) for d in (1, 3, 2)]
    queries = [query[0]] + [lax.ppermute(query[0], "zl", crossed(m)) for m in (1, 2, 3)]
    block = jnp.stack([((y - d) % SIDE) * SIDE + zl for d in (0, 1, 3, 2)])
    counts = jnp.clip(lengths[0] - block * TOK, 0, TOK).astype(jnp.int32)
    slots = jnp.stack([zl ^ m for m in range(4)]).astype(jnp.int32)

    *near, rows = attend(
        counts[:3], slots, queries[:2], key_values[:3], extras=(latent.reshape(2, 8, 128),)
    )
    far = attend(counts[:3], slots, queries[2:], key_values[:3])
    above = lax.ppermute(rows[1:2], band, moved(1))
    below = lax.ppermute(rows[0:1], band, moved(-1))
    grid = jnp.concatenate([above, rows, below], 0).reshape(4, TCOLS, 2, -1)
    grid = grid.transpose(1, 0, 2, 3).reshape(TCOLS, 128)
    latent_window = lax.dynamic_slice_in_dim(grid, cfg * 8, CUT, 0)
    even, odd = conv_matrices(conv_weight)
    part = lax.dynamic_slice_in_dim(head_weight, (zh * SIDE + x) * 2 * DH, 2 * DH, 0)
    weight = jnp.concatenate([part[:, 32:], part, part[:, :32]], 1)
    scale = jnp.where(cfg == 0, GUIDE, 1.0 - GUIDE).astype(jnp.float32).reshape(1)

    lse, top, acc = attend(
        counts[3:],
        slots,
        queries,
        key_values[3:],
        (near, far),
        (latent_window, even, odd, weight),
        last=True,
    )
    lse = lax.all_to_all(lse, "zl", 0, 0, tiled=True)
    shares = project(scale, lse, top, acc, weight)
    shares = lax.all_to_all(shares, ("cfg", "x"), 0, 0, tiled=True)
    shares = lax.all_to_all(added(shares), ("zh", "zl"), 0, 0, tiled=True)
    sigma = noise_level(timestep, STEPS)
    current, window = denoised(sigma, shares, latent_window)
    last = lax.ppermute(current, seq, moved(1))
    older = lax.ppermute(current, seq, moved(2))
    mine = lax.dynamic_slice_in_dim(window, cfg * 8, TCOLS // 2, 0)[:, 32:96]
    velocity = mine.reshape(TCOLS // 2, 2, 2, -1).transpose(1, 0, 2, 3).reshape(1, 2, TCOLS, -1)
    decoded = decode(
        cfg.astype(jnp.int32).reshape(1),
        current,
        last,
        older,
        even,
        odd,
        conv_bias.reshape(1, -1),
        gain.reshape(1, -1),
    )
    return (velocity, decoded[None])


def solution(mesh):
    split = Mesh(
        mesh.devices.reshape(2, SIDE, SIDE, SIDE, SIDE), ("cfg", "zh", "x", "y", "zl")
    )
    seq, band = ("y", "zl"), ("zh", "x")
    tokens = P("cfg", seq, band)
    return jax.shard_map(
        local,
        mesh=split,
        in_specs=(
            tokens,
            tokens,
            tokens,
            P(),
            P(),
            P(seq, band, None, None),
            P(),
            P(),
            P(),
            P(),
        ),
        out_specs=(P(seq, band, "cfg", None), P(seq, band, "cfg", None)),
        check_vma=False,
    )
```

```python
import functools
import math

import jax
import jax.numpy as jnp
from jax import lax
from jax.experimental import pallas as pl
from jax.experimental.pallas import tpu as pltpu
from jax.sharding import Mesh
from jax.sharding import PartitionSpec as P

DH = 128
STEPS = 50
GUIDE = 5.0
SHIFT_FACTOR = 5.0
NEG_FILL = -1e30
EPSILON = 1e-06
SIDE = 4
TOK = 512
ROWS, TCOLS = 16, 32
CUT = 24
LOG2_SCALE = math.log2(math.e) / math.sqrt(DH)

VMEM = pl.BlockSpec(memory_space=pltpu.VMEM)
SMEM = pl.BlockSpec(memory_space=pltpu.SMEM)
HBM = pl.BlockSpec(memory_space=pltpu.HBM)
ANY = pl.BlockSpec(memory_space=pl.ANY)


def in_hbm(value):
    return pltpu.with_memory_space_constraint(value, pltpu.HBM)


def noise_level(timestep, total_steps):
    frac = 1.0 - timestep.astype(jnp.float32) / total_steps
    return SHIFT_FACTOR * frac / (1.0 + (SHIFT_FACTOR - 1.0) * frac)


def ring(steps):
    return [(i, (i + steps) % SIDE) for i in range(SIDE)]


def crossed(mask):
    return [(i, i ^ mask) for i in range(SIDE)]


def moved(steps):
    count = SIDE * SIDE
    return [(i, i + steps) for i in range(count) if 0 <= i + steps < count]


def attention_kernel(count_ref, slot_ref, *refs, nq, nk, skip, parts, nx, last):
    refs = list(refs)
    whole = 3
    at = nq + nk + (nk > whole)
    q_refs, kv_refs = refs[:nq], refs[nq:at]
    if parts:
        top_in, denom_in, acc_in = refs[at : at + 3]
        at += 3
    at += nx
    if last:
        lse_ref, top_ref, acc_out = refs[at : at + 3]
        qs, kvs, vs, scores, sems, denom, acc_ref = refs[at + 3 :]
    else:
        top_ref, denom, acc_out = refs[at : at + 3]
        qs, kvs, vs, scores, sems, acc_ref = refs[at + 3 :]
    slots = [slot_ref[j] if last else j for j in range(nq)]
    copies = [pltpu.make_async_copy(q_refs[j], qs.at[j], sems.at[j]) for j in range(nq)]
    for b, kv_ref in enumerate(kv_refs):
        place = kvs.at[b] if b < whole else kvs.at[whole, :, pl.ds((b - whole) * 2 * DH, 2 * DH)]
        copies.append(pltpu.make_async_copy(kv_ref, place, sems.at[nq + b]))
    for copy in copies:
        copy.start()
    carried = []
    for j in range(parts):
        copy = pltpu.make_async_copy(acc_in.at[j], acc_ref.at[slots[j]], sems.at[len(copies) + j])
        copy.start()
        carried.append(copy)
        top_ref[slots[j]] = top_in[j]
        denom[slots[j]] = denom_in[j]
    for j in range(parts, nq):
        top_ref[slots[j]] = jnp.full((2, TOK), NEG_FILL, jnp.float32)
        denom[slots[j]] = jnp.zeros((2, TOK), jnp.float32)
        acc_ref[slots[j]] = jnp.zeros((2, DH, TOK), jnp.float32)
    for copy in copies + carried:
        copy.wait()
    for b in range(nk):
        for h in range(2):
            vs[b, h, :DH] = jnp.transpose(kvs[b, :, (2 + h) * DH : (3 + h) * DH])
            vs[b, h, DH:] = jnp.ones((16, TOK), jnp.bfloat16)

    def scored(j, b, h):
        return lax.dot_general(
            kvs[b, :, h * DH : (h + 1) * DH],
            qs[j, :, h * DH : (h + 1) * DH],
            (((1,), (1,)), ((), ())),
            preferred_element_type=jnp.float32,
        )

    def folded(out, b, h, score, masked):
        if masked:
            valid = lax.broadcasted_iota(jnp.int32, (TOK, TOK), 0) < count_ref[b]
            score = jnp.where(valid, score, NEG_FILL)
        old = top_ref[out, h : h + 1]
        new = jnp.maximum(old, jnp.max(score, axis=0, keepdims=True))
        weights = jnp.exp2((score - new) * LOG2_SCALE)
        if masked:
            weights = jnp.where(valid, weights, 0.0)
        factor = jnp.exp2((old - new) * LOG2_SCALE)
        top_ref[out, h : h + 1] = new
        mixed = jnp.dot(vs[b, h], weights.astype(jnp.bfloat16), preferred_element_type=jnp.float32)
        denom[out, h : h + 1] = denom[out, h : h + 1] * factor + mixed[DH : DH + 1]
        acc_ref[out, h] = acc_ref[out, h] * factor + mixed[:DH]

    done = parts * (nk - skip) if parts else 0
    total = done + (nq - parts) * nk

    def tile(t):
        if not parts:
            return lax.div(t, nk), lax.rem(t, nk)
        fresh = t >= done
        rest = nk - skip
        j = jnp.where(fresh, parts + lax.div(t - done, nk), lax.div(t, rest))
        b = jnp.where(fresh, lax.rem(t - done, nk), skip + lax.rem(t, rest))
        return j, b

    def step(t, _):
        j, b = tile(t)
        next_j, next_b = tile(jnp.minimum(t + 1, total - 1))
        out = slot_ref[j] if last else j
        count = count_ref[b]

        def update(masked):
            scores[1] = scored(j, b, 1)
            folded(out, b, 0, scores[0], masked)
            scores[0] = scored(next_j, next_b, 0)
            folded(out, b, 1, scores[1], masked)

        @pl.when(count >= TOK)
        def _():
            update(False)

        @pl.when((count > 0) & (count < TOK))
        def _():
            update(True)

        @pl.when(count <= 0)
        def _():
            scores[0] = scored(next_j, next_b, 0)

        return 0

    scores[0] = scored(0, skip if parts else 0, 0)
    lax.fori_loop(0, total, step, 0)
    copy = pltpu.make_async_copy(acc_ref, acc_out, sems.at[0])
    copy.start()
    if last:
        for out in range(nq):
            stat = top_ref[out] * LOG2_SCALE + jnp.log2(denom[out])
            for place in range(4):
                lse_ref[place, out] = stat
    copy.wait()


def attend(counts, slots, queries, key_values, state=(), skip=0, extras=(), last=False):
    f32, bf16 = jnp.float32, jnp.bfloat16
    nq, nk = len(queries), min(len(key_values), 4)
    parts = state[0].shape[0] if state else 0
    stat = jax.ShapeDtypeStruct((nq, 2, TOK), f32)
    acc = pltpu.HBM((nq, 2, DH, TOK), f32)
    first = jax.ShapeDtypeStruct((4, nq, 2, TOK), f32) if last else stat
    scratch = [
        pltpu.VMEM((nq, TOK, 2 * DH), bf16),
        pltpu.VMEM((nk, TOK, 4 * DH), bf16),
        pltpu.VMEM((nk, 2, DH + 16, TOK), bf16),
        pltpu.VMEM((2, TOK, TOK), f32),
        pltpu.SemaphoreType.DMA((nq + len(key_values) + parts,)),
    ]
    if last:
        scratch.append(pltpu.VMEM((nq, 2, TOK), f32))
    scratch.append(pltpu.VMEM((nq, 2, DH, TOK), f32))
    tiles = nq * nk - parts * skip
    work = tiles * 2 * TOK * TOK
    return pl.pallas_call(
        functools.partial(
            attention_kernel, nq=nq, nk=nk, skip=skip, parts=parts, nx=len(extras), last=last
        ),
        out_shape=(first, stat, acc),
        in_specs=[SMEM, SMEM]
        + [HBM] * (nq + len(key_values))
        + ([VMEM, VMEM, HBM] if parts else [])
        + [ANY] * len(extras),
        out_specs=(VMEM, VMEM, HBM),
        scratch_shapes=scratch,
        compiler_params=pltpu.CompilerParams(vmem_limit_bytes=24 * 2**20),
        cost_estimate=pl.CostEstimate(
            flops=work * DH * 4, transcendentals=work, bytes_accessed=(nq + 2 * nk) * TOK * 4 * DH
        ),
    )(
        counts,
        slots,
        *(in_hbm(x) for x in (*queries, *key_values)),
        *(in_hbm(x) if x.ndim == 4 else x for x in state),
        *extras,
    )


def project_kernel(
    scale_ref, place_ref, lse_ref, top_ref, acc_hbm, weight_ref, latent_ref, out_ref, acc_ref, sems
):
    copies = [pltpu.make_async_copy(acc_hbm.at[j], acc_ref.at[j], sems.at[j]) for j in range(4)]
    for copy in copies:
        copy.start()
    lane = lax.broadcasted_iota(jnp.int32, (ROWS, TCOLS, 128), 2)
    blank = jnp.zeros((1, TCOLS, 128), jnp.float32)
    for j in range(4):
        stats = [lse_ref[z, j] for z in range(4)]
        peak = jnp.maximum(jnp.maximum(stats[0], stats[1]), jnp.maximum(stats[2], stats[3]))
        total = sum(jnp.exp2(stat - peak) for stat in stats)
        factor = jnp.exp2(top_ref[j] * LOG2_SCALE - peak) / total * scale_ref[0]
        copies[j].wait()
        mixed = jnp.concatenate(
            [(acc_ref[j, h] * factor[h : h + 1]).astype(jnp.bfloat16) for h in range(2)], 0
        )
        values = lax.dot_general(
            mixed, weight_ref[...], (((0,), (0,)), ((), ())), preferred_element_type=jnp.float32
        ).reshape(ROWS, TCOLS, 128)
        above = jnp.concatenate([blank, values[:-1]], 0)
        below = jnp.concatenate([values[1:], blank], 0)
        window = jnp.where(lane < 32, above, jnp.where(lane < 96, values, below))
        for row in range(ROWS):
            for half in range(2):
                cut = window[row, half * 8 : half * 8 + CUT]
                out_ref[half * 4 + row % 4, row // 4 * 4 + j] = cut.astype(jnp.bfloat16)
    band, zl = place_ref[0], place_ref[1]
    edge = pltpu.roll(latent_ref[...], 64, 1) * scale_ref[1]
    lane = lax.broadcasted_iota(jnp.int32, (TCOLS, 128), 1)
    for target, part in ((band + 1, lane < 32), (band - 1, lane >= 96)):

        @pl.when((target >= 0) & (target < ROWS))
        def _():
            sent = jnp.where(part, edge, 0.0)
            for half in range(2):
                at = (half * 4 + (target & 3), (target >> 2) * 4 + zl)
                out_ref[at] = (
                    out_ref[at].astype(jnp.float32) + sent[half * 8 : half * 8 + CUT]
                ).astype(jnp.bfloat16)


def project(scale, place, lse, top, acc, weight, latent):
    return pl.pallas_call(
        project_kernel,
        out_shape=jax.ShapeDtypeStruct((8, 16, CUT, 128), jnp.bfloat16),
        in_specs=[SMEM, SMEM, VMEM, VMEM, HBM, VMEM, VMEM],
        out_specs=VMEM,
        scratch_shapes=[
            pltpu.VMEM((4, 2, DH, TOK), jnp.float32),
            pltpu.SemaphoreType.DMA((4,)),
        ],
        compiler_params=pltpu.CompilerParams(vmem_limit_bytes=32 * 2**20),
    )(scale, place, lse, top, in_hbm(acc), weight, latent)


def decode_kernel(half_ref, own_ref, last_ref, older_ref, even_ref, odd_ref, bias_ref, gain_ref, out_ref):
    left = half_ref[0] == 0
    blank = jnp.zeros((1, 128), jnp.float32)
    even, odd = [], []
    for ref in (older_ref, last_ref, own_ref):
        block = ref[...].astype(jnp.float32)
        here = jnp.where(left, block[0:16], block[8:24])
        before = jnp.where(left, jnp.concatenate([blank, block[0:15]], 0), block[7:23])
        after = jnp.where(left, block[1:17], jnp.concatenate([block[9:24], blank], 0))
        rows = [
            jnp.concatenate([x, pltpu.roll(x, 96, 1)], 0).astype(jnp.bfloat16)
            for x in (before, here, after)
        ]
        even += rows[0:2]
        odd += rows[1:3]
    finished = []
    for parts, weight_ref in ((even, even_ref), (odd, odd_ref)):
        features = (
            jnp.dot(
                jnp.concatenate(parts, 1), weight_ref[...], preferred_element_type=jnp.float32
            )
            + bias_ref[...]
        )
        power = jnp.mean(features * features, axis=1, keepdims=True)
        scaled = features * lax.rsqrt(power + EPSILON) * gain_ref[...]
        finished.append((scaled / (1.0 + jnp.exp(-scaled))).astype(jnp.bfloat16))
    target = lax.broadcasted_iota(jnp.int32, (32, 32), 0)
    source = lax.broadcasted_iota(jnp.int32, (32, 32), 1)
    order = ((target & 1) * 16 + (target >> 1) == source).astype(jnp.float32).astype(jnp.bfloat16)
    for row in range(2):
        both = jnp.concatenate([x[row * 16 : row * 16 + 16] for x in finished], 0)
        out_ref[row] = jnp.dot(order, both, preferred_element_type=jnp.float32).astype(jnp.bfloat16)


def decode(half, own, last, older, even, odd, bias, gain):
    chans = bias.shape[1]
    return pl.pallas_call(
        decode_kernel,
        out_shape=jax.ShapeDtypeStruct((2, 32, chans), jnp.bfloat16),
        in_specs=[SMEM] + [VMEM] * 7,
        out_specs=VMEM,
        compiler_params=pltpu.CompilerParams(vmem_limit_bytes=32 * 2**20),
    )(half, own, last, older, even, odd, bias, gain)


def conv_matrices(conv_weight):
    taps, _, _, chans, outs = conv_weight.shape
    padded = jnp.pad(conv_weight, ((0, 0), (0, 1), (0, 0), (0, 0), (0, 0)))
    blank = jnp.zeros((taps, 4, 1, chans, outs), conv_weight.dtype)
    both = []
    for parts in ([blank, padded], [padded, blank]):
        spread = jnp.concatenate(parts, 2).reshape(taps, 4, 2, 2, chans, outs)
        both.append(spread.transpose(0, 2, 1, 3, 4, 5).reshape(taps * 16 * chans, outs))
    return both


def local(
    query, keys, values, lengths, timestep, latent, head_weight, conv_weight, conv_bias, gain
):
    cfg, zh, x = lax.axis_index("cfg"), lax.axis_index("zh"), lax.axis_index("x")
    y, zl = lax.axis_index("y"), lax.axis_index("zl")
    seq = ("y", "zl")

    own = jnp.concatenate([keys[0], values[0]], 1)
    before, after = lax.ppermute(own, "y", ring(1)), lax.ppermute(own, "y", ring(-1))
    across = [
        lax.ppermute(before[:, : 2 * DH], "y", ring(1)),
        lax.ppermute(after[:, 2 * DH :], "y", ring(-1)),
    ]
    key_values = [own, before, after] + across
    queries = [query[0]] + [lax.ppermute(query[0], "zl", crossed(m)) for m in (1, 2, 3)]
    block = jnp.stack([((y - d) % SIDE) * SIDE + zl for d in (0, 1, 3, 2)])
    counts = jnp.clip(lengths[0] - block * TOK, 0, TOK).astype(jnp.int32)
    slots = jnp.stack([zl ^ m for m in range(4)]).astype(jnp.int32)

    rows = latent[0].reshape(2, TCOLS, 32)
    blank = jnp.zeros((TCOLS, 32), jnp.float32)
    grid = jnp.concatenate([blank, rows[0], rows[1], blank], 1)
    latent_window = lax.dynamic_slice_in_dim(grid, cfg * 8, CUT, 0)
    even, odd = conv_matrices(conv_weight)
    bias_row, gain_row = conv_bias.reshape(1, -1), gain.reshape(1, -1)
    part = lax.dynamic_slice_in_dim(head_weight, (zh * SIDE + x) * 2 * DH, 2 * DH, 0)
    weight = jnp.concatenate([part[:, 32:], part, part[:, :32]], 1)
    sigma = noise_level(timestep[0], STEPS)
    scale = jnp.stack(
        [
            jnp.where(cfg == 0, GUIDE, 1.0 - GUIDE).astype(jnp.float32),
            jnp.where(cfg == 0, -1.0 / sigma, 0.0),
        ]
    )
    place = jnp.stack([zh * SIDE + x, zl]).astype(jnp.int32)

    near = attend(counts[:3], slots, queries[:2], key_values[:3])
    lse, top, acc = attend(
        counts,
        slots,
        queries,
        key_values,
        near,
        skip=3,
        extras=(grid, latent_window, even, odd, weight, bias_row, gain_row, scale, place),
        last=True,
    )
    lse = lax.all_to_all(lse, "zl", 0, 0, tiled=True)
    shares = project(scale, place, lse, top, acc, weight, grid)
    shares = lax.all_to_all(shares, ("cfg", "x"), 0, 0, tiled=True)
    shares = jnp.sum(shares.astype(jnp.float32), 0).astype(jnp.bfloat16)
    shares = lax.all_to_all(shares, ("zh", "zl"), 0, 0, tiled=True)
    window = jnp.sum(shares.astype(jnp.float32), 0)

    current = (latent_window - sigma * window).astype(jnp.bfloat16)
    last = lax.ppermute(current, seq, moved(1))
    older = lax.ppermute(current, seq, moved(2))
    mine = lax.dynamic_slice_in_dim(window, cfg * 8, TCOLS // 2, 0)[:, 32:96]
    velocity = mine.reshape(TCOLS // 2, 2, 2, -1).transpose(1, 0, 2, 3).reshape(1, 2, TCOLS, -1)
    decoded = decode(
        cfg.astype(jnp.int32).reshape(1),
        current,
        last,
        older,
        even,
        odd,
        bias_row,
        gain_row,
    )
    return (velocity, decoded[None])


def solution(mesh):
    split = Mesh(
        mesh.devices.reshape(2, SIDE, SIDE, SIDE, SIDE), ("cfg", "zh", "x", "y", "zl")
    )
    seq, band = ("y", "zl"), ("zh", "x")
    tokens = P("cfg", seq, band)
    return jax.shard_map(
        local,
        mesh=split,
        in_specs=(
            tokens,
            tokens,
            tokens,
            P(),
            P(),
            P(seq, band, None, None),
            P(),
            P(),
            P(),
            P(),
        ),
        out_specs=(P(seq, band, "cfg", None), P(seq, band, "cfg", None)),
        check_vma=False,
    )
```

```python
import functools
import math

import jax
import jax.numpy as jnp
from jax import lax
from jax.experimental import pallas as pl
from jax.experimental.pallas import tpu as pltpu
from jax.sharding import Mesh
from jax.sharding import PartitionSpec as P

DH = 128
STEPS = 50
GUIDE = 5.0
SHIFT_FACTOR = 5.0
NEG_FILL = -1e30
EPSILON = 1e-06
SIDE = 4
TOK = 512
ROWS, TCOLS = 16, 32
PATCH = 64
CHUNK = 2 * PATCH + 16
CUT = 24
LOG2_SCALE = math.log2(math.e) / math.sqrt(DH)

VMEM = pl.BlockSpec(memory_space=pltpu.VMEM)
SMEM = pl.BlockSpec(memory_space=pltpu.SMEM)
HBM = pl.BlockSpec(memory_space=pltpu.HBM)
ANY = pl.BlockSpec(memory_space=pl.ANY)


def in_hbm(value):
    return pltpu.with_memory_space_constraint(value, pltpu.HBM)


def noise_level(timestep, total_steps):
    frac = 1.0 - timestep.astype(jnp.float32) / total_steps
    return SHIFT_FACTOR * frac / (1.0 + (SHIFT_FACTOR - 1.0) * frac)


def ring(steps):
    return [(i, (i + steps) % SIDE) for i in range(SIDE)]


def crossed(mask):
    return [(i, i ^ mask) for i in range(SIDE)]


def moved(steps):
    count = SIDE * SIDE
    return [(i, i + steps) for i in range(count) if 0 <= i + steps < count]


def prepare_kernel(keys_ref, values_ref, out_ref, values, turned, sems):
    first = pltpu.make_async_copy(keys_ref, out_ref.at[pl.ds(0, TOK)], sems.at[0])
    second = pltpu.make_async_copy(values_ref, values, sems.at[1])
    first.start()
    second.start()
    second.wait()
    for half in range(2):
        rows = slice(half * 2 * DH, (half + 1) * 2 * DH)
        turned[rows] = jnp.transpose(values[rows])
    third = pltpu.make_async_copy(turned, out_ref.at[pl.ds(TOK, TOK)], sems.at[1])
    third.start()
    first.wait()
    third.wait()


def prepared(keys, values):
    return pl.pallas_call(
        prepare_kernel,
        out_shape=pltpu.HBM((2 * TOK, 2 * DH), jnp.bfloat16),
        in_specs=[HBM] * 2,
        out_specs=HBM,
        scratch_shapes=[pltpu.VMEM((TOK, 2 * DH), jnp.bfloat16)] * 2
        + [pltpu.SemaphoreType.DMA((2,))],
    )(in_hbm(keys), in_hbm(values))


def attention_kernel(count_ref, *refs, nq, whole, split, carry, nx, last):
    refs = list(refs)

    def take(size):
        taken = refs[:size]
        del refs[:size]
        return taken

    nk = whole + split
    q_refs, kv_refs = take(nq), take(whole + 2 * split)
    weight_hbm = take(1)[0] if last else None
    if carry:
        top_in, denom_in, acc_in = take(3)
    take(nx)
    if last:
        chunk_refs = take(nq)
        qs, ks, vs, scores, sems, acc_ref, top_ref, denom, weight_ref = refs
    else:
        top_ref, denom, acc_out = take(3)
        qs, ks, vs, scores, sems, acc_ref = refs

    sem = iter(range(64))

    def copied(source, target):
        copy = pltpu.make_async_copy(source, target, sems.at[next(sem)])
        copy.start()
        return copy

    arriving = []
    for b in range(nk):
        if b < whole:
            keys, values = kv_refs[b].at[pl.ds(0, TOK)], kv_refs[b].at[pl.ds(TOK, TOK)]
        else:
            keys, values = kv_refs[whole], kv_refs[whole + 1]
        group = [copied(keys, ks.at[b])]
        for half in range(2):
            for h in range(2):
                group.append(
                    copied(
                        values.at[pl.ds(half * 2 * DH + h * DH, DH)],
                        vs.at[b, h, pl.ds(0, DH), pl.ds(half * 2 * DH, 2 * DH)],
                    )
                )
        if b == 0:
            group += [copied(q_refs[j], qs.at[j]) for j in range(nq)]
            if carry:
                group.append(copied(acc_in, acc_ref))
        arriving.append(group)
    if last:
        arriving[0].append(copied(weight_hbm, weight_ref))
    if carry:
        top_ref[...] = top_in[...]
        denom[...] = denom_in[...]
    else:
        top_ref[...] = jnp.full((nq, 2, TOK), NEG_FILL, jnp.float32)
        denom[...] = jnp.zeros((nq, 2, TOK), jnp.float32)
        acc_ref[...] = jnp.zeros((nq, 2, DH, TOK), jnp.float32)
    for b in range(nk):
        for h in range(2):
            vs[b, h, DH:] = jnp.ones((16, TOK), jnp.bfloat16)
    for copy in arriving[0]:
        copy.wait()

    def scored(j, b, h):
        return lax.dot_general(
            ks[b, :, h * DH : (h + 1) * DH],
            qs[j, :, h * DH : (h + 1) * DH],
            (((1,), (1,)), ((), ())),
            preferred_element_type=jnp.float32,
        )

    def folded(j, b, h, score, masked):
        if masked:
            valid = lax.broadcasted_iota(jnp.int32, (TOK, TOK), 0) < count_ref[b]
            score = jnp.where(valid, score, NEG_FILL)
        old = top_ref[j, h : h + 1]
        new = jnp.maximum(old, jnp.max(score, axis=0, keepdims=True))
        weights = jnp.exp2((score - new) * LOG2_SCALE)
        if masked:
            weights = jnp.where(valid, weights, 0.0)
        factor = jnp.exp2((old - new) * LOG2_SCALE)
        top_ref[j, h : h + 1] = new
        mixed = jnp.dot(vs[b, h], weights.astype(jnp.bfloat16), preferred_element_type=jnp.float32)
        denom[j, h : h + 1] = denom[j, h : h + 1] * factor + mixed[DH : DH + 1]
        acc_ref[j, h] = acc_ref[j, h] * factor + mixed[:DH]

    total = nq * nk

    def step(t, _):
        j, b = lax.div(t, nk), lax.rem(t, nk)
        later = jnp.minimum(t + 1, total - 1)
        next_j, next_b = lax.div(later, nk), lax.rem(later, nk)
        count = count_ref[b]
        for needed in range(1, nk):

            @pl.when(t == needed - 1)
            def _():
                for copy in arriving[needed]:
                    copy.wait()

        def update(masked):
            scores[1] = scored(j, b, 1)
            folded(j, b, 0, scores[0], masked)
            scores[0] = scored(next_j, next_b, 0)
            folded(j, b, 1, scores[1], masked)

        @pl.when(count >= TOK)
        def _():
            update(False)

        @pl.when((count > 0) & (count < TOK))
        def _():
            update(True)

        @pl.when(count <= 0)
        def _():
            scores[0] = scored(next_j, next_b, 0)

        return 0

    scores[0] = scored(0, 0, 0)
    lax.fori_loop(0, total, step, 0)
    if not last:
        copy = pltpu.make_async_copy(acc_ref, acc_out, sems.at[0])
        copy.start()
        copy.wait()
        return
    for j in range(nq):
        parts, rows = [], []
        for h in range(2):
            mixed = (acc_ref[j, h] * (1.0 / denom[j, h : h + 1])).astype(jnp.bfloat16)
            parts.append(jnp.dot(weight_ref[h], mixed, preferred_element_type=jnp.float32))
            stat = top_ref[j, h : h + 1] * LOG2_SCALE + jnp.log2(denom[j, h : h + 1])
            for _ in range(3):
                piece = stat.astype(jnp.bfloat16).astype(jnp.float32)
                rows.append(piece)
                stat = stat - piece
        blank = jnp.zeros((CHUNK - 2 * PATCH - 6, TOK), jnp.float32)
        chunk_refs[j][...] = jnp.concatenate(parts + rows + [blank], 0).astype(jnp.bfloat16)


def attend(counts, queries, blocks, pair=(), weight=None, state=(), extras=()):
    f32, bf16 = jnp.float32, jnp.bfloat16
    nq, whole, split, last = len(queries), len(blocks), len(pair) // 2, weight is not None
    nk = whole + split
    stat = jax.ShapeDtypeStruct((nq, 2, TOK), f32)
    chunk = jax.ShapeDtypeStruct((CHUNK, TOK), bf16)
    acc = pltpu.HBM((nq, 2, DH, TOK), f32)
    scratch = [
        pltpu.VMEM((nq, TOK, 2 * DH), bf16),
        pltpu.VMEM((nk, TOK, 2 * DH), bf16),
        pltpu.VMEM((nk, 2, DH + 16, TOK), bf16),
        pltpu.VMEM((2, TOK, TOK), f32),
        pltpu.SemaphoreType.DMA((5 * nk + nq + 2,)),
        pltpu.VMEM((nq, 2, DH, TOK), f32),
    ]
    if last:
        scratch += [pltpu.VMEM((nq, 2, TOK), f32)] * 2 + [pltpu.VMEM((2, PATCH, DH), bf16)]
    work = nq * nk * 2 * TOK * TOK
    return pl.pallas_call(
        functools.partial(
            attention_kernel,
            nq=nq,
            whole=whole,
            split=split,
            carry=bool(state),
            nx=len(extras),
            last=last,
        ),
        out_shape=(chunk,) * nq if last else (stat, stat, acc),
        in_specs=[SMEM]
        + [HBM] * (nq + whole + len(pair) + last)
        + ([VMEM, VMEM, HBM] if state else [])
        + [ANY] * len(extras),
        out_specs=(VMEM,) * nq if last else (VMEM, VMEM, HBM),
        scratch_shapes=scratch,
        compiler_params=pltpu.CompilerParams(vmem_limit_bytes=24 * 2**20),
        cost_estimate=pl.CostEstimate(
            flops=work * DH * 4, transcendentals=work, bytes_accessed=(nq + 2 * nk) * TOK * 4 * DH
        ),
    )(
        counts,
        *(in_hbm(x) for x in (*queries, *blocks, *pair)),
        *((in_hbm(weight),) if last else ()),
        *(in_hbm(x) if x.ndim == 4 else x for x in state),
        *extras,
    )


def combine_kernel(scale_ref, place_ref, *refs):
    chunk_refs, (latent_ref, out_ref) = refs[:4], refs[4:]
    stats = []
    for h in range(2):
        base = 2 * PATCH + 3 * h
        pieces = [ref[2 * PATCH :].astype(jnp.float32) for ref in chunk_refs]
        at = base - 2 * PATCH
        stats.append([x[at : at + 1] + x[at + 1 : at + 2] + x[at + 2 : at + 3] for x in pieces])
    values = jnp.zeros((PATCH, TOK), jnp.float32)
    for h in range(2):
        peak = jnp.maximum(
            jnp.maximum(stats[h][0], stats[h][1]), jnp.maximum(stats[h][2], stats[h][3])
        )
        shares = [jnp.exp2(stat - peak) for stat in stats[h]]
        norm = scale_ref[0] / (shares[0] + shares[1] + shares[2] + shares[3])
        for ref, share in zip(chunk_refs, shares):
            values += ref[h * PATCH : (h + 1) * PATCH].astype(jnp.float32) * (share * norm)
    values = jnp.transpose(jnp.concatenate([values[32:], values, values[:32]], 0))
    values = values.reshape(ROWS, TCOLS, 128)
    lane = lax.broadcasted_iota(jnp.int32, (ROWS, TCOLS, 128), 2)
    blank = jnp.zeros((1, TCOLS, 128), jnp.float32)
    above = jnp.concatenate([blank, values[:-1]], 0)
    below = jnp.concatenate([values[1:], blank], 0)
    window = jnp.where(lane < 32, above, jnp.where(lane < 96, values, below))
    for row in range(ROWS):
        for half in range(2):
            cut = window[row, half * 8 : half * 8 + CUT]
            out_ref[half * ROWS + row] = cut.astype(jnp.bfloat16)
    band = place_ref[0]
    edge = pltpu.roll(latent_ref[...], 64, 1) * scale_ref[1]
    lane = lax.broadcasted_iota(jnp.int32, (TCOLS, 128), 1)
    for target, part in ((band + 1, lane < 32), (band - 1, lane >= 96)):

        @pl.when((target >= 0) & (target < ROWS))
        def _():
            sent = jnp.where(part, edge, 0.0)
            for half in range(2):
                at = half * ROWS + target
                out_ref[at] = (
                    out_ref[at].astype(jnp.float32) + sent[half * 8 : half * 8 + CUT]
                ).astype(jnp.bfloat16)


def combine(scale, place, chunks, latent):
    return pl.pallas_call(
        combine_kernel,
        out_shape=jax.ShapeDtypeStruct((2 * ROWS, CUT, 128), jnp.bfloat16),
        in_specs=[SMEM, SMEM] + [VMEM] * 5,
        out_specs=VMEM,
        compiler_params=pltpu.CompilerParams(vmem_limit_bytes=16 * 2**20),
    )(scale, place, *chunks, latent)


def decode_kernel(half_ref, own_ref, last_ref, older_ref, even_ref, odd_ref, bias_ref, gain_ref, out_ref):
    left = half_ref[0] == 0
    blank = jnp.zeros((1, 128), jnp.float32)
    even, odd = [], []
    for ref in (older_ref, last_ref, own_ref):
        block = ref[...].astype(jnp.float32)
        here = jnp.where(left, block[0:16], block[8:24])
        before = jnp.where(left, jnp.concatenate([blank, block[0:15]], 0), block[7:23])
        after = jnp.where(left, block[1:17], jnp.concatenate([block[9:24], blank], 0))
        rows = [
            jnp.concatenate([x, pltpu.roll(x, 96, 1)], 0).astype(jnp.bfloat16)
            for x in (before, here, after)
        ]
        even += rows[0:2]
        odd += rows[1:3]
    finished = []
    for parts, weight_ref in ((even, even_ref), (odd, odd_ref)):
        features = (
            jnp.dot(
                jnp.concatenate(parts, 1), weight_ref[...], preferred_element_type=jnp.float32
            )
            + bias_ref[...]
        )
        power = jnp.mean(features * features, axis=1, keepdims=True)
        scaled = features * lax.rsqrt(power + EPSILON) * gain_ref[...]
        finished.append((scaled / (1.0 + jnp.exp(-scaled))).astype(jnp.bfloat16))
    target = lax.broadcasted_iota(jnp.int32, (32, 32), 0)
    source = lax.broadcasted_iota(jnp.int32, (32, 32), 1)
    order = ((target & 1) * 16 + (target >> 1) == source).astype(jnp.float32).astype(jnp.bfloat16)
    for row in range(2):
        both = jnp.concatenate([x[row * 16 : row * 16 + 16] for x in finished], 0)
        out_ref[row] = jnp.dot(order, both, preferred_element_type=jnp.float32).astype(jnp.bfloat16)


def decode(half, own, last, older, even, odd, bias, gain):
    chans = bias.shape[1]
    return pl.pallas_call(
        decode_kernel,
        out_shape=jax.ShapeDtypeStruct((2, 32, chans), jnp.bfloat16),
        in_specs=[SMEM] + [VMEM] * 7,
        out_specs=VMEM,
        compiler_params=pltpu.CompilerParams(vmem_limit_bytes=32 * 2**20),
    )(half, own, last, older, even, odd, bias, gain)


def conv_matrices(conv_weight):
    taps, _, _, chans, outs = conv_weight.shape
    padded = jnp.pad(conv_weight, ((0, 0), (0, 1), (0, 0), (0, 0), (0, 0)))
    blank = jnp.zeros((taps, 4, 1, chans, outs), conv_weight.dtype)
    both = []
    for parts in ([blank, padded], [padded, blank]):
        spread = jnp.concatenate(parts, 2).reshape(taps, 4, 2, 2, chans, outs)
        both.append(spread.transpose(0, 2, 1, 3, 4, 5).reshape(taps * 16 * chans, outs))
    return both


def local(
    query, keys, values, lengths, timestep, latent, head_weight, conv_weight, conv_bias, gain
):
    cfg, zh, x = lax.axis_index("cfg"), lax.axis_index("zh"), lax.axis_index("x")
    y, zl = lax.axis_index("y"), lax.axis_index("zl")
    seq = ("y", "zl")

    own = prepared(keys[0], values[0])
    before, after = lax.ppermute(own, "y", ring(1)), lax.ppermute(own, "y", ring(-1))
    pair = [
        lax.ppermute(before[:TOK], "y", ring(1)),
        lax.ppermute(after[TOK:], "y", ring(-1)),
    ]
    blocks = [own, before, after]
    queries = [query[0]] + [lax.ppermute(query[0], "zl", crossed(m)) for m in (1, 2, 3)]
    block = jnp.stack([((y - d) % SIDE) * SIDE + zl for d in (0, 1, 3, 2)])
    counts = jnp.clip(lengths[0] - block * TOK, 0, TOK).astype(jnp.int32)

    rows = latent[0].reshape(2, TCOLS, 32)
    blank = jnp.zeros((TCOLS, 32), jnp.float32)
    grid = jnp.concatenate([blank, rows[0], rows[1], blank], 1)
    latent_window = lax.dynamic_slice_in_dim(grid, cfg * 8, CUT, 0)
    even, odd = conv_matrices(conv_weight)
    bias_row, gain_row = conv_bias.reshape(1, -1), gain.reshape(1, -1)
    part = lax.dynamic_slice_in_dim(head_weight, (zh * SIDE + x) * 2 * DH, 2 * DH, 0)
    weight = part.T.reshape(PATCH, 2, DH).transpose(1, 0, 2)
    sigma = noise_level(timestep[0], STEPS)
    scale = jnp.stack(
        [
            jnp.where(cfg == 0, GUIDE, 1.0 - GUIDE).astype(jnp.float32),
            jnp.where(cfg == 0, -1.0 / sigma, 0.0),
        ]
    )
    place = jnp.stack([zh * SIDE + x, zl]).astype(jnp.int32)

    near = attend(counts[:3], queries[:2], blocks)
    constants = (grid, latent_window, even, odd, bias_row, gain_row)
    (third,) = attend(counts, queries[3:], blocks, pair, weight, extras=constants)
    (second,) = attend(counts, queries[2:3], blocks, pair, weight, extras=(third,))
    mine, first = attend(counts[3:], queries[:2], [], pair, weight, near, (second,))
    chunks = [mine] + [
        lax.ppermute(chunk, "zl", crossed(m)) for m, chunk in ((3, third), (2, second), (1, first))
    ]
    shares = combine(scale, place, chunks, grid)
    shares = lax.all_to_all(shares, ("cfg", "zh", "x"), 0, 0, tiled=True)
    window = jnp.sum(shares.astype(jnp.float32), 0)

    current = (latent_window - sigma * window).astype(jnp.bfloat16)
    last = lax.ppermute(current, seq, moved(1))
    older = lax.ppermute(current, seq, moved(2))
    cells = lax.dynamic_slice_in_dim(window, cfg * 8, TCOLS // 2, 0)[:, 32:96]
    velocity = cells.reshape(TCOLS // 2, 2, 2, -1).transpose(1, 0, 2, 3).reshape(1, 2, TCOLS, -1)
    decoded = decode(
        cfg.astype(jnp.int32).reshape(1),
        current,
        last,
        older,
        even,
        odd,
        bias_row,
        gain_row,
    )
    return (velocity, decoded[None])


def solution(mesh):
    split = Mesh(
        mesh.devices.reshape(2, SIDE, SIDE, SIDE, SIDE), ("cfg", "zh", "x", "y", "zl")
    )
    seq, band = ("y", "zl"), ("zh", "x")
    tokens = P("cfg", seq, band)
    return jax.shard_map(
        local,
        mesh=split,
        in_specs=(
            tokens,
            tokens,
            tokens,
            P(),
            P(),
            P(seq, band, None, None),
            P(),
            P(),
            P(),
            P(),
        ),
        out_specs=(P(seq, band, "cfg", None), P(seq, band, "cfg", None)),
        check_vma=False,
    )
```

```python
import functools
import math

import jax
import jax.numpy as jnp
from jax import lax
from jax.experimental import pallas as pl
from jax.experimental.pallas import tpu as pltpu
from jax.sharding import Mesh
from jax.sharding import PartitionSpec as P

DH = 128
STEPS = 50
GUIDE = 5.0
SHIFT_FACTOR = 5.0
NEG_FILL = -1e30
EPSILON = 1e-06
SIDE = 4
TOK = 512
ROWS, TCOLS = 16, 32
PATCH = 64
CHUNK = 2 * PATCH + 16
CUT = 24
LOG2_SCALE = math.log2(math.e) / math.sqrt(DH)

VMEM = pl.BlockSpec(memory_space=pltpu.VMEM)
SMEM = pl.BlockSpec(memory_space=pltpu.SMEM)
HBM = pl.BlockSpec(memory_space=pltpu.HBM)
ANY = pl.BlockSpec(memory_space=pl.ANY)


def in_hbm(value):
    return pltpu.with_memory_space_constraint(value, pltpu.HBM)


def noise_level(timestep, total_steps):
    frac = 1.0 - timestep.astype(jnp.float32) / total_steps
    return SHIFT_FACTOR * frac / (1.0 + (SHIFT_FACTOR - 1.0) * frac)


def ring(steps):
    return [(i, (i + steps) % SIDE) for i in range(SIDE)]


def crossed(mask):
    return [(i, i ^ mask) for i in range(SIDE)]


def moved(steps):
    count = SIDE * SIDE
    return [(i, i + steps) for i in range(count) if 0 <= i + steps < count]


def prepare_kernel(keys_ref, values_ref, out_ref, values, both, sems):
    first = pltpu.make_async_copy(keys_ref, both.at[pl.ds(0, TOK)], sems.at[0])
    second = pltpu.make_async_copy(values_ref, values, sems.at[1])
    first.start()
    second.start()
    second.wait()
    for half in range(2):
        at = half * 2 * DH
        both[TOK + at : TOK + at + 2 * DH] = jnp.transpose(values[at : at + 2 * DH])
    first.wait()
    third = pltpu.make_async_copy(both, out_ref, sems.at[0])
    third.start()
    third.wait()


def prepared(keys, values):
    return pl.pallas_call(
        prepare_kernel,
        out_shape=pltpu.HBM((2 * TOK, 2 * DH), jnp.bfloat16),
        in_specs=[HBM] * 2,
        out_specs=HBM,
        scratch_shapes=[
            pltpu.VMEM((TOK, 2 * DH), jnp.bfloat16),
            pltpu.VMEM((2 * TOK, 2 * DH), jnp.bfloat16),
            pltpu.SemaphoreType.DMA((2,)),
        ],
    )(in_hbm(keys), in_hbm(values))


def attention_kernel(count_ref, *refs, nq, nk, start, carry, nx, last):
    refs = list(refs)

    def take(size):
        taken = refs[:size]
        del refs[:size]
        return taken

    q_refs, kv_refs = take(nq), take(nk)
    weight_hbm = take(1)[0] if last else None
    if carry:
        top_in, denom_in, acc_in = take(3)
    take(nx)
    if last:
        chunk_refs = take(nq)
        qs, ks, vs, scores, sems, acc_ref, top_ref, denom, weight_ref = refs
    else:
        top_ref, denom, acc_out = take(3)
        qs, ks, vs, scores, sems, acc_ref = refs

    sem = iter(range(64))

    def copied(source, target):
        copy = pltpu.make_async_copy(source, target, sems.at[next(sem)])
        copy.start()
        return copy

    arriving = []
    for b in range(nk):
        keys, values = kv_refs[b].at[pl.ds(0, TOK)], kv_refs[b].at[pl.ds(TOK, TOK)]
        group = [copied(keys, ks.at[b])]
        for half in range(2):
            for h in range(2):
                group.append(
                    copied(
                        values.at[pl.ds(half * 2 * DH + h * DH, DH)],
                        vs.at[b, h, pl.ds(0, DH), pl.ds(half * 2 * DH, 2 * DH)],
                    )
                )
        if b == 0:
            group += [copied(q_refs[j], qs.at[j]) for j in range(nq)]
            if carry:
                group.append(copied(acc_in, acc_ref))
        arriving.append(group)
    if last:
        arriving[0].append(copied(weight_hbm, weight_ref))
    if carry:
        top_ref[...] = top_in[...]
        denom[...] = denom_in[...]
    else:
        top_ref[...] = jnp.full((nq, 2, TOK), NEG_FILL, jnp.float32)
        denom[...] = jnp.zeros((nq, 2, TOK), jnp.float32)
        acc_ref[...] = jnp.zeros((nq, 2, DH, TOK), jnp.float32)
    for b in range(nk):
        for h in range(2):
            vs[b, h, DH:] = jnp.ones((16, TOK), jnp.bfloat16)
    for copy in arriving[0]:
        copy.wait()

    def scored(j, b, h):
        return lax.dot_general(
            ks[b, :, h * DH : (h + 1) * DH],
            qs[j, :, h * DH : (h + 1) * DH],
            (((1,), (1,)), ((), ())),
            preferred_element_type=jnp.float32,
        )

    def folded(j, b, h, score, masked):
        if masked:
            valid = lax.broadcasted_iota(jnp.int32, (TOK, TOK), 0) < count_ref[start + b]
            score = jnp.where(valid, score, NEG_FILL)
        old = top_ref[j, h : h + 1]
        new = jnp.maximum(old, jnp.max(score, axis=0, keepdims=True))
        weights = jnp.exp2((score - new) * LOG2_SCALE)
        if masked:
            weights = jnp.where(valid, weights, 0.0)
        factor = jnp.exp2((old - new) * LOG2_SCALE)
        top_ref[j, h : h + 1] = new
        mixed = jnp.dot(vs[b, h], weights.astype(jnp.bfloat16), preferred_element_type=jnp.float32)
        denom[j, h : h + 1] = denom[j, h : h + 1] * factor + mixed[DH : DH + 1]
        acc_ref[j, h] = acc_ref[j, h] * factor + mixed[:DH]

    total = nq * nk

    def step(t, _):
        j, b = lax.div(t, nk), lax.rem(t, nk)
        later = jnp.minimum(t + 1, total - 1)
        next_j, next_b = lax.div(later, nk), lax.rem(later, nk)
        count = count_ref[start + b]
        for needed in range(1, nk):

            @pl.when(t == needed - 1)
            def _():
                for copy in arriving[needed]:
                    copy.wait()

        def update(masked):
            scores[1] = scored(j, b, 1)
            folded(j, b, 0, scores[0], masked)
            scores[0] = scored(next_j, next_b, 0)
            folded(j, b, 1, scores[1], masked)

        @pl.when(count >= TOK)
        def _():
            update(False)

        @pl.when((count > 0) & (count < TOK))
        def _():
            update(True)

        @pl.when(count <= 0)
        def _():
            scores[0] = scored(next_j, next_b, 0)

        return 0

    scores[0] = scored(0, 0, 0)
    lax.fori_loop(0, total, step, 0)
    if not last:
        copy = pltpu.make_async_copy(acc_ref, acc_out, sems.at[0])
        copy.start()
        copy.wait()
        return
    for j in range(nq):
        parts, rows = [], []
        for h in range(2):
            mixed = (acc_ref[j, h] * (1.0 / denom[j, h : h + 1])).astype(jnp.bfloat16)
            parts.append(jnp.dot(weight_ref[h], mixed, preferred_element_type=jnp.float32))
            stat = top_ref[j, h : h + 1] * LOG2_SCALE + jnp.log2(denom[j, h : h + 1])
            for _ in range(3):
                piece = stat.astype(jnp.bfloat16).astype(jnp.float32)
                rows.append(piece)
                stat = stat - piece
        blank = jnp.zeros((CHUNK - 2 * PATCH - 6, TOK), jnp.float32)
        chunk_refs[j][...] = jnp.concatenate(parts + rows + [blank], 0).astype(jnp.bfloat16)


def attend(counts, queries, blocks, start=0, weight=None, state=(), extras=()):
    f32, bf16 = jnp.float32, jnp.bfloat16
    nq, nk, last = len(queries), len(blocks), weight is not None
    stat = jax.ShapeDtypeStruct((nq, 2, TOK), f32)
    chunk = jax.ShapeDtypeStruct((CHUNK, TOK), bf16)
    acc = pltpu.HBM((nq, 2, DH, TOK), f32)
    scratch = [
        pltpu.VMEM((nq, TOK, 2 * DH), bf16),
        pltpu.VMEM((nk, TOK, 2 * DH), bf16),
        pltpu.VMEM((nk, 2, DH + 16, TOK), bf16),
        pltpu.VMEM((2, TOK, TOK), f32),
        pltpu.SemaphoreType.DMA((5 * nk + nq + 2,)),
        pltpu.VMEM((nq, 2, DH, TOK), f32),
    ]
    if last:
        scratch += [pltpu.VMEM((nq, 2, TOK), f32)] * 2 + [pltpu.VMEM((2, PATCH, DH), bf16)]
    work = nq * nk * 2 * TOK * TOK
    return pl.pallas_call(
        functools.partial(
            attention_kernel,
            nq=nq,
            nk=nk,
            start=start,
            carry=bool(state),
            nx=len(extras),
            last=last,
        ),
        out_shape=(chunk,) * nq if last else (stat, stat, acc),
        in_specs=[SMEM]
        + [HBM] * (nq + nk + last)
        + ([VMEM, VMEM, HBM] if state else [])
        + [ANY] * len(extras),
        out_specs=(VMEM,) * nq if last else (VMEM, VMEM, HBM),
        scratch_shapes=scratch,
        compiler_params=pltpu.CompilerParams(vmem_limit_bytes=24 * 2**20),
        cost_estimate=pl.CostEstimate(
            flops=work * DH * 4, transcendentals=work, bytes_accessed=(nq + 2 * nk) * TOK * 4 * DH
        ),
    )(
        counts,
        *(in_hbm(x) for x in (*queries, *blocks)),
        *((in_hbm(weight),) if last else ()),
        *(in_hbm(x) if x.ndim == 4 else x for x in state),
        *extras,
    )


def combine_kernel(scale_ref, place_ref, *refs):
    chunk_refs, (latent_ref, out_ref) = refs[:4], refs[4:]
    stats = []
    for h in range(2):
        base = 2 * PATCH + 3 * h
        pieces = [ref[2 * PATCH :].astype(jnp.float32) for ref in chunk_refs]
        at = base - 2 * PATCH
        stats.append([x[at : at + 1] + x[at + 1 : at + 2] + x[at + 2 : at + 3] for x in pieces])
    values = jnp.zeros((PATCH, TOK), jnp.float32)
    for h in range(2):
        peak = jnp.maximum(
            jnp.maximum(stats[h][0], stats[h][1]), jnp.maximum(stats[h][2], stats[h][3])
        )
        shares = [jnp.exp2(stat - peak) for stat in stats[h]]
        norm = scale_ref[0] / (shares[0] + shares[1] + shares[2] + shares[3])
        for ref, share in zip(chunk_refs, shares):
            values += ref[h * PATCH : (h + 1) * PATCH].astype(jnp.float32) * (share * norm)
    values = jnp.transpose(jnp.concatenate([values[32:], values, values[:32]], 0))
    values = values.reshape(ROWS, TCOLS, 128)
    lane = lax.broadcasted_iota(jnp.int32, (ROWS, TCOLS, 128), 2)
    blank = jnp.zeros((1, TCOLS, 128), jnp.float32)
    above = jnp.concatenate([blank, values[:-1]], 0)
    below = jnp.concatenate([values[1:], blank], 0)
    window = jnp.where(lane < 32, above, jnp.where(lane < 96, values, below))
    for row in range(ROWS):
        for half in range(2):
            cut = window[row, half * 8 : half * 8 + CUT]
            out_ref[half * ROWS + row] = cut.astype(jnp.bfloat16)
    band = place_ref[0]
    edge = pltpu.roll(latent_ref[...], 64, 1) * scale_ref[1]
    lane = lax.broadcasted_iota(jnp.int32, (TCOLS, 128), 1)
    for target, part in ((band + 1, lane < 32), (band - 1, lane >= 96)):

        @pl.when((target >= 0) & (target < ROWS))
        def _():
            sent = jnp.where(part, edge, 0.0)
            for half in range(2):
                at = half * ROWS + target
                out_ref[at] = (
                    out_ref[at].astype(jnp.float32) + sent[half * 8 : half * 8 + CUT]
                ).astype(jnp.bfloat16)


def combine(scale, place, chunks, latent):
    return pl.pallas_call(
        combine_kernel,
        out_shape=jax.ShapeDtypeStruct((2 * ROWS, CUT, 128), jnp.bfloat16),
        in_specs=[SMEM, SMEM] + [VMEM] * 5,
        out_specs=VMEM,
        compiler_params=pltpu.CompilerParams(vmem_limit_bytes=16 * 2**20),
    )(scale, place, *chunks, latent)


def decode_kernel(half_ref, own_ref, last_ref, older_ref, even_ref, odd_ref, bias_ref, gain_ref, out_ref):
    left = half_ref[0] == 0
    blank = jnp.zeros((1, 128), jnp.float32)
    even, odd = [], []
    for ref in (older_ref, last_ref, own_ref):
        block = ref[...].astype(jnp.float32)
        here = jnp.where(left, block[0:16], block[8:24])
        before = jnp.where(left, jnp.concatenate([blank, block[0:15]], 0), block[7:23])
        after = jnp.where(left, block[1:17], jnp.concatenate([block[9:24], blank], 0))
        rows = [
            jnp.concatenate([x, pltpu.roll(x, 96, 1)], 0).astype(jnp.bfloat16)
            for x in (before, here, after)
        ]
        even += rows[0:2]
        odd += rows[1:3]
    finished = []
    for parts, weight_ref in ((even, even_ref), (odd, odd_ref)):
        features = (
            jnp.dot(
                jnp.concatenate(parts, 1), weight_ref[...], preferred_element_type=jnp.float32
            )
            + bias_ref[...]
        )
        power = jnp.mean(features * features, axis=1, keepdims=True)
        scaled = features * lax.rsqrt(power + EPSILON) * gain_ref[...]
        finished.append((scaled / (1.0 + jnp.exp(-scaled))).astype(jnp.bfloat16))
    target = lax.broadcasted_iota(jnp.int32, (32, 32), 0)
    source = lax.broadcasted_iota(jnp.int32, (32, 32), 1)
    order = ((target & 1) * 16 + (target >> 1) == source).astype(jnp.float32).astype(jnp.bfloat16)
    for row in range(2):
        both = jnp.concatenate([x[row * 16 : row * 16 + 16] for x in finished], 0)
        out_ref[row] = jnp.dot(order, both, preferred_element_type=jnp.float32).astype(jnp.bfloat16)


def decode(half, own, last, older, even, odd, bias, gain):
    chans = bias.shape[1]
    return pl.pallas_call(
        decode_kernel,
        out_shape=jax.ShapeDtypeStruct((2, 32, chans), jnp.bfloat16),
        in_specs=[SMEM] + [VMEM] * 7,
        out_specs=VMEM,
        compiler_params=pltpu.CompilerParams(vmem_limit_bytes=32 * 2**20),
    )(half, own, last, older, even, odd, bias, gain)


def conv_matrices(conv_weight):
    taps, _, _, chans, outs = conv_weight.shape
    padded = jnp.pad(conv_weight, ((0, 0), (0, 1), (0, 0), (0, 0), (0, 0)))
    blank = jnp.zeros((taps, 4, 1, chans, outs), conv_weight.dtype)
    both = []
    for parts in ([blank, padded], [padded, blank]):
        spread = jnp.concatenate(parts, 2).reshape(taps, 4, 2, 2, chans, outs)
        both.append(spread.transpose(0, 2, 1, 3, 4, 5).reshape(taps * 16 * chans, outs))
    return both


def local(
    query, keys, values, lengths, timestep, latent, head_weight, conv_weight, conv_bias, gain
):
    cfg, zh, x = lax.axis_index("cfg"), lax.axis_index("zh"), lax.axis_index("x")
    y, zl = lax.axis_index("y"), lax.axis_index("zl")
    seq = ("y", "zl")

    own = prepared(keys[0], values[0])
    blocks = [own] + [lax.ppermute(own, "y", ring(d)) for d in (1, 3, 2)]
    queries = [query[0]] + [lax.ppermute(query[0], "zl", crossed(m)) for m in (1, 2, 3)]
    block = jnp.stack([((y - d) % SIDE) * SIDE + zl for d in (0, 1, 3, 2)])
    counts = jnp.clip(lengths[0] - block * TOK, 0, TOK).astype(jnp.int32)

    rows = latent[0].reshape(2, TCOLS, 32)
    blank = jnp.zeros((TCOLS, 32), jnp.float32)
    grid = jnp.concatenate([blank, rows[0], rows[1], blank], 1)
    latent_window = lax.dynamic_slice_in_dim(grid, cfg * 8, CUT, 0)
    even, odd = conv_matrices(conv_weight)
    bias_row, gain_row = conv_bias.reshape(1, -1), gain.reshape(1, -1)
    part = lax.dynamic_slice_in_dim(head_weight, (zh * SIDE + x) * 2 * DH, 2 * DH, 0)
    weight = part.T.reshape(PATCH, 2, DH).transpose(1, 0, 2)
    sigma = noise_level(timestep[0], STEPS)
    scale = jnp.stack(
        [
            jnp.where(cfg == 0, GUIDE, 1.0 - GUIDE).astype(jnp.float32),
            jnp.where(cfg == 0, -1.0 / sigma, 0.0),
        ]
    )
    place = jnp.stack([zh * SIDE + x, zl]).astype(jnp.int32)

    near = attend(counts, queries[:2], blocks[:3])
    (third,) = attend(counts, queries[3:], blocks, weight=weight, extras=near[:1])
    (second,) = attend(counts, queries[2:3], blocks, weight=weight, extras=(third,))
    mine, first = attend(counts, queries[:2], blocks[3:], 3, weight, near, (second,))
    chunks = [mine] + [
        lax.ppermute(chunk, "zl", crossed(m)) for m, chunk in ((3, third), (2, second), (1, first))
    ]
    shares = combine(scale, place, chunks, grid)
    shares = lax.all_to_all(shares, ("cfg", "zh", "x"), 0, 0, tiled=True)
    window = jnp.sum(shares.astype(jnp.float32), 0)

    current = (latent_window - sigma * window).astype(jnp.bfloat16)
    last = lax.ppermute(current, seq, moved(1))
    older = lax.ppermute(current, seq, moved(2))
    cells = lax.dynamic_slice_in_dim(window, cfg * 8, TCOLS // 2, 0)[:, 32:96]
    velocity = cells.reshape(TCOLS // 2, 2, 2, -1).transpose(1, 0, 2, 3).reshape(1, 2, TCOLS, -1)
    decoded = decode(
        cfg.astype(jnp.int32).reshape(1),
        current,
        last,
        older,
        even,
        odd,
        bias_row,
        gain_row,
    )
    return (velocity, decoded[None])


def solution(mesh):
    split = Mesh(
        mesh.devices.reshape(2, SIDE, SIDE, SIDE, SIDE), ("cfg", "zh", "x", "y", "zl")
    )
    seq, band = ("y", "zl"), ("zh", "x")
    tokens = P("cfg", seq, band)
    return jax.shard_map(
        local,
        mesh=split,
        in_specs=(
            tokens,
            tokens,
            tokens,
            P(),
            P(),
            P(seq, band, None, None),
            P(),
            P(),
            P(),
            P(),
        ),
        out_specs=(P(seq, band, "cfg", None), P(seq, band, "cfg", None)),
        check_vma=False,
    )
```

```python
import functools
import math

import jax
import jax.numpy as jnp
from jax import lax
from jax.experimental import pallas as pl
from jax.experimental.pallas import tpu as pltpu
from jax.sharding import Mesh
from jax.sharding import PartitionSpec as P

DH = 128
STEPS = 50
GUIDE = 5.0
SHIFT_FACTOR = 5.0
NEG_FILL = -1e30
EPSILON = 1e-06
SIDE = 4
TOK = 512
ROWS, TCOLS = 16, 32
PATCH = 64
CHUNK = 2 * PATCH + 16
CUT = 24
LOG2_SCALE = math.log2(math.e) / math.sqrt(DH)

VMEM = pl.BlockSpec(memory_space=pltpu.VMEM)
SMEM = pl.BlockSpec(memory_space=pltpu.SMEM)
HBM = pl.BlockSpec(memory_space=pltpu.HBM)
ANY = pl.BlockSpec(memory_space=pl.ANY)


def in_hbm(value):
    return pltpu.with_memory_space_constraint(value, pltpu.HBM)


def noise_level(timestep, total_steps):
    frac = 1.0 - timestep.astype(jnp.float32) / total_steps
    return SHIFT_FACTOR * frac / (1.0 + (SHIFT_FACTOR - 1.0) * frac)


def ring(steps):
    return [(i, (i + steps) % SIDE) for i in range(SIDE)]


def crossed(mask):
    return [(i, i ^ mask) for i in range(SIDE)]


def moved(steps):
    count = SIDE * SIDE
    return [(i, i + steps) for i in range(count) if 0 <= i + steps < count]


def prepare_kernel(keys_ref, values_ref, out_ref, values, both, sems):
    first = pltpu.make_async_copy(keys_ref, both.at[pl.ds(0, TOK)], sems.at[0])
    second = pltpu.make_async_copy(values_ref, values, sems.at[1])
    first.start()
    second.start()
    second.wait()
    for half in range(2):
        at = half * 2 * DH
        both[TOK + at : TOK + at + 2 * DH] = jnp.transpose(values[at : at + 2 * DH])
    first.wait()
    third = pltpu.make_async_copy(both, out_ref, sems.at[0])
    third.start()
    third.wait()


def prepared(keys, values):
    return pl.pallas_call(
        prepare_kernel,
        out_shape=pltpu.HBM((2 * TOK, 2 * DH), jnp.bfloat16),
        in_specs=[HBM] * 2,
        out_specs=HBM,
        scratch_shapes=[
            pltpu.VMEM((TOK, 2 * DH), jnp.bfloat16),
            pltpu.VMEM((2 * TOK, 2 * DH), jnp.bfloat16),
            pltpu.SemaphoreType.DMA((2,)),
        ],
    )(in_hbm(keys), in_hbm(values))


def attention_kernel(count_ref, *refs, nq, nk, start, carry, nx, last):
    refs = list(refs)

    def take(size):
        taken = refs[:size]
        del refs[:size]
        return taken

    q_refs, kv_refs = take(nq), take(nk)
    weight_hbm = take(1)[0] if last else None
    if carry:
        top_in, denom_in, acc_in = take(3)
    take(nx)
    if last:
        chunk_refs = take(nq)
        qs, ks, vs, scores, sems, acc_ref, top_ref, denom, weight_ref = refs
    else:
        top_ref, denom, acc_out = take(3)
        qs, ks, vs, scores, sems, acc_ref = refs

    sem = iter(range(64))

    def copied(source, target):
        copy = pltpu.make_async_copy(source, target, sems.at[next(sem)])
        copy.start()
        return copy

    arriving = []
    for b in range(nk):
        keys, values = kv_refs[b].at[pl.ds(0, TOK)], kv_refs[b].at[pl.ds(TOK, TOK)]
        group = [copied(keys, ks.at[b])]
        for half in range(2):
            for h in range(2):
                group.append(
                    copied(
                        values.at[pl.ds(half * 2 * DH + h * DH, DH)],
                        vs.at[b, h, pl.ds(0, DH), pl.ds(half * 2 * DH, 2 * DH)],
                    )
                )
        if b == 0:
            group += [copied(q_refs[j], qs.at[j]) for j in range(nq)]
            if carry:
                group.append(copied(acc_in, acc_ref))
        arriving.append(group)
    if last:
        arriving[0].append(copied(weight_hbm, weight_ref))
    if carry:
        top_ref[...] = top_in[...]
        denom[...] = denom_in[...]
    else:
        top_ref[...] = jnp.full((nq, 2, TOK), NEG_FILL, jnp.float32)
        denom[...] = jnp.zeros((nq, 2, TOK), jnp.float32)
        acc_ref[...] = jnp.zeros((nq, 2, DH, TOK), jnp.float32)
    for b in range(nk):
        for h in range(2):
            vs[b, h, DH:] = jnp.ones((16, TOK), jnp.bfloat16)
    for copy in arriving[0]:
        copy.wait()

    def scored(j, b, h):
        return lax.dot_general(
            ks[b, :, h * DH : (h + 1) * DH],
            qs[j, :, h * DH : (h + 1) * DH],
            (((1,), (1,)), ((), ())),
            preferred_element_type=jnp.float32,
        )

    def folded(j, b, h, score, masked):
        if masked:
            valid = lax.broadcasted_iota(jnp.int32, (TOK, TOK), 0) < count_ref[start + b]
            score = jnp.where(valid, score, NEG_FILL)
        old = top_ref[j, h : h + 1]
        new = jnp.maximum(old, jnp.max(score, axis=0, keepdims=True))
        weights = jnp.exp2((score - new) * LOG2_SCALE)
        if masked:
            weights = jnp.where(valid, weights, 0.0)
        factor = jnp.exp2((old - new) * LOG2_SCALE)
        top_ref[j, h : h + 1] = new
        mixed = jnp.dot(vs[b, h], weights.astype(jnp.bfloat16), preferred_element_type=jnp.float32)
        denom[j, h : h + 1] = denom[j, h : h + 1] * factor + mixed[DH : DH + 1]
        acc_ref[j, h] = acc_ref[j, h] * factor + mixed[:DH]

    total = nq * nk

    def step(t, _):
        j, b = lax.div(t, nk), lax.rem(t, nk)
        later = jnp.minimum(t + 1, total - 1)
        next_j, next_b = lax.div(later, nk), lax.rem(later, nk)
        count = count_ref[start + b]
        for needed in range(1, nk):

            @pl.when(t == needed - 1)
            def _():
                for copy in arriving[needed]:
                    copy.wait()

        def update(masked):
            scores[1] = scored(j, b, 1)
            folded(j, b, 0, scores[0], masked)
            scores[0] = scored(next_j, next_b, 0)
            folded(j, b, 1, scores[1], masked)

        @pl.when(count >= TOK)
        def _():
            update(False)

        @pl.when((count > 0) & (count < TOK))
        def _():
            update(True)

        @pl.when(count <= 0)
        def _():
            scores[0] = scored(next_j, next_b, 0)

        return 0

    scores[0] = scored(0, 0, 0)
    lax.fori_loop(0, total, step, 0)
    if not last:
        copy = pltpu.make_async_copy(acc_ref, acc_out, sems.at[0])
        copy.start()
        copy.wait()
        return
    for j in range(nq):
        parts, rows = [], []
        for h in range(2):
            mixed = (acc_ref[j, h] * (1.0 / denom[j, h : h + 1])).astype(jnp.bfloat16)
            parts.append(jnp.dot(weight_ref[h], mixed, preferred_element_type=jnp.float32))
            stat = top_ref[j, h : h + 1] * LOG2_SCALE + jnp.log2(denom[j, h : h + 1])
            for _ in range(3):
                piece = stat.astype(jnp.bfloat16).astype(jnp.float32)
                rows.append(piece)
                stat = stat - piece
        blank = jnp.zeros((CHUNK - 2 * PATCH - 6, TOK), jnp.float32)
        chunk_refs[j][...] = jnp.concatenate(parts + rows + [blank], 0).astype(jnp.bfloat16)


def attend(counts, queries, blocks, start=0, weight=None, state=(), extras=()):
    f32, bf16 = jnp.float32, jnp.bfloat16
    nq, nk, last = len(queries), len(blocks), weight is not None
    stat = jax.ShapeDtypeStruct((nq, 2, TOK), f32)
    chunk = jax.ShapeDtypeStruct((CHUNK, TOK), bf16)
    acc = pltpu.HBM((nq, 2, DH, TOK), f32)
    scratch = [
        pltpu.VMEM((nq, TOK, 2 * DH), bf16),
        pltpu.VMEM((nk, TOK, 2 * DH), bf16),
        pltpu.VMEM((nk, 2, DH + 16, TOK), bf16),
        pltpu.VMEM((2, TOK, TOK), f32),
        pltpu.SemaphoreType.DMA((5 * nk + nq + 2,)),
        pltpu.VMEM((nq, 2, DH, TOK), f32),
    ]
    if last:
        scratch += [pltpu.VMEM((nq, 2, TOK), f32)] * 2 + [pltpu.VMEM((2, PATCH, DH), bf16)]
    work = nq * nk * 2 * TOK * TOK
    return pl.pallas_call(
        functools.partial(
            attention_kernel,
            nq=nq,
            nk=nk,
            start=start,
            carry=bool(state),
            nx=len(extras),
            last=last,
        ),
        out_shape=(chunk,) * nq if last else (stat, stat, acc),
        in_specs=[SMEM]
        + [HBM] * (nq + nk + last)
        + ([VMEM, VMEM, HBM] if state else [])
        + [ANY] * len(extras),
        out_specs=(VMEM,) * nq if last else (VMEM, VMEM, HBM),
        scratch_shapes=scratch,
        compiler_params=pltpu.CompilerParams(vmem_limit_bytes=24 * 2**20),
        cost_estimate=pl.CostEstimate(
            flops=work * DH * 4, transcendentals=work, bytes_accessed=(nq + 2 * nk) * TOK * 4 * DH
        ),
    )(
        counts,
        *(in_hbm(x) for x in (*queries, *blocks)),
        *((in_hbm(weight),) if last else ()),
        *(in_hbm(x) if x.ndim == 4 else x for x in state),
        *extras,
    )


def combine_kernel(scale_ref, place_ref, *refs):
    chunk_refs, (latent_ref, out_ref) = refs[:4], refs[4:]
    zh = place_ref[0]
    stats = []
    for h in range(2):
        base = 2 * PATCH + 3 * h
        pieces = [ref[2 * PATCH :].astype(jnp.float32) for ref in chunk_refs]
        at = base - 2 * PATCH
        stats.append([x[at : at + 1] + x[at + 1 : at + 2] + x[at + 2 : at + 3] for x in pieces])
    values = jnp.zeros((PATCH, TOK), jnp.float32)
    for h in range(2):
        peak = jnp.maximum(
            jnp.maximum(stats[h][0], stats[h][1]), jnp.maximum(stats[h][2], stats[h][3])
        )
        shares = [jnp.exp2(stat - peak) for stat in stats[h]]
        norm = scale_ref[0] / (shares[0] + shares[1] + shares[2] + shares[3])
        for ref, share in zip(chunk_refs, shares):
            values += ref[h * PATCH : (h + 1) * PATCH].astype(jnp.float32) * (share * norm)
    values = jnp.transpose(jnp.concatenate([values[32:], values, values[:32]], 0))
    values = values.reshape(ROWS, TCOLS, 128)
    lane = lax.broadcasted_iota(jnp.int32, (ROWS, TCOLS, 128), 2)
    blank = jnp.zeros((1, TCOLS, 128), jnp.float32)
    above = jnp.concatenate([blank, values[:-1]], 0)
    below = jnp.concatenate([values[1:], blank], 0)
    window = jnp.where(lane < 32, above, jnp.where(lane < 96, values, below))
    for row in range(ROWS):
        for half in range(2):
            cut = window[row, half * 8 : half * 8 + CUT]
            out_ref[half * SIDE + row % SIDE, (row // SIDE) ^ zh] = cut.astype(jnp.bfloat16)
    band = zh * SIDE + place_ref[1]
    edge = pltpu.roll(latent_ref[...], 64, 1) * scale_ref[1]
    lane = lax.broadcasted_iota(jnp.int32, (TCOLS, 128), 1)
    for target, part in ((band + 1, lane < 32), (band - 1, lane >= 96)):

        @pl.when((target >= 0) & (target < ROWS))
        def _():
            sent = jnp.where(part, edge, 0.0)
            for half in range(2):
                at = (half * SIDE + (target & 3), (target >> 2) ^ zh)
                out_ref[at] = (
                    out_ref[at].astype(jnp.float32) + sent[half * 8 : half * 8 + CUT]
                ).astype(jnp.bfloat16)


def combine(scale, place, chunks, latent):
    return pl.pallas_call(
        combine_kernel,
        out_shape=jax.ShapeDtypeStruct((2 * SIDE, SIDE, CUT, 128), jnp.bfloat16),
        in_specs=[SMEM, SMEM] + [VMEM] * 5,
        out_specs=VMEM,
        compiler_params=pltpu.CompilerParams(vmem_limit_bytes=16 * 2**20),
    )(scale, place, *chunks, latent)


def decode_kernel(half_ref, own_ref, last_ref, older_ref, even_ref, odd_ref, bias_ref, gain_ref, out_ref):
    left = half_ref[0] == 0
    blank = jnp.zeros((1, 128), jnp.float32)
    even, odd = [], []
    for ref in (older_ref, last_ref, own_ref):
        block = ref[...].astype(jnp.float32)
        here = jnp.where(left, block[0:16], block[8:24])
        before = jnp.where(left, jnp.concatenate([blank, block[0:15]], 0), block[7:23])
        after = jnp.where(left, block[1:17], jnp.concatenate([block[9:24], blank], 0))
        rows = [
            jnp.concatenate([x, pltpu.roll(x, 96, 1)], 0).astype(jnp.bfloat16)
            for x in (before, here, after)
        ]
        even += rows[0:2]
        odd += rows[1:3]
    finished = []
    for parts, weight_ref in ((even, even_ref), (odd, odd_ref)):
        features = (
            jnp.dot(
                jnp.concatenate(parts, 1), weight_ref[...], preferred_element_type=jnp.float32
            )
            + bias_ref[...]
        )
        power = jnp.mean(features * features, axis=1, keepdims=True)
        scaled = features * lax.rsqrt(power + EPSILON) * gain_ref[...]
        finished.append((scaled / (1.0 + jnp.exp(-scaled))).astype(jnp.bfloat16))
    target = lax.broadcasted_iota(jnp.int32, (32, 32), 0)
    source = lax.broadcasted_iota(jnp.int32, (32, 32), 1)
    order = ((target & 1) * 16 + (target >> 1) == source).astype(jnp.float32).astype(jnp.bfloat16)
    for row in range(2):
        both = jnp.concatenate([x[row * 16 : row * 16 + 16] for x in finished], 0)
        out_ref[row] = jnp.dot(order, both, preferred_element_type=jnp.float32).astype(jnp.bfloat16)


def decode(half, own, last, older, even, odd, bias, gain):
    chans = bias.shape[1]
    return pl.pallas_call(
        decode_kernel,
        out_shape=jax.ShapeDtypeStruct((2, 32, chans), jnp.bfloat16),
        in_specs=[SMEM] + [VMEM] * 7,
        out_specs=VMEM,
        compiler_params=pltpu.CompilerParams(vmem_limit_bytes=32 * 2**20),
    )(half, own, last, older, even, odd, bias, gain)


def conv_matrices(conv_weight):
    taps, _, _, chans, outs = conv_weight.shape
    padded = jnp.pad(conv_weight, ((0, 0), (0, 1), (0, 0), (0, 0), (0, 0)))
    blank = jnp.zeros((taps, 4, 1, chans, outs), conv_weight.dtype)
    both = []
    for parts in ([blank, padded], [padded, blank]):
        spread = jnp.concatenate(parts, 2).reshape(taps, 4, 2, 2, chans, outs)
        both.append(spread.transpose(0, 2, 1, 3, 4, 5).reshape(taps * 16 * chans, outs))
    return both


def local(
    query, keys, values, lengths, timestep, latent, head_weight, conv_weight, conv_bias, gain
):
    cfg, zh, x = lax.axis_index("cfg"), lax.axis_index("zh"), lax.axis_index("x")
    y, zl = lax.axis_index("y"), lax.axis_index("zl")
    seq = ("y", "zl")

    own = prepared(keys[0], values[0])
    blocks = [own] + [lax.ppermute(own, "y", ring(d)) for d in (1, 3, 2)]
    queries = [query[0]] + [lax.ppermute(query[0], "zl", crossed(m)) for m in (1, 2, 3)]
    block = jnp.stack([((y - d) % SIDE) * SIDE + zl for d in (0, 1, 3, 2)])
    counts = jnp.clip(lengths[0] - block * TOK, 0, TOK).astype(jnp.int32)

    rows = latent[0].reshape(2, TCOLS, 32)
    blank = jnp.zeros((TCOLS, 32), jnp.float32)
    grid = jnp.concatenate([blank, rows[0], rows[1], blank], 1)
    latent_window = lax.dynamic_slice_in_dim(grid, cfg * 8, CUT, 0)
    even, odd = conv_matrices(conv_weight)
    bias_row, gain_row = conv_bias.reshape(1, -1), gain.reshape(1, -1)
    part = lax.dynamic_slice_in_dim(head_weight, (zh * SIDE + x) * 2 * DH, 2 * DH, 0)
    weight = part.T.reshape(PATCH, 2, DH).transpose(1, 0, 2)
    sigma = noise_level(timestep[0], STEPS)
    scale = jnp.stack(
        [
            jnp.where(cfg == 0, GUIDE, 1.0 - GUIDE).astype(jnp.float32),
            jnp.where(cfg == 0, -1.0 / sigma, 0.0),
        ]
    )
    place = jnp.stack([zh, x]).astype(jnp.int32)

    near = attend(counts, queries[:1], blocks[:3])
    (third,) = attend(counts, queries[3:], blocks, weight=weight, extras=near[:1])
    second, first = attend(counts, queries[2:0:-1], blocks, weight=weight, extras=(third,))
    (mine,) = attend(counts, queries[:1], blocks[3:], 3, weight, near, (second, first))
    chunks = [mine] + [
        lax.ppermute(chunk, "zl", crossed(m)) for m, chunk in ((3, third), (2, second), (1, first))
    ]
    shares = combine(scale, place, chunks, grid)
    shares = lax.all_to_all(shares, ("cfg", "x"), 0, 0, tiled=True)
    shares = jnp.sum(shares.astype(jnp.float32), 0)
    other = lax.ppermute(shares[1:3], "zh", crossed(1))
    passed = lax.ppermute(shares[3] + other[1], "zh", crossed(3))
    window = shares[0] + other[0] + passed

    current = (latent_window - sigma * window).astype(jnp.bfloat16)
    last = lax.ppermute(current, seq, moved(1))
    older = lax.ppermute(current, seq, moved(2))
    cells = lax.dynamic_slice_in_dim(window, cfg * 8, TCOLS // 2, 0)[:, 32:96]
    velocity = cells.reshape(TCOLS // 2, 2, 2, -1).transpose(1, 0, 2, 3).reshape(1, 2, TCOLS, -1)
    decoded = decode(
        cfg.astype(jnp.int32).reshape(1),
        current,
        last,
        older,
        even,
        odd,
        bias_row,
        gain_row,
    )
    return (velocity, decoded[None])


def solution(mesh):
    split = Mesh(
        mesh.devices.reshape(2, SIDE, SIDE, SIDE, SIDE), ("cfg", "zh", "x", "y", "zl")
    )
    seq, band = ("y", "zl"), ("zh", "x")
    tokens = P("cfg", seq, band)
    return jax.shard_map(
        local,
        mesh=split,
        in_specs=(
            tokens,
            tokens,
            tokens,
            P(),
            P(),
            P(seq, band, None, None),
            P(),
            P(),
            P(),
            P(),
        ),
        out_specs=(P(seq, band, "cfg", None), P(seq, band, "cfg", None)),
        check_vma=False,
    )
```

```python
import functools
import math

import jax
import jax.numpy as jnp
from jax import lax
from jax.experimental import pallas as pl
from jax.experimental.pallas import tpu as pltpu
from jax.sharding import Mesh
from jax.sharding import PartitionSpec as P

DH = 128
STEPS = 50
GUIDE = 5.0
SHIFT_FACTOR = 5.0
NEG_FILL = -1e30
EPSILON = 1e-06
SIDE = 4
TOK = 512
ROWS, TCOLS = 16, 32
PATCH = 64
CHUNK = 2 * PATCH + 16
CUT = 24
LOG2_SCALE = math.log2(math.e) / math.sqrt(DH)

VMEM = pl.BlockSpec(memory_space=pltpu.VMEM)
SMEM = pl.BlockSpec(memory_space=pltpu.SMEM)
HBM = pl.BlockSpec(memory_space=pltpu.HBM)
ANY = pl.BlockSpec(memory_space=pl.ANY)


def in_hbm(value):
    return pltpu.with_memory_space_constraint(value, pltpu.HBM)


def noise_level(timestep, total_steps):
    frac = 1.0 - timestep.astype(jnp.float32) / total_steps
    return SHIFT_FACTOR * frac / (1.0 + (SHIFT_FACTOR - 1.0) * frac)


def ring(steps):
    return [(i, (i + steps) % SIDE) for i in range(SIDE)]


def crossed(mask):
    return [(i, i ^ mask) for i in range(SIDE)]


def moved(steps):
    count = SIDE * SIDE
    return [(i, i + steps) for i in range(count) if 0 <= i + steps < count]


def prepare_kernel(keys_ref, values_ref, out_ref, values, both, sems):
    first = pltpu.make_async_copy(keys_ref, both.at[pl.ds(0, TOK)], sems.at[0])
    second = pltpu.make_async_copy(values_ref, values, sems.at[1])
    first.start()
    second.start()
    second.wait()
    for half in range(2):
        at = half * 2 * DH
        both[TOK + at : TOK + at + 2 * DH] = jnp.transpose(values[at : at + 2 * DH])
    first.wait()
    third = pltpu.make_async_copy(both, out_ref, sems.at[0])
    third.start()
    third.wait()


def prepared(keys, values):
    return pl.pallas_call(
        prepare_kernel,
        out_shape=pltpu.HBM((2 * TOK, 2 * DH), jnp.bfloat16),
        in_specs=[HBM] * 2,
        out_specs=HBM,
        scratch_shapes=[
            pltpu.VMEM((TOK, 2 * DH), jnp.bfloat16),
            pltpu.VMEM((2 * TOK, 2 * DH), jnp.bfloat16),
            pltpu.SemaphoreType.DMA((2,)),
        ],
    )(in_hbm(keys), in_hbm(values))


def attention_kernel(count_ref, *refs, nq, nk, nx):
    refs = list(refs)

    def take(size):
        taken = refs[:size]
        del refs[:size]
        return taken

    q_refs, kv_refs = take(nq), take(nk)
    weight_hbm = take(1 + nx)[0]
    chunk_refs = take(nq)
    qs, ks, vs, scores, sems, acc_ref, top_ref, denom, weight_ref = refs

    sem = iter(range(64))

    def copied(source, target):
        copy = pltpu.make_async_copy(source, target, sems.at[next(sem)])
        copy.start()
        return copy

    arriving = []
    for b in range(nk):
        keys, values = kv_refs[b].at[pl.ds(0, TOK)], kv_refs[b].at[pl.ds(TOK, TOK)]
        group = [copied(keys, ks.at[b])]
        for half in range(2):
            for h in range(2):
                group.append(
                    copied(
                        values.at[pl.ds(half * 2 * DH + h * DH, DH)],
                        vs.at[b, h, pl.ds(0, DH), pl.ds(half * 2 * DH, 2 * DH)],
                    )
                )
        if b == 0:
            group += [copied(q_refs[j], qs.at[j]) for j in range(nq)]
        arriving.append(group)
    arriving[0].append(copied(weight_hbm, weight_ref))
    top_ref[...] = jnp.full((nq, 2, TOK), NEG_FILL, jnp.float32)
    denom[...] = jnp.zeros((nq, 2, TOK), jnp.float32)
    acc_ref[...] = jnp.zeros((nq, 2, DH, TOK), jnp.float32)
    for b in range(nk):
        for h in range(2):
            vs[b, h, DH:] = jnp.ones((16, TOK), jnp.bfloat16)
    for copy in arriving[0]:
        copy.wait()

    def scored(j, b, h):
        return lax.dot_general(
            ks[b, :, h * DH : (h + 1) * DH],
            qs[j, :, h * DH : (h + 1) * DH],
            (((1,), (1,)), ((), ())),
            preferred_element_type=jnp.float32,
        )

    def folded(j, b, h, score, masked):
        if masked:
            valid = lax.broadcasted_iota(jnp.int32, (TOK, TOK), 0) < count_ref[b]
            score = jnp.where(valid, score, NEG_FILL)
        old = top_ref[j, h : h + 1]
        new = jnp.maximum(old, jnp.max(score, axis=0, keepdims=True))
        weights = jnp.exp2((score - new) * LOG2_SCALE)
        if masked:
            weights = jnp.where(valid, weights, 0.0)
        factor = jnp.exp2((old - new) * LOG2_SCALE)
        top_ref[j, h : h + 1] = new
        mixed = jnp.dot(vs[b, h], weights.astype(jnp.bfloat16), preferred_element_type=jnp.float32)
        denom[j, h : h + 1] = denom[j, h : h + 1] * factor + mixed[DH : DH + 1]
        acc_ref[j, h] = acc_ref[j, h] * factor + mixed[:DH]

    total = nq * nk

    def step(t, _):
        j, b = lax.div(t, nk), lax.rem(t, nk)
        later = jnp.minimum(t + 1, total - 1)
        next_j, next_b = lax.div(later, nk), lax.rem(later, nk)
        count = count_ref[b]
        for needed in range(1, nk):

            @pl.when(t == needed - 1)
            def _():
                for copy in arriving[needed]:
                    copy.wait()

        def update(masked):
            scores[1] = scored(j, b, 1)
            folded(j, b, 0, scores[0], masked)
            scores[0] = scored(next_j, next_b, 0)
            folded(j, b, 1, scores[1], masked)

        @pl.when(count >= TOK)
        def _():
            update(False)

        @pl.when((count > 0) & (count < TOK))
        def _():
            update(True)

        @pl.when(count <= 0)
        def _():
            scores[0] = scored(next_j, next_b, 0)

        return 0

    scores[0] = scored(0, 0, 0)
    lax.fori_loop(0, total, step, 0)
    for j in range(nq):
        parts, rows = [], []
        for h in range(2):
            mixed = (acc_ref[j, h] * (1.0 / denom[j, h : h + 1])).astype(jnp.bfloat16)
            parts.append(jnp.dot(weight_ref[h], mixed, preferred_element_type=jnp.float32))
            stat = top_ref[j, h : h + 1] * LOG2_SCALE + jnp.log2(denom[j, h : h + 1])
            for _ in range(3):
                piece = stat.astype(jnp.bfloat16).astype(jnp.float32)
                rows.append(piece)
                stat = stat - piece
        blank = jnp.zeros((CHUNK - 2 * PATCH - 6, TOK), jnp.float32)
        chunk_refs[j][...] = jnp.concatenate(parts + rows + [blank], 0).astype(jnp.bfloat16)


def attend(counts, queries, blocks, weight, extras=()):
    f32, bf16 = jnp.float32, jnp.bfloat16
    nq, nk = len(queries), len(blocks)
    work = nq * nk * 2 * TOK * TOK
    return pl.pallas_call(
        functools.partial(attention_kernel, nq=nq, nk=nk, nx=len(extras)),
        out_shape=(jax.ShapeDtypeStruct((CHUNK, TOK), bf16),) * nq,
        in_specs=[SMEM] + [HBM] * (nq + nk + 1) + [ANY] * len(extras),
        out_specs=(VMEM,) * nq,
        scratch_shapes=[
            pltpu.VMEM((nq, TOK, 2 * DH), bf16),
            pltpu.VMEM((nk, TOK, 2 * DH), bf16),
            pltpu.VMEM((nk, 2, DH + 16, TOK), bf16),
            pltpu.VMEM((2, TOK, TOK), f32),
            pltpu.SemaphoreType.DMA((5 * nk + nq + 1,)),
            pltpu.VMEM((nq, 2, DH, TOK), f32),
            pltpu.VMEM((nq, 2, TOK), f32),
            pltpu.VMEM((nq, 2, TOK), f32),
            pltpu.VMEM((2, PATCH, DH), bf16),
        ],
        compiler_params=pltpu.CompilerParams(vmem_limit_bytes=24 * 2**20),
        cost_estimate=pl.CostEstimate(
            flops=work * DH * 4, transcendentals=work, bytes_accessed=(nq + 2 * nk) * TOK * 4 * DH
        ),
    )(counts, *(in_hbm(x) for x in (*queries, *blocks, weight)), *extras)


def combine_kernel(scale_ref, place_ref, *refs):
    chunk_refs, (latent_ref, out_ref) = refs[:4], refs[4:]
    stats = []
    for h in range(2):
        base = 2 * PATCH + 3 * h
        pieces = [ref[2 * PATCH :].astype(jnp.float32) for ref in chunk_refs]
        at = base - 2 * PATCH
        stats.append([x[at : at + 1] + x[at + 1 : at + 2] + x[at + 2 : at + 3] for x in pieces])
    values = jnp.zeros((PATCH, TOK), jnp.float32)
    for h in range(2):
        peak = jnp.maximum(
            jnp.maximum(stats[h][0], stats[h][1]), jnp.maximum(stats[h][2], stats[h][3])
        )
        shares = [jnp.exp2(stat - peak) for stat in stats[h]]
        norm = scale_ref[0] / (shares[0] + shares[1] + shares[2] + shares[3])
        for ref, share in zip(chunk_refs, shares):
            values += ref[h * PATCH : (h + 1) * PATCH].astype(jnp.float32) * (share * norm)
    values = jnp.transpose(jnp.concatenate([values[32:], values, values[:32]], 0))
    values = values.reshape(ROWS, TCOLS, 128)
    lane = lax.broadcasted_iota(jnp.int32, (ROWS, TCOLS, 128), 2)
    blank = jnp.zeros((1, TCOLS, 128), jnp.float32)
    above = jnp.concatenate([blank, values[:-1]], 0)
    below = jnp.concatenate([values[1:], blank], 0)
    window = jnp.where(lane < 32, above, jnp.where(lane < 96, values, below))
    for row in range(ROWS):
        for half in range(2):
            cut = window[row, half * 8 : half * 8 + CUT]
            out_ref[half * SIDE + row % SIDE, row // SIDE] = cut.astype(jnp.bfloat16)
    band = place_ref[0]
    edge = pltpu.roll(latent_ref[...], 64, 1) * scale_ref[1]
    lane = lax.broadcasted_iota(jnp.int32, (TCOLS, 128), 1)
    for target, part in ((band + 1, lane < 32), (band - 1, lane >= 96)):

        @pl.when((target >= 0) & (target < ROWS))
        def _():
            sent = jnp.where(part, edge, 0.0)
            for half in range(2):
                at = (half * SIDE + (target & 3), target >> 2)
                out_ref[at] = (
                    out_ref[at].astype(jnp.float32) + sent[half * 8 : half * 8 + CUT]
                ).astype(jnp.bfloat16)


def combine(scale, place, chunks, latent):
    return pl.pallas_call(
        combine_kernel,
        out_shape=jax.ShapeDtypeStruct((2 * SIDE, SIDE, CUT, 128), jnp.bfloat16),
        in_specs=[SMEM, SMEM] + [VMEM] * 5,
        out_specs=VMEM,
        compiler_params=pltpu.CompilerParams(vmem_limit_bytes=16 * 2**20),
    )(scale, place, *chunks, latent)


def decode_kernel(half_ref, own_ref, last_ref, older_ref, even_ref, odd_ref, bias_ref, gain_ref, out_ref):
    left = half_ref[0] == 0
    blank = jnp.zeros((1, 128), jnp.float32)
    even, odd = [], []
    for ref in (older_ref, last_ref, own_ref):
        block = ref[...].astype(jnp.float32)
        here = jnp.where(left, block[0:16], block[8:24])
        before = jnp.where(left, jnp.concatenate([blank, block[0:15]], 0), block[7:23])
        after = jnp.where(left, block[1:17], jnp.concatenate([block[9:24], blank], 0))
        rows = [
            jnp.concatenate([x, pltpu.roll(x, 96, 1)], 0).astype(jnp.bfloat16)
            for x in (before, here, after)
        ]
        even += rows[0:2]
        odd += rows[1:3]
    finished = []
    for parts, weight_ref in ((even, even_ref), (odd, odd_ref)):
        features = (
            jnp.dot(
                jnp.concatenate(parts, 1), weight_ref[...], preferred_element_type=jnp.float32
            )
            + bias_ref[...]
        )
        power = jnp.mean(features * features, axis=1, keepdims=True)
        scaled = features * lax.rsqrt(power + EPSILON) * gain_ref[...]
        finished.append((scaled / (1.0 + jnp.exp(-scaled))).astype(jnp.bfloat16))
    target = lax.broadcasted_iota(jnp.int32, (32, 32), 0)
    source = lax.broadcasted_iota(jnp.int32, (32, 32), 1)
    order = ((target & 1) * 16 + (target >> 1) == source).astype(jnp.float32).astype(jnp.bfloat16)
    for row in range(2):
        both = jnp.concatenate([x[row * 16 : row * 16 + 16] for x in finished], 0)
        out_ref[row] = jnp.dot(order, both, preferred_element_type=jnp.float32).astype(jnp.bfloat16)


def decode(half, own, last, older, even, odd, bias, gain):
    chans = bias.shape[1]
    return pl.pallas_call(
        decode_kernel,
        out_shape=jax.ShapeDtypeStruct((2, 32, chans), jnp.bfloat16),
        in_specs=[SMEM] + [VMEM] * 7,
        out_specs=VMEM,
        compiler_params=pltpu.CompilerParams(vmem_limit_bytes=32 * 2**20),
    )(half, own, last, older, even, odd, bias, gain)


def conv_matrices(conv_weight):
    taps, _, _, chans, outs = conv_weight.shape
    padded = jnp.pad(conv_weight, ((0, 0), (0, 1), (0, 0), (0, 0), (0, 0)))
    blank = jnp.zeros((taps, 4, 1, chans, outs), conv_weight.dtype)
    both = []
    for parts in ([blank, padded], [padded, blank]):
        spread = jnp.concatenate(parts, 2).reshape(taps, 4, 2, 2, chans, outs)
        both.append(spread.transpose(0, 2, 1, 3, 4, 5).reshape(taps * 16 * chans, outs))
    return both


def local(
    query, keys, values, lengths, timestep, latent, head_weight, conv_weight, conv_bias, gain
):
    cfg, zh, x = lax.axis_index("cfg"), lax.axis_index("zh"), lax.axis_index("x")
    y, zl = lax.axis_index("y"), lax.axis_index("zl")
    seq = ("y", "zl")

    own = prepared(keys[0], values[0])
    blocks = [own] + [lax.ppermute(own, "y", ring(d)) for d in (1, 3, 2)]
    queries = [query[0]] + [lax.ppermute(query[0], "zl", crossed(m)) for m in (1, 2, 3)]
    block = jnp.stack([((y - d) % SIDE) * SIDE + zl for d in (0, 1, 3, 2)])
    counts = jnp.clip(lengths[0] - block * TOK, 0, TOK).astype(jnp.int32)

    rows = latent[0].reshape(2, TCOLS, 32)
    blank = jnp.zeros((TCOLS, 32), jnp.float32)
    grid = jnp.concatenate([blank, rows[0], rows[1], blank], 1)
    latent_window = lax.dynamic_slice_in_dim(grid, cfg * 8, CUT, 0)
    even, odd = conv_matrices(conv_weight)
    bias_row, gain_row = conv_bias.reshape(1, -1), gain.reshape(1, -1)
    part = lax.dynamic_slice_in_dim(head_weight, (zh * SIDE + x) * 2 * DH, 2 * DH, 0)
    weight = part.T.reshape(PATCH, 2, DH).transpose(1, 0, 2)
    sigma = noise_level(timestep[0], STEPS)
    scale = jnp.stack(
        [
            jnp.where(cfg == 0, GUIDE, 1.0 - GUIDE).astype(jnp.float32),
            jnp.where(cfg == 0, -1.0 / sigma, 0.0),
        ]
    )
    place = (zh * SIDE + x).astype(jnp.int32).reshape(1)

    third, second, first = attend(counts, queries[3:0:-1], blocks, weight)
    (mine,) = attend(counts, queries[:1], blocks, weight, extras=(third,))
    chunks = [mine] + [
        lax.ppermute(chunk, "zl", crossed(m)) for m, chunk in ((3, third), (2, second), (1, first))
    ]
    shares = combine(scale, place, chunks, grid)
    shares = lax.all_to_all(shares, ("cfg", "x"), 0, 0, tiled=True)
    shares = jnp.sum(shares.astype(jnp.float32), 0)
    shares = lax.all_to_all(shares, "zh", 0, 0, tiled=True)
    window = jnp.sum(shares, 0)

    current = (latent_window - sigma * window).astype(jnp.bfloat16)
    last = lax.ppermute(current, seq, moved(1))
    older = lax.ppermute(current, seq, moved(2))
    cells = lax.dynamic_slice_in_dim(window, cfg * 8, TCOLS // 2, 0)[:, 32:96]
    velocity = cells.reshape(TCOLS // 2, 2, 2, -1).transpose(1, 0, 2, 3).reshape(1, 2, TCOLS, -1)
    decoded = decode(
        cfg.astype(jnp.int32).reshape(1),
        current,
        last,
        older,
        even,
        odd,
        bias_row,
        gain_row,
    )
    return (velocity, decoded[None])


def solution(mesh):
    split = Mesh(
        mesh.devices.reshape(2, SIDE, SIDE, SIDE, SIDE), ("cfg", "zh", "x", "y", "zl")
    )
    seq, band = ("y", "zl"), ("zh", "x")
    tokens = P("cfg", seq, band)
    return jax.shard_map(
        local,
        mesh=split,
        in_specs=(
            tokens,
            tokens,
            tokens,
            P(),
            P(),
            P(seq, band, None, None),
            P(),
            P(),
            P(),
            P(),
        ),
        out_specs=(P(seq, band, "cfg", None), P(seq, band, "cfg", None)),
        check_vma=False,
    )
```

```python
import functools
import math

import jax
import jax.numpy as jnp
from jax import lax
from jax.experimental import pallas as pl
from jax.experimental.pallas import tpu as pltpu
from jax.sharding import Mesh
from jax.sharding import PartitionSpec as P

DH = 128
STEPS = 50
GUIDE = 5.0
SHIFT_FACTOR = 5.0
NEG_FILL = -1e30
EPSILON = 1e-06
SIDE = 4
TOK = 512
ROWS, TCOLS = 16, 32
PATCH = 64
CHUNK = 2 * PATCH + 16
LOG2_SCALE = math.log2(math.e) / math.sqrt(DH)

VMEM = pl.BlockSpec(memory_space=pltpu.VMEM)
SMEM = pl.BlockSpec(memory_space=pltpu.SMEM)
HBM = pl.BlockSpec(memory_space=pltpu.HBM)
ANY = pl.BlockSpec(memory_space=pl.ANY)


def in_hbm(value):
    return pltpu.with_memory_space_constraint(value, pltpu.HBM)


def noise_level(timestep, total_steps):
    frac = 1.0 - timestep.astype(jnp.float32) / total_steps
    return SHIFT_FACTOR * frac / (1.0 + (SHIFT_FACTOR - 1.0) * frac)


def ring(steps):
    return [(i, (i + steps) % SIDE) for i in range(SIDE)]


def crossed(mask):
    return [(i, i ^ mask) for i in range(SIDE)]


def moved(steps):
    count = SIDE * SIDE
    return [(i, i + steps) for i in range(count) if 0 <= i + steps < count]


def prepare_kernel(keys_ref, values_ref, out_ref, values, both, sems):
    first = pltpu.make_async_copy(keys_ref, both.at[pl.ds(0, TOK)], sems.at[0])
    second = pltpu.make_async_copy(values_ref, values, sems.at[1])
    first.start()
    second.start()
    second.wait()
    for half in range(2):
        at = half * 2 * DH
        both[TOK + at : TOK + at + 2 * DH] = jnp.transpose(values[at : at + 2 * DH])
    first.wait()
    third = pltpu.make_async_copy(both, out_ref, sems.at[0])
    third.start()
    third.wait()


def prepared(keys, values):
    return pl.pallas_call(
        prepare_kernel,
        out_shape=pltpu.HBM((2 * TOK, 2 * DH), jnp.bfloat16),
        in_specs=[HBM] * 2,
        out_specs=HBM,
        scratch_shapes=[
            pltpu.VMEM((TOK, 2 * DH), jnp.bfloat16),
            pltpu.VMEM((2 * TOK, 2 * DH), jnp.bfloat16),
            pltpu.SemaphoreType.DMA((2,)),
        ],
    )(in_hbm(keys), in_hbm(values))


def attention_kernel(count_ref, *refs, nq, nk, nx):
    refs = list(refs)

    def take(size):
        taken = refs[:size]
        del refs[:size]
        return taken

    q_refs, kv_refs = take(nq), take(nk)
    weight_hbm = take(1 + nx)[0]
    chunk_refs = take(nq)
    qs, ks, vs, scores, sems, acc_ref, top_ref, denom, weight_ref = refs

    sem = iter(range(64))

    def copied(source, target):
        copy = pltpu.make_async_copy(source, target, sems.at[next(sem)])
        copy.start()
        return copy

    arriving = []
    for b in range(nk):
        keys, values = kv_refs[b].at[pl.ds(0, TOK)], kv_refs[b].at[pl.ds(TOK, TOK)]
        group = [copied(keys, ks.at[b])]
        for half in range(2):
            for h in range(2):
                group.append(
                    copied(
                        values.at[pl.ds(half * 2 * DH + h * DH, DH)],
                        vs.at[b, h, pl.ds(0, DH), pl.ds(half * 2 * DH, 2 * DH)],
                    )
                )
        if b == 0:
            group += [copied(q_refs[j], qs.at[j]) for j in range(nq)]
        arriving.append(group)
    arriving[0].append(copied(weight_hbm, weight_ref))
    top_ref[...] = jnp.full((nq, 2, TOK), NEG_FILL, jnp.float32)
    denom[...] = jnp.zeros((nq, 2, TOK), jnp.float32)
    acc_ref[...] = jnp.zeros((nq, 2, DH, TOK), jnp.float32)
    for b in range(nk):
        for h in range(2):
            vs[b, h, DH:] = jnp.ones((16, TOK), jnp.bfloat16)
    for copy in arriving[0]:
        copy.wait()

    def scored(j, b, h):
        return lax.dot_general(
            ks[b, :, h * DH : (h + 1) * DH],
            qs[j, :, h * DH : (h + 1) * DH],
            (((1,), (1,)), ((), ())),
            preferred_element_type=jnp.float32,
        )

    def folded(j, b, h, score, masked):
        if masked:
            valid = lax.broadcasted_iota(jnp.int32, (TOK, TOK), 0) < count_ref[b]
            score = jnp.where(valid, score, NEG_FILL)
        old = top_ref[j, h : h + 1]
        new = jnp.maximum(old, jnp.max(score, axis=0, keepdims=True))
        weights = jnp.exp2((score - new) * LOG2_SCALE)
        if masked:
            weights = jnp.where(valid, weights, 0.0)
        factor = jnp.exp2((old - new) * LOG2_SCALE)
        top_ref[j, h : h + 1] = new
        mixed = jnp.dot(vs[b, h], weights.astype(jnp.bfloat16), preferred_element_type=jnp.float32)
        denom[j, h : h + 1] = denom[j, h : h + 1] * factor + mixed[DH : DH + 1]
        acc_ref[j, h] = acc_ref[j, h] * factor + mixed[:DH]

    total = nq * nk

    def step(t, _):
        j, b = lax.div(t, nk), lax.rem(t, nk)
        later = jnp.minimum(t + 1, total - 1)
        next_j, next_b = lax.div(later, nk), lax.rem(later, nk)
        count = count_ref[b]
        for needed in range(1, nk):

            @pl.when(t == needed - 1)
            def _():
                for copy in arriving[needed]:
                    copy.wait()

        def update(masked):
            scores[1] = scored(j, b, 1)
            folded(j, b, 0, scores[0], masked)
            scores[0] = scored(next_j, next_b, 0)
            folded(j, b, 1, scores[1], masked)

        @pl.when(count >= TOK)
        def _():
            update(False)

        @pl.when((count > 0) & (count < TOK))
        def _():
            update(True)

        @pl.when(count <= 0)
        def _():
            scores[0] = scored(next_j, next_b, 0)

        return 0

    scores[0] = scored(0, 0, 0)
    lax.fori_loop(0, total, step, 0)
    for j in range(nq):
        parts, rows = [], []
        for h in range(2):
            mixed = (acc_ref[j, h] * (1.0 / denom[j, h : h + 1])).astype(jnp.bfloat16)
            parts.append(jnp.dot(weight_ref[h], mixed, preferred_element_type=jnp.float32))
            stat = top_ref[j, h : h + 1] * LOG2_SCALE + jnp.log2(denom[j, h : h + 1])
            for _ in range(3):
                piece = stat.astype(jnp.bfloat16).astype(jnp.float32)
                rows.append(piece)
                stat = stat - piece
        blank = jnp.zeros((CHUNK - 2 * PATCH - 6, TOK), jnp.float32)
        chunk_refs[j][...] = jnp.concatenate(parts + rows + [blank], 0).astype(jnp.bfloat16)


def attend(counts, queries, blocks, weight, extras=()):
    f32, bf16 = jnp.float32, jnp.bfloat16
    nq, nk = len(queries), len(blocks)
    work = nq * nk * 2 * TOK * TOK
    return pl.pallas_call(
        functools.partial(attention_kernel, nq=nq, nk=nk, nx=len(extras)),
        out_shape=(jax.ShapeDtypeStruct((CHUNK, TOK), bf16),) * nq,
        in_specs=[SMEM] + [HBM] * (nq + nk + 1) + [ANY] * len(extras),
        out_specs=(VMEM,) * nq,
        scratch_shapes=[
            pltpu.VMEM((nq, TOK, 2 * DH), bf16),
            pltpu.VMEM((nk, TOK, 2 * DH), bf16),
            pltpu.VMEM((nk, 2, DH + 16, TOK), bf16),
            pltpu.VMEM((2, TOK, TOK), f32),
            pltpu.SemaphoreType.DMA((5 * nk + nq + 1,)),
            pltpu.VMEM((nq, 2, DH, TOK), f32),
            pltpu.VMEM((nq, 2, TOK), f32),
            pltpu.VMEM((nq, 2, TOK), f32),
            pltpu.VMEM((2, PATCH, DH), bf16),
        ],
        compiler_params=pltpu.CompilerParams(vmem_limit_bytes=24 * 2**20),
        cost_estimate=pl.CostEstimate(
            flops=work * DH * 4, transcendentals=work, bytes_accessed=(nq + 2 * nk) * TOK * 4 * DH
        ),
    )(counts, *(in_hbm(x) for x in (*queries, *blocks, weight)), *extras)


def combine_kernel(scale_ref, place_ref, *refs):
    chunk_refs, (latent_ref, out_ref) = refs[:4], refs[4:]
    stats = []
    for h in range(2):
        base = 2 * PATCH + 3 * h
        pieces = [ref[2 * PATCH :].astype(jnp.float32) for ref in chunk_refs]
        at = base - 2 * PATCH
        stats.append([x[at : at + 1] + x[at + 1 : at + 2] + x[at + 2 : at + 3] for x in pieces])
    values = jnp.zeros((PATCH, TOK), jnp.float32)
    for h in range(2):
        peak = jnp.maximum(
            jnp.maximum(stats[h][0], stats[h][1]), jnp.maximum(stats[h][2], stats[h][3])
        )
        shares = [jnp.exp2(stat - peak) for stat in stats[h]]
        norm = scale_ref[0] / (shares[0] + shares[1] + shares[2] + shares[3])
        for ref, share in zip(chunk_refs, shares):
            values += ref[h * PATCH : (h + 1) * PATCH].astype(jnp.float32) * (share * norm)
    values = jnp.transpose(jnp.concatenate([values[32:], values, values[:32]], 0))
    values = values.reshape(ROWS, TCOLS, 128)
    lane = lax.broadcasted_iota(jnp.int32, (ROWS, TCOLS, 128), 2)
    blank = jnp.zeros((1, TCOLS, 128), jnp.float32)
    above = jnp.concatenate([blank, values[:-1]], 0)
    below = jnp.concatenate([values[1:], blank], 0)
    window = jnp.where(lane < 32, above, jnp.where(lane < 96, values, below))
    out_ref[...] = window.astype(jnp.bfloat16)
    band = place_ref[0]
    edge = pltpu.roll(latent_ref[...], 64, 1) * scale_ref[1]
    lane = lax.broadcasted_iota(jnp.int32, (TCOLS, 128), 1)
    for target, part in ((band + 1, lane < 32), (band - 1, lane >= 96)):

        @pl.when((target >= 0) & (target < ROWS))
        def _():
            sent = jnp.where(part, edge, 0.0)
            out_ref[target] = (out_ref[target].astype(jnp.float32) + sent).astype(jnp.bfloat16)


def combine(scale, place, chunks, latent):
    return pl.pallas_call(
        combine_kernel,
        out_shape=jax.ShapeDtypeStruct((ROWS, TCOLS, 128), jnp.bfloat16),
        in_specs=[SMEM, SMEM] + [VMEM] * 5,
        out_specs=VMEM,
        compiler_params=pltpu.CompilerParams(vmem_limit_bytes=16 * 2**20),
    )(scale, place, *chunks, latent)


def decode_kernel(half_ref, own_ref, last_ref, older_ref, even_ref, odd_ref, bias_ref, gain_ref, out_ref):
    left = half_ref[0] == 0
    blank = jnp.zeros((1, 128), jnp.float32)
    even, odd = [], []
    for ref in (older_ref, last_ref, own_ref):
        block = ref[...].astype(jnp.float32)
        here = jnp.where(left, block[0:16], block[16:32])
        before = jnp.where(left, jnp.concatenate([blank, block[0:15]], 0), block[15:31])
        after = jnp.where(left, block[1:17], jnp.concatenate([block[17:32], blank], 0))
        rows = [
            jnp.concatenate([x, pltpu.roll(x, 96, 1)], 0).astype(jnp.bfloat16)
            for x in (before, here, after)
        ]
        even += rows[0:2]
        odd += rows[1:3]
    finished = []
    for parts, weight_ref in ((even, even_ref), (odd, odd_ref)):
        features = (
            jnp.dot(
                jnp.concatenate(parts, 1), weight_ref[...], preferred_element_type=jnp.float32
            )
            + bias_ref[...]
        )
        power = jnp.mean(features * features, axis=1, keepdims=True)
        scaled = features * lax.rsqrt(power + EPSILON) * gain_ref[...]
        finished.append((scaled / (1.0 + jnp.exp(-scaled))).astype(jnp.bfloat16))
    target = lax.broadcasted_iota(jnp.int32, (32, 32), 0)
    source = lax.broadcasted_iota(jnp.int32, (32, 32), 1)
    order = ((target & 1) * 16 + (target >> 1) == source).astype(jnp.float32).astype(jnp.bfloat16)
    for row in range(2):
        both = jnp.concatenate([x[row * 16 : row * 16 + 16] for x in finished], 0)
        out_ref[row] = jnp.dot(order, both, preferred_element_type=jnp.float32).astype(jnp.bfloat16)


def decode(half, own, last, older, even, odd, bias, gain):
    chans = bias.shape[1]
    return pl.pallas_call(
        decode_kernel,
        out_shape=jax.ShapeDtypeStruct((2, 32, chans), jnp.bfloat16),
        in_specs=[SMEM] + [VMEM] * 7,
        out_specs=VMEM,
        compiler_params=pltpu.CompilerParams(vmem_limit_bytes=32 * 2**20),
    )(half, own, last, older, even, odd, bias, gain)


def conv_matrices(conv_weight):
    taps, _, _, chans, outs = conv_weight.shape
    padded = jnp.pad(conv_weight, ((0, 0), (0, 1), (0, 0), (0, 0), (0, 0)))
    blank = jnp.zeros((taps, 4, 1, chans, outs), conv_weight.dtype)
    both = []
    for parts in ([blank, padded], [padded, blank]):
        spread = jnp.concatenate(parts, 2).reshape(taps, 4, 2, 2, chans, outs)
        both.append(spread.transpose(0, 2, 1, 3, 4, 5).reshape(taps * 16 * chans, outs))
    return both


def local(
    query, keys, values, lengths, timestep, latent, head_weight, conv_weight, conv_bias, gain
):
    cfg, zh, x = lax.axis_index("cfg"), lax.axis_index("zh"), lax.axis_index("x")
    y, zl = lax.axis_index("y"), lax.axis_index("zl")
    seq = ("y", "zl")

    own = prepared(keys[0], values[0])
    blocks = [own] + [lax.ppermute(own, "y", ring(d)) for d in (1, 3, 2)]
    queries = [query[0]] + [lax.ppermute(query[0], "zl", crossed(m)) for m in (1, 2, 3)]
    block = jnp.stack([((y - d) % SIDE) * SIDE + zl for d in (0, 1, 3, 2)])
    counts = jnp.clip(lengths[0] - block * TOK, 0, TOK).astype(jnp.int32)

    rows = latent[0].reshape(2, TCOLS, 32)
    blank = jnp.zeros((TCOLS, 32), jnp.float32)
    grid = jnp.concatenate([blank, rows[0], rows[1], blank], 1)
    even, odd = conv_matrices(conv_weight)
    bias_row, gain_row = conv_bias.reshape(1, -1), gain.reshape(1, -1)
    part = lax.dynamic_slice_in_dim(head_weight, (zh * SIDE + x) * 2 * DH, 2 * DH, 0)
    weight = part.T.reshape(PATCH, 2, DH).transpose(1, 0, 2)
    sigma = noise_level(timestep[0], STEPS)
    scale = jnp.stack(
        [
            jnp.where(cfg == 0, GUIDE, 1.0 - GUIDE).astype(jnp.float32),
            jnp.where(cfg == 0, -1.0 / sigma, 0.0),
        ]
    )
    place = (zh * SIDE + x).astype(jnp.int32).reshape(1)

    third, second, first = attend(counts, queries[3:0:-1], blocks, weight)
    (mine,) = attend(counts, queries[:1], blocks, weight, extras=(third,))
    chunks = [mine] + [
        lax.ppermute(chunk, "zl", crossed(m)) for m, chunk in ((3, third), (2, second), (1, first))
    ]
    shares = combine(scale, place, chunks, grid)
    shares = lax.all_to_all(shares, ("zh", "x"), 0, 0, tiled=True)
    window = lax.psum(jnp.sum(shares.astype(jnp.float32), 0), "cfg")

    current = (grid - sigma * window).astype(jnp.bfloat16)
    last = lax.ppermute(current, seq, moved(1))
    older = lax.ppermute(current, seq, moved(2))
    cells = lax.dynamic_slice_in_dim(window, cfg * (TCOLS // 2), TCOLS // 2, 0)[:, 32:96]
    velocity = cells.reshape(TCOLS // 2, 2, 2, -1).transpose(1, 0, 2, 3).reshape(1, 2, TCOLS, -1)
    decoded = decode(
        cfg.astype(jnp.int32).reshape(1),
        current,
        last,
        older,
        even,
        odd,
        bias_row,
        gain_row,
    )
    return (velocity, decoded[None])


def solution(mesh):
    split = Mesh(
        mesh.devices.reshape(2, SIDE, SIDE, SIDE, SIDE), ("cfg", "zh", "x", "y", "zl")
    )
    seq, band = ("y", "zl"), ("zh", "x")
    tokens = P("cfg", seq, band)
    return jax.shard_map(
        local,
        mesh=split,
        in_specs=(
            tokens,
            tokens,
            tokens,
            P(),
            P(),
            P(seq, band, None, None),
            P(),
            P(),
            P(),
            P(),
        ),
        out_specs=(P(seq, band, "cfg", None), P(seq, band, "cfg", None)),
        check_vma=False,
    )
```

```python
import functools
import math

import jax
import jax.numpy as jnp
from jax import lax
from jax.experimental import pallas as pl
from jax.experimental.pallas import tpu as pltpu
from jax.sharding import Mesh
from jax.sharding import PartitionSpec as P

DH = 128
STEPS = 50
GUIDE = 5.0
SHIFT_FACTOR = 5.0
NEG_FILL = -1e30
EPSILON = 1e-06
SIDE = 4
TOK = 512
ROWS, TCOLS = 16, 32
PATCH = 64
CHUNK = 2 * PATCH + 16
LOG2_SCALE = math.log2(math.e) / math.sqrt(DH)

VMEM = pl.BlockSpec(memory_space=pltpu.VMEM)
SMEM = pl.BlockSpec(memory_space=pltpu.SMEM)
HBM = pl.BlockSpec(memory_space=pltpu.HBM)
ANY = pl.BlockSpec(memory_space=pl.ANY)


def in_hbm(value):
    return pltpu.with_memory_space_constraint(value, pltpu.HBM)


def noise_level(timestep, total_steps):
    frac = 1.0 - timestep.astype(jnp.float32) / total_steps
    return SHIFT_FACTOR * frac / (1.0 + (SHIFT_FACTOR - 1.0) * frac)


def ring(steps):
    return [(i, (i + steps) % SIDE) for i in range(SIDE)]


def crossed(mask):
    return [(i, i ^ mask) for i in range(SIDE)]


def moved(steps):
    count = SIDE * SIDE
    return [(i, i + steps) for i in range(count) if 0 <= i + steps < count]


def prepare_kernel(keys_ref, values_ref, out_ref, values, both, sems):
    first = pltpu.make_async_copy(keys_ref, both.at[pl.ds(0, TOK)], sems.at[0])
    second = pltpu.make_async_copy(values_ref, values, sems.at[1])
    first.start()
    second.start()
    second.wait()
    for half in range(2):
        at = half * 2 * DH
        both[TOK + at : TOK + at + 2 * DH] = jnp.transpose(values[at : at + 2 * DH])
    first.wait()
    third = pltpu.make_async_copy(both, out_ref, sems.at[0])
    third.start()
    third.wait()


def prepared(keys, values):
    return pl.pallas_call(
        prepare_kernel,
        out_shape=pltpu.HBM((2 * TOK, 2 * DH), jnp.bfloat16),
        in_specs=[HBM] * 2,
        out_specs=HBM,
        scratch_shapes=[
            pltpu.VMEM((TOK, 2 * DH), jnp.bfloat16),
            pltpu.VMEM((2 * TOK, 2 * DH), jnp.bfloat16),
            pltpu.SemaphoreType.DMA((2,)),
        ],
    )(in_hbm(keys), in_hbm(values))


def attention_kernel(count_ref, *refs, nq, nk, nx):
    refs = list(refs)

    def take(size):
        taken = refs[:size]
        del refs[:size]
        return taken

    q_refs, kv_refs = take(nq), take(nk)
    weight_hbm = take(1 + nx)[0]
    chunk_refs = take(nq)
    qs, ks, vs, scores, sems, acc_ref, top_ref, denom, weight_ref = refs

    sem = iter(range(64))

    def copied(source, target):
        copy = pltpu.make_async_copy(source, target, sems.at[next(sem)])
        copy.start()
        return copy

    arriving = []
    for b in range(nk):
        keys, values = kv_refs[b].at[pl.ds(0, TOK)], kv_refs[b].at[pl.ds(TOK, TOK)]
        group = [copied(keys, ks.at[b])]
        for half in range(2):
            for h in range(2):
                group.append(
                    copied(
                        values.at[pl.ds(half * 2 * DH + h * DH, DH)],
                        vs.at[b, h, pl.ds(0, DH), pl.ds(half * 2 * DH, 2 * DH)],
                    )
                )
        if b == 0:
            group += [copied(q_refs[j], qs.at[j]) for j in range(nq)]
        arriving.append(group)
    arriving[0].append(copied(weight_hbm, weight_ref))
    top_ref[...] = jnp.full((nq, 2, TOK), NEG_FILL, jnp.float32)
    denom[...] = jnp.zeros((nq, 2, TOK), jnp.float32)
    acc_ref[...] = jnp.zeros((nq, 2, DH, TOK), jnp.float32)
    for b in range(nk):
        for h in range(2):
            vs[b, h, DH:] = jnp.ones((16, TOK), jnp.bfloat16)
    for copy in arriving[0]:
        copy.wait()

    def scored(j, b, h):
        return lax.dot_general(
            ks[b, :, h * DH : (h + 1) * DH],
            qs[j, :, h * DH : (h + 1) * DH],
            (((1,), (1,)), ((), ())),
            preferred_element_type=jnp.float32,
        )

    def folded(j, b, h, score, masked):
        if masked:
            valid = lax.broadcasted_iota(jnp.int32, (TOK, TOK), 0) < count_ref[b]
            score = jnp.where(valid, score, NEG_FILL)
        old = top_ref[j, h : h + 1]
        new = jnp.maximum(old, jnp.max(score, axis=0, keepdims=True))
        weights = jnp.exp2((score - new) * LOG2_SCALE)
        if masked:
            weights = jnp.where(valid, weights, 0.0)
        factor = jnp.exp2((old - new) * LOG2_SCALE)
        top_ref[j, h : h + 1] = new
        mixed = jnp.dot(vs[b, h], weights.astype(jnp.bfloat16), preferred_element_type=jnp.float32)
        denom[j, h : h + 1] = denom[j, h : h + 1] * factor + mixed[DH : DH + 1]
        acc_ref[j, h] = acc_ref[j, h] * factor + mixed[:DH]

    total = nq * nk

    def step(t, _):
        j, b = lax.div(t, nk), lax.rem(t, nk)
        later = jnp.minimum(t + 1, total - 1)
        next_j, next_b = lax.div(later, nk), lax.rem(later, nk)
        count = count_ref[b]
        for needed in range(1, nk):

            @pl.when(t == needed - 1)
            def _():
                for copy in arriving[needed]:
                    copy.wait()

        def update(masked):
            scores[1] = scored(j, b, 1)
            folded(j, b, 0, scores[0], masked)
            scores[0] = scored(next_j, next_b, 0)
            folded(j, b, 1, scores[1], masked)

        @pl.when(count >= TOK)
        def _():
            update(False)

        @pl.when((count > 0) & (count < TOK))
        def _():
            update(True)

        @pl.when(count <= 0)
        def _():
            scores[0] = scored(next_j, next_b, 0)

        return 0

    scores[0] = scored(0, 0, 0)
    lax.fori_loop(0, total, step, 0)
    for j in range(nq):
        parts, rows = [], []
        for h in range(2):
            mixed = (acc_ref[j, h] * (1.0 / denom[j, h : h + 1])).astype(jnp.bfloat16)
            parts.append(jnp.dot(weight_ref[h], mixed, preferred_element_type=jnp.float32))
            stat = top_ref[j, h : h + 1] * LOG2_SCALE + jnp.log2(denom[j, h : h + 1])
            for _ in range(3):
                piece = stat.astype(jnp.bfloat16).astype(jnp.float32)
                rows.append(piece)
                stat = stat - piece
        blank = jnp.zeros((CHUNK - 2 * PATCH - 6, TOK), jnp.float32)
        chunk_refs[j][...] = jnp.concatenate(parts + rows + [blank], 0).astype(jnp.bfloat16)


def attend(counts, queries, blocks, weight, extras=()):
    f32, bf16 = jnp.float32, jnp.bfloat16
    nq, nk = len(queries), len(blocks)
    work = nq * nk * 2 * TOK * TOK
    return pl.pallas_call(
        functools.partial(attention_kernel, nq=nq, nk=nk, nx=len(extras)),
        out_shape=(jax.ShapeDtypeStruct((CHUNK, TOK), bf16),) * nq,
        in_specs=[SMEM] + [ANY] * (nq + nk + 1 + len(extras)),
        out_specs=(VMEM,) * nq,
        scratch_shapes=[
            pltpu.VMEM((nq, TOK, 2 * DH), bf16),
            pltpu.VMEM((nk, TOK, 2 * DH), bf16),
            pltpu.VMEM((nk, 2, DH + 16, TOK), bf16),
            pltpu.VMEM((2, TOK, TOK), f32),
            pltpu.SemaphoreType.DMA((5 * nk + nq + 1,)),
            pltpu.VMEM((nq, 2, DH, TOK), f32),
            pltpu.VMEM((nq, 2, TOK), f32),
            pltpu.VMEM((nq, 2, TOK), f32),
            pltpu.VMEM((2, PATCH, DH), bf16),
        ],
        compiler_params=pltpu.CompilerParams(vmem_limit_bytes=24 * 2**20),
        cost_estimate=pl.CostEstimate(
            flops=work * DH * 4, transcendentals=work, bytes_accessed=(nq + 2 * nk) * TOK * 4 * DH
        ),
    )(counts, *queries, *blocks, weight, *extras)


def combine_kernel(scale_ref, place_ref, *refs):
    chunk_refs, (latent_ref, out_ref) = refs[:4], refs[4:]
    stats = []
    for h in range(2):
        base = 2 * PATCH + 3 * h
        pieces = [ref[2 * PATCH :].astype(jnp.float32) for ref in chunk_refs]
        at = base - 2 * PATCH
        stats.append([x[at : at + 1] + x[at + 1 : at + 2] + x[at + 2 : at + 3] for x in pieces])
    values = jnp.zeros((PATCH, TOK), jnp.float32)
    for h in range(2):
        peak = jnp.maximum(
            jnp.maximum(stats[h][0], stats[h][1]), jnp.maximum(stats[h][2], stats[h][3])
        )
        shares = [jnp.exp2(stat - peak) for stat in stats[h]]
        norm = scale_ref[0] / (shares[0] + shares[1] + shares[2] + shares[3])
        for ref, share in zip(chunk_refs, shares):
            values += ref[h * PATCH : (h + 1) * PATCH].astype(jnp.float32) * (share * norm)
    values = jnp.transpose(jnp.concatenate([values[32:], values, values[:32]], 0))
    values = values.reshape(ROWS, TCOLS, 128)
    lane = lax.broadcasted_iota(jnp.int32, (ROWS, TCOLS, 128), 2)
    blank = jnp.zeros((1, TCOLS, 128), jnp.float32)
    above = jnp.concatenate([blank, values[:-1]], 0)
    below = jnp.concatenate([values[1:], blank], 0)
    window = jnp.where(lane < 32, above, jnp.where(lane < 96, values, below))
    for row in range(ROWS):
        out_ref[row] = window[row].astype(jnp.bfloat16)
    band = place_ref[0]
    edge = pltpu.roll(latent_ref[...], 64, 1) * scale_ref[1]
    lane = lax.broadcasted_iota(jnp.int32, (TCOLS, 128), 1)
    for target, part in ((band + 1, lane < 32), (band - 1, lane >= 96)):

        @pl.when((target >= 0) & (target < ROWS))
        def _():
            sent = jnp.where(part, edge, 0.0)
            out_ref[target] = (out_ref[target].astype(jnp.float32) + sent).astype(jnp.bfloat16)


def combine(scale, place, chunks, latent):
    return pl.pallas_call(
        combine_kernel,
        out_shape=jax.ShapeDtypeStruct((ROWS, TCOLS, 128), jnp.bfloat16),
        in_specs=[SMEM, SMEM] + [VMEM] * 5,
        out_specs=VMEM,
        compiler_params=pltpu.CompilerParams(vmem_limit_bytes=16 * 2**20),
    )(scale, place, *chunks, latent)


def decode_kernel(
    half_ref,
    own_ref,
    last_ref,
    older_ref,
    even_hbm,
    odd_hbm,
    bias_hbm,
    gain_hbm,
    out_ref,
    even_ref,
    odd_ref,
    bias_ref,
    gain_ref,
    sems,
):
    copies = [
        pltpu.make_async_copy(even_hbm, even_ref, sems.at[0]),
        pltpu.make_async_copy(odd_hbm, odd_ref, sems.at[1]),
        pltpu.make_async_copy(bias_hbm, bias_ref.at[0], sems.at[2]),
        pltpu.make_async_copy(gain_hbm, gain_ref.at[0], sems.at[3]),
    ]
    for copy in copies:
        copy.start()
    left = half_ref[0] == 0
    blank = jnp.zeros((1, 128), jnp.float32)
    even, odd = [], []
    for ref in (older_ref, last_ref, own_ref):
        block = ref[...].astype(jnp.float32)
        here = jnp.where(left, block[0:16], block[16:32])
        before = jnp.where(left, jnp.concatenate([blank, block[0:15]], 0), block[15:31])
        after = jnp.where(left, block[1:17], jnp.concatenate([block[17:32], blank], 0))
        rows = [
            jnp.concatenate([x, pltpu.roll(x, 96, 1)], 0).astype(jnp.bfloat16)
            for x in (before, here, after)
        ]
        even += rows[0:2]
        odd += rows[1:3]
    for copy in copies:
        copy.wait()
    finished = []
    for parts, weight_ref in ((even, even_ref), (odd, odd_ref)):
        features = (
            jnp.dot(
                jnp.concatenate(parts, 1), weight_ref[...], preferred_element_type=jnp.float32
            )
            + bias_ref[...]
        )
        power = jnp.mean(features * features, axis=1, keepdims=True)
        scaled = features * lax.rsqrt(power + EPSILON) * gain_ref[...]
        finished.append((scaled / (1.0 + jnp.exp(-scaled))).astype(jnp.bfloat16))
    target = lax.broadcasted_iota(jnp.int32, (32, 32), 0)
    source = lax.broadcasted_iota(jnp.int32, (32, 32), 1)
    order = ((target & 1) * 16 + (target >> 1) == source).astype(jnp.float32).astype(jnp.bfloat16)
    for row in range(2):
        both = jnp.concatenate([x[row * 16 : row * 16 + 16] for x in finished], 0)
        out_ref[row] = jnp.dot(order, both, preferred_element_type=jnp.float32).astype(jnp.bfloat16)


def decode(half, own, last, older, even, odd, bias, gain):
    chans = bias.shape[0]
    return pl.pallas_call(
        decode_kernel,
        out_shape=jax.ShapeDtypeStruct((2, 32, chans), jnp.bfloat16),
        in_specs=[SMEM] + [VMEM] * 3 + [ANY] * 4,
        out_specs=VMEM,
        scratch_shapes=[
            pltpu.VMEM(even.shape, even.dtype),
            pltpu.VMEM(odd.shape, odd.dtype),
            pltpu.VMEM((1, chans), jnp.float32),
            pltpu.VMEM((1, chans), jnp.float32),
            pltpu.SemaphoreType.DMA((4,)),
        ],
        compiler_params=pltpu.CompilerParams(vmem_limit_bytes=32 * 2**20),
    )(half, own, last, older, even, odd, bias, gain)


def conv_matrices(conv_weight):
    taps, _, _, chans, outs = conv_weight.shape
    padded = jnp.pad(conv_weight, ((0, 0), (0, 1), (0, 0), (0, 0), (0, 0)))
    blank = jnp.zeros((taps, 4, 1, chans, outs), conv_weight.dtype)
    both = []
    for parts in ([blank, padded], [padded, blank]):
        spread = jnp.concatenate(parts, 2).reshape(taps, 4, 2, 2, chans, outs)
        both.append(spread.transpose(0, 2, 1, 3, 4, 5).reshape(taps * 16 * chans, outs))
    return both


def local(
    query, keys, values, lengths, timestep, latent, head_weight, conv_weight, conv_bias, gain
):
    cfg, zh, x = lax.axis_index("cfg"), lax.axis_index("zh"), lax.axis_index("x")
    y, zl = lax.axis_index("y"), lax.axis_index("zl")
    seq = ("y", "zl")

    own = prepared(keys[0], values[0])
    blocks = [own] + [lax.ppermute(own, "y", ring(d)) for d in (1, 3, 2)]
    queries = [query[0]] + [lax.ppermute(query[0], "zl", crossed(m)) for m in (1, 2, 3)]
    block = jnp.stack([((y - d) % SIDE) * SIDE + zl for d in (0, 1, 3, 2)])
    counts = jnp.clip(lengths[0] - block * TOK, 0, TOK).astype(jnp.int32)

    rows = latent[0].reshape(2, TCOLS, 32)
    blank = jnp.zeros((TCOLS, 32), jnp.float32)
    grid = jnp.concatenate([blank, rows[0], rows[1], blank], 1)
    even, odd = conv_matrices(conv_weight)
    part = lax.dynamic_slice_in_dim(head_weight, (zh * SIDE + x) * 2 * DH, 2 * DH, 0)
    weight = part.T.reshape(PATCH, 2, DH).transpose(1, 0, 2)
    sigma = noise_level(timestep[0], STEPS)
    scale = jnp.stack(
        [
            jnp.where(cfg == 0, GUIDE, 1.0 - GUIDE).astype(jnp.float32),
            jnp.where(cfg == 0, -1.0 / sigma, 0.0),
        ]
    )
    place = (zh * SIDE + x).astype(jnp.int32).reshape(1)

    third, second, first = attend(counts, queries[3:0:-1], blocks, weight)
    (mine,) = attend(counts, queries[:1], blocks, weight, extras=(third, even, odd))
    chunks = [mine] + [
        lax.ppermute(chunk, "zl", crossed(m)) for m, chunk in ((3, third), (2, second), (1, first))
    ]
    shares = combine(scale, place, chunks, grid)
    shares = lax.all_to_all(shares, ("zh", "x"), 0, 0, tiled=True)
    window = lax.psum(jnp.sum(shares.astype(jnp.float32), 0), "cfg")

    current = (grid - sigma * window).astype(jnp.bfloat16)
    last = lax.ppermute(current, seq, moved(1))
    older = lax.ppermute(current, seq, moved(2))
    cells = lax.dynamic_slice_in_dim(window, cfg * (TCOLS // 2), TCOLS // 2, 0)[:, 32:96]
    velocity = cells.reshape(TCOLS // 2, 2, 2, -1).transpose(1, 0, 2, 3).reshape(1, 2, TCOLS, -1)
    decoded = decode(
        cfg.astype(jnp.int32).reshape(1),
        current,
        last,
        older,
        even,
        odd,
        conv_bias,
        gain,
    )
    return (velocity, decoded[None])


def solution(mesh):
    split = Mesh(
        mesh.devices.reshape(2, SIDE, SIDE, SIDE, SIDE), ("cfg", "zh", "x", "y", "zl")
    )
    seq, band = ("y", "zl"), ("zh", "x")
    tokens = P("cfg", seq, band)
    return jax.shard_map(
        local,
        mesh=split,
        in_specs=(
            tokens,
            tokens,
            tokens,
            P(),
            P(),
            P(seq, band, None, None),
            P(),
            P(),
            P(),
            P(),
        ),
        out_specs=(P(seq, band, "cfg", None), P(seq, band, "cfg", None)),
        check_vma=False,
    )
```

```python
import functools
import math

import jax
import jax.numpy as jnp
from jax import lax
from jax.experimental import pallas as pl
from jax.experimental.pallas import tpu as pltpu
from jax.sharding import Mesh
from jax.sharding import PartitionSpec as P

DH = 128
STEPS = 50
GUIDE = 5.0
SHIFT_FACTOR = 5.0
NEG_FILL = -1e30
EPSILON = 1e-06
SIDE = 4
TOK = 512
ROWS, TCOLS = 16, 32
PATCH = 64
CHUNK = 2 * PATCH + 16
LOG2_SCALE = math.log2(math.e) / math.sqrt(DH)

VMEM = pl.BlockSpec(memory_space=pltpu.VMEM)
SMEM = pl.BlockSpec(memory_space=pltpu.SMEM)
HBM = pl.BlockSpec(memory_space=pltpu.HBM)
ANY = pl.BlockSpec(memory_space=pl.ANY)


def in_hbm(value):
    return pltpu.with_memory_space_constraint(value, pltpu.HBM)


def noise_level(timestep, total_steps):
    frac = 1.0 - timestep.astype(jnp.float32) / total_steps
    return SHIFT_FACTOR * frac / (1.0 + (SHIFT_FACTOR - 1.0) * frac)


def ring(steps):
    return [(i, (i + steps) % SIDE) for i in range(SIDE)]


def crossed(mask):
    return [(i, i ^ mask) for i in range(SIDE)]


def moved(steps):
    count = SIDE * SIDE
    return [(i, i + steps) for i in range(count) if 0 <= i + steps < count]


def prepare_kernel(keys_ref, values_ref, out_ref, values, both, sems):
    first = pltpu.make_async_copy(keys_ref, both.at[pl.ds(0, TOK)], sems.at[0])
    second = pltpu.make_async_copy(values_ref, values, sems.at[1])
    first.start()
    second.start()
    second.wait()
    for half in range(2):
        at = half * 2 * DH
        both[TOK + at : TOK + at + 2 * DH] = jnp.transpose(values[at : at + 2 * DH])
    first.wait()
    third = pltpu.make_async_copy(both, out_ref, sems.at[0])
    third.start()
    third.wait()


def prepared(keys, values):
    return pl.pallas_call(
        prepare_kernel,
        out_shape=pltpu.HBM((2 * TOK, 2 * DH), jnp.bfloat16),
        in_specs=[HBM] * 2,
        out_specs=HBM,
        scratch_shapes=[
            pltpu.VMEM((TOK, 2 * DH), jnp.bfloat16),
            pltpu.VMEM((2 * TOK, 2 * DH), jnp.bfloat16),
            pltpu.SemaphoreType.DMA((2,)),
        ],
    )(in_hbm(keys), in_hbm(values))


def attention_kernel(count_ref, *refs, nq, nk, nx):
    refs = list(refs)

    def take(size):
        taken = refs[:size]
        del refs[:size]
        return taken

    q_refs, kv_refs = take(nq), take(nk)
    weight_hbm = take(1 + nx)[0]
    chunk_refs = take(nq)
    qs, ks, vs, scores, sems, acc_ref, top_ref, denom, weight_ref = refs

    sem = iter(range(64))

    def copied(source, target):
        copy = pltpu.make_async_copy(source, target, sems.at[next(sem)])
        copy.start()
        return copy

    arriving = []
    for b in range(nk):
        keys, values = kv_refs[b].at[pl.ds(0, TOK)], kv_refs[b].at[pl.ds(TOK, TOK)]
        group = [copied(keys, ks.at[b])]
        for half in range(2):
            for h in range(2):
                group.append(
                    copied(
                        values.at[pl.ds(half * 2 * DH + h * DH, DH)],
                        vs.at[b, h, pl.ds(0, DH), pl.ds(half * 2 * DH, 2 * DH)],
                    )
                )
        if b == 0:
            group += [copied(q_refs[j], qs.at[j]) for j in range(nq)]
        arriving.append(group)
    arriving[0].append(copied(weight_hbm, weight_ref))
    top_ref[...] = jnp.full((nq, 2, TOK), NEG_FILL, jnp.float32)
    denom[...] = jnp.zeros((nq, 2, TOK), jnp.float32)
    acc_ref[...] = jnp.zeros((nq, 2, DH, TOK), jnp.float32)
    for b in range(nk):
        for h in range(2):
            vs[b, h, DH:] = jnp.ones((16, TOK), jnp.bfloat16)
    for copy in arriving[0]:
        copy.wait()

    def scored(j, b, h):
        return lax.dot_general(
            ks[b, :, h * DH : (h + 1) * DH],
            qs[j, :, h * DH : (h + 1) * DH],
            (((1,), (1,)), ((), ())),
            preferred_element_type=jnp.float32,
        )

    def folded(j, b, h, score, masked):
        if masked:
            valid = lax.broadcasted_iota(jnp.int32, (TOK, TOK), 0) < count_ref[b]
            score = jnp.where(valid, score, NEG_FILL)
        old = top_ref[j, h : h + 1]
        new = jnp.maximum(old, jnp.max(score, axis=0, keepdims=True))
        weights = jnp.exp2((score - new) * LOG2_SCALE)
        if masked:
            weights = jnp.where(valid, weights, 0.0)
        factor = jnp.exp2((old - new) * LOG2_SCALE)
        top_ref[j, h : h + 1] = new
        mixed = jnp.dot(vs[b, h], weights.astype(jnp.bfloat16), preferred_element_type=jnp.float32)
        denom[j, h : h + 1] = denom[j, h : h + 1] * factor + mixed[DH : DH + 1]
        acc_ref[j, h] = acc_ref[j, h] * factor + mixed[:DH]

    total = nq * nk

    def step(t, _):
        j, b = lax.div(t, nk), lax.rem(t, nk)
        later = jnp.minimum(t + 1, total - 1)
        next_j, next_b = lax.div(later, nk), lax.rem(later, nk)
        count = count_ref[b]
        for needed in range(1, nk):

            @pl.when(t == needed - 1)
            def _():
                for copy in arriving[needed]:
                    copy.wait()

        def update(masked):
            scores[1] = scored(j, b, 1)
            folded(j, b, 0, scores[0], masked)
            scores[0] = scored(next_j, next_b, 0)
            folded(j, b, 1, scores[1], masked)

        @pl.when(count >= TOK)
        def _():
            update(False)

        @pl.when((count > 0) & (count < TOK))
        def _():
            update(True)

        @pl.when(count <= 0)
        def _():
            scores[0] = scored(next_j, next_b, 0)

        return 0

    scores[0] = scored(0, 0, 0)
    lax.fori_loop(0, total, step, 0)
    for j in range(nq):
        parts, rows = [], []
        for h in range(2):
            mixed = (acc_ref[j, h] * (1.0 / denom[j, h : h + 1])).astype(jnp.bfloat16)
            parts.append(jnp.dot(weight_ref[h], mixed, preferred_element_type=jnp.float32))
            stat = top_ref[j, h : h + 1] * LOG2_SCALE + jnp.log2(denom[j, h : h + 1])
            for _ in range(3):
                piece = stat.astype(jnp.bfloat16).astype(jnp.float32)
                rows.append(piece)
                stat = stat - piece
        blank = jnp.zeros((CHUNK - 2 * PATCH - 6, TOK), jnp.float32)
        chunk_refs[j][...] = jnp.concatenate(parts + rows + [blank], 0).astype(jnp.bfloat16)


def attend(counts, queries, blocks, weight, extras=()):
    f32, bf16 = jnp.float32, jnp.bfloat16
    nq, nk = len(queries), len(blocks)
    work = nq * nk * 2 * TOK * TOK
    return pl.pallas_call(
        functools.partial(attention_kernel, nq=nq, nk=nk, nx=len(extras)),
        out_shape=(jax.ShapeDtypeStruct((CHUNK, TOK), bf16),) * nq,
        in_specs=[SMEM] + [ANY] * (nq + nk + 1 + len(extras)),
        out_specs=(VMEM,) * nq,
        scratch_shapes=[
            pltpu.VMEM((nq, TOK, 2 * DH), bf16),
            pltpu.VMEM((nk, TOK, 2 * DH), bf16),
            pltpu.VMEM((nk, 2, DH + 16, TOK), bf16),
            pltpu.VMEM((2, TOK, TOK), f32),
            pltpu.SemaphoreType.DMA((5 * nk + nq + 1,)),
            pltpu.VMEM((nq, 2, DH, TOK), f32),
            pltpu.VMEM((nq, 2, TOK), f32),
            pltpu.VMEM((nq, 2, TOK), f32),
            pltpu.VMEM((2, PATCH, DH), bf16),
        ],
        compiler_params=pltpu.CompilerParams(vmem_limit_bytes=24 * 2**20),
        cost_estimate=pl.CostEstimate(
            flops=work * DH * 4, transcendentals=work, bytes_accessed=(nq + 2 * nk) * TOK * 4 * DH
        ),
    )(counts, *queries, *blocks, weight, *extras)


def combine_kernel(scale_ref, place_ref, *refs):
    chunk_refs, (latent_ref, out_ref) = refs[:4], refs[4:]
    stats = []
    for h in range(2):
        base = 2 * PATCH + 3 * h
        pieces = [ref[2 * PATCH :].astype(jnp.float32) for ref in chunk_refs]
        at = base - 2 * PATCH
        stats.append([x[at : at + 1] + x[at + 1 : at + 2] + x[at + 2 : at + 3] for x in pieces])
    values = jnp.zeros((PATCH, TOK), jnp.float32)
    for h in range(2):
        peak = jnp.maximum(
            jnp.maximum(stats[h][0], stats[h][1]), jnp.maximum(stats[h][2], stats[h][3])
        )
        shares = [jnp.exp2(stat - peak) for stat in stats[h]]
        norm = scale_ref[0] / (shares[0] + shares[1] + shares[2] + shares[3])
        for ref, share in zip(chunk_refs, shares):
            values += ref[h * PATCH : (h + 1) * PATCH].astype(jnp.float32) * (share * norm)
    values = jnp.transpose(jnp.concatenate([values[32:], values, values[:32]], 0))
    values = values.reshape(ROWS, TCOLS, 128)
    lane = lax.broadcasted_iota(jnp.int32, (ROWS, TCOLS, 128), 2)
    blank = jnp.zeros((1, TCOLS, 128), jnp.float32)
    above = jnp.concatenate([blank, values[:-1]], 0)
    below = jnp.concatenate([values[1:], blank], 0)
    window = jnp.where(lane < 32, above, jnp.where(lane < 96, values, below))
    for row in range(ROWS):
        out_ref[row] = window[row].astype(jnp.bfloat16)
    band = place_ref[0]
    edge = pltpu.roll(latent_ref[...], 64, 1) * scale_ref[1]
    lane = lax.broadcasted_iota(jnp.int32, (TCOLS, 128), 1)
    for target, part in ((band + 1, lane < 32), (band - 1, lane >= 96)):

        @pl.when((target >= 0) & (target < ROWS))
        def _():
            sent = jnp.where(part, edge, 0.0)
            out_ref[target] = (out_ref[target].astype(jnp.float32) + sent).astype(jnp.bfloat16)


def combine(scale, place, chunks, latent):
    return pl.pallas_call(
        combine_kernel,
        out_shape=jax.ShapeDtypeStruct((ROWS, TCOLS, 128), jnp.bfloat16),
        in_specs=[SMEM, SMEM] + [VMEM] * 5,
        out_specs=VMEM,
        compiler_params=pltpu.CompilerParams(vmem_limit_bytes=16 * 2**20),
    )(scale, place, *chunks, latent)


def decode_kernel(
    half_ref,
    own_ref,
    last_ref,
    older_ref,
    even_ref,
    odd_ref,
    bias_hbm,
    gain_hbm,
    out_ref,
    bias_ref,
    gain_ref,
    sems,
):
    copies = [
        pltpu.make_async_copy(bias_hbm, bias_ref.at[0], sems.at[0]),
        pltpu.make_async_copy(gain_hbm, gain_ref.at[0], sems.at[1]),
    ]
    for copy in copies:
        copy.start()
    left = half_ref[0] == 0
    blank = jnp.zeros((1, 128), jnp.float32)
    even, odd = [], []
    for ref in (older_ref, last_ref, own_ref):
        block = ref[...].astype(jnp.float32)
        here = jnp.where(left, block[0:16], block[16:32])
        before = jnp.where(left, jnp.concatenate([blank, block[0:15]], 0), block[15:31])
        after = jnp.where(left, block[1:17], jnp.concatenate([block[17:32], blank], 0))
        rows = [
            jnp.concatenate([x, pltpu.roll(x, 96, 1)], 0).astype(jnp.bfloat16)
            for x in (before, here, after)
        ]
        even += rows[0:2]
        odd += rows[1:3]
    for copy in copies:
        copy.wait()
    finished = []
    for parts, weight_ref in ((even, even_ref), (odd, odd_ref)):
        features = (
            jnp.dot(
                jnp.concatenate(parts, 1), weight_ref[...], preferred_element_type=jnp.float32
            )
            + bias_ref[...]
        )
        power = jnp.mean(features * features, axis=1, keepdims=True)
        scaled = features * lax.rsqrt(power + EPSILON) * gain_ref[...]
        finished.append((scaled / (1.0 + jnp.exp(-scaled))).astype(jnp.bfloat16))
    target = lax.broadcasted_iota(jnp.int32, (32, 32), 0)
    source = lax.broadcasted_iota(jnp.int32, (32, 32), 1)
    order = ((target & 1) * 16 + (target >> 1) == source).astype(jnp.float32).astype(jnp.bfloat16)
    for row in range(2):
        both = jnp.concatenate([x[row * 16 : row * 16 + 16] for x in finished], 0)
        out_ref[row] = jnp.dot(order, both, preferred_element_type=jnp.float32).astype(jnp.bfloat16)


def decode(half, own, last, older, even, odd, bias, gain):
    chans = bias.shape[0]
    return pl.pallas_call(
        decode_kernel,
        out_shape=jax.ShapeDtypeStruct((2, 32, chans), jnp.bfloat16),
        in_specs=[SMEM] + [VMEM] * 5 + [HBM] * 2,
        out_specs=VMEM,
        scratch_shapes=[
            pltpu.VMEM((1, chans), jnp.float32),
            pltpu.VMEM((1, chans), jnp.float32),
            pltpu.SemaphoreType.DMA((2,)),
        ],
        compiler_params=pltpu.CompilerParams(vmem_limit_bytes=32 * 2**20),
    )(half, own, last, older, even, odd, in_hbm(bias), in_hbm(gain))


def conv_matrices(conv_weight):
    taps, _, _, chans, outs = conv_weight.shape
    padded = jnp.pad(conv_weight, ((0, 0), (0, 1), (0, 0), (0, 0), (0, 0)))
    blank = jnp.zeros((taps, 4, 1, chans, outs), conv_weight.dtype)
    both = []
    for parts in ([blank, padded], [padded, blank]):
        spread = jnp.concatenate(parts, 2).reshape(taps, 4, 2, 2, chans, outs)
        both.append(spread.transpose(0, 2, 1, 3, 4, 5).reshape(taps * 16 * chans, outs))
    return both


def local(
    query, keys, values, lengths, timestep, latent, head_weight, conv_weight, conv_bias, gain
):
    cfg, zh, x = lax.axis_index("cfg"), lax.axis_index("zh"), lax.axis_index("x")
    y, zl = lax.axis_index("y"), lax.axis_index("zl")
    seq = ("y", "zl")

    own = prepared(keys[0], values[0])
    blocks = [own] + [lax.ppermute(own, "y", ring(d)) for d in (1, 3, 2)]
    queries = [query[0]] + [lax.ppermute(query[0], "zl", crossed(m)) for m in (1, 2, 3)]
    block = jnp.stack([((y - d) % SIDE) * SIDE + zl for d in (0, 1, 3, 2)])
    counts = jnp.clip(lengths[0] - block * TOK, 0, TOK).astype(jnp.int32)

    rows = latent[0].reshape(2, TCOLS, 32)
    blank = jnp.zeros((TCOLS, 32), jnp.float32)
    grid = jnp.concatenate([blank, rows[0], rows[1], blank], 1)
    even, odd = conv_matrices(conv_weight)
    part = lax.dynamic_slice_in_dim(head_weight, (zh * SIDE + x) * 2 * DH, 2 * DH, 0)
    weight = part.T.reshape(PATCH, 2, DH).transpose(1, 0, 2)
    sigma = noise_level(timestep[0], STEPS)
    scale = jnp.stack(
        [
            jnp.where(cfg == 0, GUIDE, 1.0 - GUIDE).astype(jnp.float32),
            jnp.where(cfg == 0, -1.0 / sigma, 0.0),
        ]
    )
    place = (zh * SIDE + x).astype(jnp.int32).reshape(1)

    third, second, first = attend(counts, queries[3:0:-1], blocks, weight)
    (mine,) = attend(counts, queries[:1], blocks, weight, extras=(third,))
    chunks = [mine] + [
        lax.ppermute(chunk, "zl", crossed(m)) for m, chunk in ((3, third), (2, second), (1, first))
    ]
    shares = combine(scale, place, chunks, grid)
    shares = lax.all_to_all(shares, ("zh", "x"), 0, 0, tiled=True)
    window = lax.psum(jnp.sum(shares.astype(jnp.float32), 0), "cfg")

    current = (grid - sigma * window).astype(jnp.bfloat16)
    last = lax.ppermute(current, seq, moved(1))
    older = lax.ppermute(current, seq, moved(2))
    cells = lax.dynamic_slice_in_dim(window, cfg * (TCOLS // 2), TCOLS // 2, 0)[:, 32:96]
    velocity = cells.reshape(TCOLS // 2, 2, 2, -1).transpose(1, 0, 2, 3).reshape(1, 2, TCOLS, -1)
    decoded = decode(
        cfg.astype(jnp.int32).reshape(1),
        current,
        last,
        older,
        even,
        odd,
        conv_bias,
        gain,
    )
    return (velocity, decoded[None])


def solution(mesh):
    split = Mesh(
        mesh.devices.reshape(2, SIDE, SIDE, SIDE, SIDE), ("cfg", "zh", "x", "y", "zl")
    )
    seq, band = ("y", "zl"), ("zh", "x")
    tokens = P("cfg", seq, band)
    return jax.shard_map(
        local,
        mesh=split,
        in_specs=(
            tokens,
            tokens,
            tokens,
            P(),
            P(),
            P(seq, band, None, None),
            P(),
            P(),
            P(),
            P(),
        ),
        out_specs=(P(seq, band, "cfg", None), P(seq, band, "cfg", None)),
        check_vma=False,
    )
```

```python
import functools
import math

import jax
import jax.numpy as jnp
from jax import lax
from jax.experimental import pallas as pl
from jax.experimental.pallas import tpu as pltpu
from jax.sharding import Mesh
from jax.sharding import PartitionSpec as P

DH = 128
STEPS = 50
GUIDE = 5.0
SHIFT_FACTOR = 5.0
NEG_FILL = -1e30
EPSILON = 1e-06
SIDE = 4
TOK = 512
ROWS, TCOLS = 16, 32
PATCH = 64
CHUNK = 2 * PATCH + 16
LOG2_SCALE = math.log2(math.e) / math.sqrt(DH)

VMEM = pl.BlockSpec(memory_space=pltpu.VMEM)
SMEM = pl.BlockSpec(memory_space=pltpu.SMEM)
HBM = pl.BlockSpec(memory_space=pltpu.HBM)
ANY = pl.BlockSpec(memory_space=pl.ANY)


def in_hbm(value):
    return pltpu.with_memory_space_constraint(value, pltpu.HBM)


def noise_level(timestep, total_steps):
    frac = 1.0 - timestep.astype(jnp.float32) / total_steps
    return SHIFT_FACTOR * frac / (1.0 + (SHIFT_FACTOR - 1.0) * frac)


def ring(steps):
    return [(i, (i + steps) % SIDE) for i in range(SIDE)]


def crossed(mask):
    return [(i, i ^ mask) for i in range(SIDE)]


def moved(steps):
    count = SIDE * SIDE
    return [(i, i + steps) for i in range(count) if 0 <= i + steps < count]


def prepare_kernel(keys_ref, values_ref, out_ref, values, both, sems):
    first = pltpu.make_async_copy(keys_ref, both.at[pl.ds(0, TOK)], sems.at[0])
    second = pltpu.make_async_copy(values_ref, values, sems.at[1])
    first.start()
    second.start()
    second.wait()
    for half in range(2):
        at = half * 2 * DH
        both[TOK + at : TOK + at + 2 * DH] = jnp.transpose(values[at : at + 2 * DH])
    first.wait()
    third = pltpu.make_async_copy(both, out_ref, sems.at[0])
    third.start()
    third.wait()


def prepared(keys, values):
    return pl.pallas_call(
        prepare_kernel,
        out_shape=pltpu.HBM((2 * TOK, 2 * DH), jnp.bfloat16),
        in_specs=[HBM] * 2,
        out_specs=HBM,
        scratch_shapes=[
            pltpu.VMEM((TOK, 2 * DH), jnp.bfloat16),
            pltpu.VMEM((2 * TOK, 2 * DH), jnp.bfloat16),
            pltpu.SemaphoreType.DMA((2,)),
        ],
    )(in_hbm(keys), in_hbm(values))


def attention_kernel(count_ref, *refs, nq, nk, nx):
    refs = list(refs)

    def take(size):
        taken = refs[:size]
        del refs[:size]
        return taken

    q_refs, kv_refs = take(nq), take(nk)
    weight_hbm = take(1 + nx)[0]
    chunk_refs = take(nq)
    qs, ks, vs, scores, sems, acc_ref, top_ref, denom, weight_ref = refs

    sem = iter(range(64))

    def copied(source, target):
        copy = pltpu.make_async_copy(source, target, sems.at[next(sem)])
        copy.start()
        return copy

    arriving = []
    for b in range(nk):
        keys, values = kv_refs[b].at[pl.ds(0, TOK)], kv_refs[b].at[pl.ds(TOK, TOK)]
        group = [copied(keys, ks.at[b])]
        for half in range(2):
            for h in range(2):
                group.append(
                    copied(
                        values.at[pl.ds(half * 2 * DH + h * DH, DH)],
                        vs.at[b, h, pl.ds(0, DH), pl.ds(half * 2 * DH, 2 * DH)],
                    )
                )
        if b == 0:
            group += [copied(q_refs[j], qs.at[j]) for j in range(nq)]
        arriving.append(group)
    arriving[0].append(copied(weight_hbm, weight_ref))
    top_ref[...] = jnp.full((nq, 2, TOK), NEG_FILL, jnp.float32)
    denom[...] = jnp.zeros((nq, 2, TOK), jnp.float32)
    acc_ref[...] = jnp.zeros((nq, 2, DH, TOK), jnp.float32)
    for b in range(nk):
        for h in range(2):
            vs[b, h, DH:] = jnp.ones((16, TOK), jnp.bfloat16)
    for copy in arriving[0]:
        copy.wait()

    def scored(j, b, h):
        return lax.dot_general(
            ks[b, :, h * DH : (h + 1) * DH],
            qs[j, :, h * DH : (h + 1) * DH],
            (((1,), (1,)), ((), ())),
            preferred_element_type=jnp.float32,
        )

    def folded(j, b, h, score, masked):
        if masked:
            valid = lax.broadcasted_iota(jnp.int32, (TOK, TOK), 0) < count_ref[b]
            score = jnp.where(valid, score, NEG_FILL)
        old = top_ref[j, h : h + 1]
        new = jnp.maximum(old, jnp.max(score, axis=0, keepdims=True))
        weights = jnp.exp2((score - new) * LOG2_SCALE)
        if masked:
            weights = jnp.where(valid, weights, 0.0)
        factor = jnp.exp2((old - new) * LOG2_SCALE)
        top_ref[j, h : h + 1] = new
        mixed = jnp.dot(vs[b, h], weights.astype(jnp.bfloat16), preferred_element_type=jnp.float32)
        denom[j, h : h + 1] = denom[j, h : h + 1] * factor + mixed[DH : DH + 1]
        acc_ref[j, h] = acc_ref[j, h] * factor + mixed[:DH]

    total = nq * nk

    def step(t, _):
        j, b = lax.div(t, nk), lax.rem(t, nk)
        later = jnp.minimum(t + 1, total - 1)
        next_j, next_b = lax.div(later, nk), lax.rem(later, nk)
        count = count_ref[b]
        for needed in range(1, nk):

            @pl.when(t == needed - 1)
            def _():
                for copy in arriving[needed]:
                    copy.wait()

        def update(masked):
            scores[1] = scored(j, b, 1)
            folded(j, b, 0, scores[0], masked)
            scores[0] = scored(next_j, next_b, 0)
            folded(j, b, 1, scores[1], masked)

        @pl.when(count >= TOK)
        def _():
            update(False)

        @pl.when((count > 0) & (count < TOK))
        def _():
            update(True)

        @pl.when(count <= 0)
        def _():
            scores[0] = scored(next_j, next_b, 0)

        return 0

    scores[0] = scored(0, 0, 0)
    lax.fori_loop(0, total, step, 0)
    for j in range(nq):
        parts, rows = [], []
        for h in range(2):
            mixed = (acc_ref[j, h] * (1.0 / denom[j, h : h + 1])).astype(jnp.bfloat16)
            parts.append(jnp.dot(weight_ref[h], mixed, preferred_element_type=jnp.float32))
            stat = top_ref[j, h : h + 1] * LOG2_SCALE + jnp.log2(denom[j, h : h + 1])
            for _ in range(3):
                piece = stat.astype(jnp.bfloat16).astype(jnp.float32)
                rows.append(piece)
                stat = stat - piece
        blank = jnp.zeros((CHUNK - 2 * PATCH - 6, TOK), jnp.float32)
        chunk_refs[j][...] = jnp.concatenate(parts + rows + [blank], 0).astype(jnp.bfloat16)


def attend(counts, queries, blocks, weight, extras=()):
    f32, bf16 = jnp.float32, jnp.bfloat16
    nq, nk = len(queries), len(blocks)
    work = nq * nk * 2 * TOK * TOK
    return pl.pallas_call(
        functools.partial(attention_kernel, nq=nq, nk=nk, nx=len(extras)),
        out_shape=(jax.ShapeDtypeStruct((CHUNK, TOK), bf16),) * nq,
        in_specs=[SMEM] + [ANY] * (nq + nk + 1 + len(extras)),
        out_specs=(VMEM,) * nq,
        scratch_shapes=[
            pltpu.VMEM((nq, TOK, 2 * DH), bf16),
            pltpu.VMEM((nk, TOK, 2 * DH), bf16),
            pltpu.VMEM((nk, 2, DH + 16, TOK), bf16),
            pltpu.VMEM((2, TOK, TOK), f32),
            pltpu.SemaphoreType.DMA((5 * nk + nq + 1,)),
            pltpu.VMEM((nq, 2, DH, TOK), f32),
            pltpu.VMEM((nq, 2, TOK), f32),
            pltpu.VMEM((nq, 2, TOK), f32),
            pltpu.VMEM((2, PATCH, DH), bf16),
        ],
        compiler_params=pltpu.CompilerParams(vmem_limit_bytes=24 * 2**20),
        cost_estimate=pl.CostEstimate(
            flops=work * DH * 4, transcendentals=work, bytes_accessed=(nq + 2 * nk) * TOK * 4 * DH
        ),
    )(counts, *queries, *blocks, weight, *extras)


def combine_kernel(scale_ref, place_ref, *refs):
    chunk_refs, (latent_ref, out_ref) = refs[:4], refs[4:]
    stats = []
    for h in range(2):
        base = 2 * PATCH + 3 * h
        pieces = [ref[2 * PATCH :].astype(jnp.float32) for ref in chunk_refs]
        at = base - 2 * PATCH
        stats.append([x[at : at + 1] + x[at + 1 : at + 2] + x[at + 2 : at + 3] for x in pieces])
    values = jnp.zeros((PATCH, TOK), jnp.float32)
    for h in range(2):
        peak = jnp.maximum(
            jnp.maximum(stats[h][0], stats[h][1]), jnp.maximum(stats[h][2], stats[h][3])
        )
        shares = [jnp.exp2(stat - peak) for stat in stats[h]]
        norm = scale_ref[0] / (shares[0] + shares[1] + shares[2] + shares[3])
        for ref, share in zip(chunk_refs, shares):
            values += ref[h * PATCH : (h + 1) * PATCH].astype(jnp.float32) * (share * norm)
    values = jnp.transpose(jnp.concatenate([values[32:], values, values[:32]], 0))
    values = values.reshape(ROWS, TCOLS, 128)
    lane = lax.broadcasted_iota(jnp.int32, (ROWS, TCOLS, 128), 2)
    blank = jnp.zeros((1, TCOLS, 128), jnp.float32)
    above = jnp.concatenate([blank, values[:-1]], 0)
    below = jnp.concatenate([values[1:], blank], 0)
    window = jnp.where(lane < 32, above, jnp.where(lane < 96, values, below))
    for row in range(ROWS):
        out_ref[row] = window[row].astype(jnp.bfloat16)
    band = place_ref[0]
    edge = pltpu.roll(latent_ref[...], 64, 1) * scale_ref[1]
    lane = lax.broadcasted_iota(jnp.int32, (TCOLS, 128), 1)
    for target, part in ((band + 1, lane < 32), (band - 1, lane >= 96)):

        @pl.when((target >= 0) & (target < ROWS))
        def _():
            sent = jnp.where(part, edge, 0.0)
            out_ref[target] = (out_ref[target].astype(jnp.float32) + sent).astype(jnp.bfloat16)


def combine(scale, place, chunks, latent):
    return pl.pallas_call(
        combine_kernel,
        out_shape=jax.ShapeDtypeStruct((ROWS, TCOLS, 128), jnp.bfloat16),
        in_specs=[SMEM, SMEM] + [VMEM] * 5,
        out_specs=VMEM,
        compiler_params=pltpu.CompilerParams(vmem_limit_bytes=16 * 2**20),
    )(scale, place, *chunks, latent)


def decode_kernel(
    half_ref,
    own_ref,
    last_ref,
    older_ref,
    taps_hbm,
    bias_hbm,
    gain_hbm,
    out_ref,
    taps_ref,
    even_ref,
    odd_ref,
    bias_ref,
    gain_ref,
    sems,
):
    copies = [
        pltpu.make_async_copy(taps_hbm, taps_ref, sems.at[2]),
        pltpu.make_async_copy(bias_hbm, bias_ref.at[0], sems.at[0]),
        pltpu.make_async_copy(gain_hbm, gain_ref.at[0], sems.at[1]),
    ]
    for copy in copies:
        copy.start()
    left = half_ref[0] == 0
    blank = jnp.zeros((1, 128), jnp.float32)
    even, odd = [], []
    for ref in (older_ref, last_ref, own_ref):
        block = ref[...].astype(jnp.float32)
        here = jnp.where(left, block[0:16], block[16:32])
        before = jnp.where(left, jnp.concatenate([blank, block[0:15]], 0), block[15:31])
        after = jnp.where(left, block[1:17], jnp.concatenate([block[17:32], blank], 0))
        rows = [
            jnp.concatenate([x, pltpu.roll(x, 96, 1)], 0).astype(jnp.bfloat16)
            for x in (before, here, after)
        ]
        even += rows[0:2]
        odd += rows[1:3]
    even_ref[...] = jnp.zeros(even_ref.shape, jnp.bfloat16)
    odd_ref[...] = jnp.zeros(odd_ref.shape, jnp.bfloat16)
    for copy in copies:
        copy.wait()
    for a in range(3):
        for u in range(3):
            for v in range(3):
                tap = taps_ref[a * 9 + u * 3 + v]
                for ref, place in ((even_ref, v + 1), (odd_ref, v)):
                    at = a * 256 + place // 2 * 128 + u * 32 + place % 2 * 16
                    ref[at : at + 16] = tap
    finished = []
    for parts, weight_ref in ((even, even_ref), (odd, odd_ref)):
        features = (
            jnp.dot(
                jnp.concatenate(parts, 1), weight_ref[...], preferred_element_type=jnp.float32
            )
            + bias_ref[...]
        )
        power = jnp.mean(features * features, axis=1, keepdims=True)
        scaled = features * lax.rsqrt(power + EPSILON) * gain_ref[...]
        finished.append((scaled / (1.0 + jnp.exp(-scaled))).astype(jnp.bfloat16))
    target = lax.broadcasted_iota(jnp.int32, (32, 32), 0)
    source = lax.broadcasted_iota(jnp.int32, (32, 32), 1)
    order = ((target & 1) * 16 + (target >> 1) == source).astype(jnp.float32).astype(jnp.bfloat16)
    for row in range(2):
        both = jnp.concatenate([x[row * 16 : row * 16 + 16] for x in finished], 0)
        out_ref[row] = jnp.dot(order, both, preferred_element_type=jnp.float32).astype(jnp.bfloat16)


def decode(half, own, last, older, taps, bias, gain):
    chans = bias.shape[0]
    return pl.pallas_call(
        decode_kernel,
        out_shape=jax.ShapeDtypeStruct((2, 32, chans), jnp.bfloat16),
        in_specs=[SMEM] + [VMEM] * 3 + [HBM] * 3,
        out_specs=VMEM,
        scratch_shapes=[
            pltpu.VMEM(taps.shape, taps.dtype),
            pltpu.VMEM((768, chans), taps.dtype),
            pltpu.VMEM((768, chans), taps.dtype),
            pltpu.VMEM((1, chans), jnp.float32),
            pltpu.VMEM((1, chans), jnp.float32),
            pltpu.SemaphoreType.DMA((3,)),
        ],
        compiler_params=pltpu.CompilerParams(vmem_limit_bytes=32 * 2**20),
    )(half, own, last, older, in_hbm(taps), in_hbm(bias), in_hbm(gain))


def local(
    query, keys, values, lengths, timestep, latent, head_weight, conv_weight, conv_bias, gain
):
    cfg, zh, x = lax.axis_index("cfg"), lax.axis_index("zh"), lax.axis_index("x")
    y, zl = lax.axis_index("y"), lax.axis_index("zl")
    seq = ("y", "zl")

    own = prepared(keys[0], values[0])
    blocks = [own] + [lax.ppermute(own, "y", ring(d)) for d in (1, 3, 2)]
    queries = [query[0]] + [lax.ppermute(query[0], "zl", crossed(m)) for m in (1, 2, 3)]
    block = jnp.stack([((y - d) % SIDE) * SIDE + zl for d in (0, 1, 3, 2)])
    counts = jnp.clip(lengths[0] - block * TOK, 0, TOK).astype(jnp.int32)

    rows = latent[0].reshape(2, TCOLS, 32)
    blank = jnp.zeros((TCOLS, 32), jnp.float32)
    grid = jnp.concatenate([blank, rows[0], rows[1], blank], 1)
    part = lax.dynamic_slice_in_dim(head_weight, (zh * SIDE + x) * 2 * DH, 2 * DH, 0)
    weight = part.T.reshape(PATCH, 2, DH).transpose(1, 0, 2)
    sigma = noise_level(timestep[0], STEPS)
    scale = jnp.stack(
        [
            jnp.where(cfg == 0, GUIDE, 1.0 - GUIDE).astype(jnp.float32),
            jnp.where(cfg == 0, -1.0 / sigma, 0.0),
            sigma,
        ]
    )
    place = (zh * SIDE + x).astype(jnp.int32).reshape(1)

    third, second, first = attend(counts, queries[3:0:-1], blocks, weight)
    (mine,) = attend(counts, queries[:1], blocks, weight, extras=(third,))
    chunks = [mine] + [
        lax.ppermute(chunk, "zl", crossed(m)) for m, chunk in ((3, third), (2, second), (1, first))
    ]
    shares = combine(scale, place, chunks, grid)
    shares = lax.all_to_all(shares, ("zh", "x"), 0, 0, tiled=True)
    window = lax.psum(jnp.sum(shares.astype(jnp.float32), 0), "cfg")

    current = (grid - sigma * window).astype(jnp.bfloat16)
    last = lax.ppermute(current, seq, moved(1))
    older = lax.ppermute(current, seq, moved(2))
    cells = lax.dynamic_slice_in_dim(window, cfg * (TCOLS // 2), TCOLS // 2, 0)[:, 32:96]
    velocity = cells.reshape(TCOLS // 2, 2, 2, -1).transpose(1, 0, 2, 3).reshape(1, 2, TCOLS, -1)
    decoded = decode(
        cfg.astype(jnp.int32).reshape(1),
        current,
        last,
        older,
        conv_weight.reshape(27, *conv_weight.shape[3:]),
        conv_bias,
        gain,
    )
    return (velocity, decoded[None])


def solution(mesh):
    split = Mesh(
        mesh.devices.reshape(2, SIDE, SIDE, SIDE, SIDE), ("cfg", "zh", "x", "y", "zl")
    )
    seq, band = ("y", "zl"), ("zh", "x")
    tokens = P("cfg", seq, band)
    return jax.shard_map(
        local,
        mesh=split,
        in_specs=(
            tokens,
            tokens,
            tokens,
            P(),
            P(),
            P(seq, band, None, None),
            P(),
            P(),
            P(),
            P(),
        ),
        out_specs=(P(seq, band, "cfg", None), P(seq, band, "cfg", None)),
        check_vma=False,
    )
```

```python
import functools
import math

import jax
import jax.numpy as jnp
from jax import lax
from jax.experimental import pallas as pl
from jax.experimental.pallas import tpu as pltpu
from jax.sharding import Mesh
from jax.sharding import PartitionSpec as P

DH = 128
STEPS = 50
GUIDE = 5.0
SHIFT_FACTOR = 5.0
NEG_FILL = -1e30
EPSILON = 1e-06
SIDE = 4
TOK = 512
ROWS, TCOLS = 16, 32
PATCH = 64
CHUNK = 2 * PATCH + 16
LOG2_SCALE = math.log2(math.e) / math.sqrt(DH)

VMEM = pl.BlockSpec(memory_space=pltpu.VMEM)
SMEM = pl.BlockSpec(memory_space=pltpu.SMEM)
HBM = pl.BlockSpec(memory_space=pltpu.HBM)
ANY = pl.BlockSpec(memory_space=pl.ANY)


def in_hbm(value):
    return pltpu.with_memory_space_constraint(value, pltpu.HBM)


def noise_level(timestep, total_steps):
    frac = 1.0 - timestep.astype(jnp.float32) / total_steps
    return SHIFT_FACTOR * frac / (1.0 + (SHIFT_FACTOR - 1.0) * frac)


def ring(steps):
    return [(i, (i + steps) % SIDE) for i in range(SIDE)]


def crossed(mask):
    return [(i, i ^ mask) for i in range(SIDE)]


def moved(steps):
    count = SIDE * SIDE
    return [(i, i + steps) for i in range(count) if 0 <= i + steps < count]


def prepare_kernel(keys_ref, values_ref, out_ref, values, both, sems):
    first = pltpu.make_async_copy(keys_ref, both.at[pl.ds(0, TOK)], sems.at[0])
    second = pltpu.make_async_copy(values_ref, values, sems.at[1])
    first.start()
    second.start()
    second.wait()
    for half in range(2):
        at = half * 2 * DH
        both[TOK + at : TOK + at + 2 * DH] = jnp.transpose(values[at : at + 2 * DH])
    first.wait()
    third = pltpu.make_async_copy(both, out_ref, sems.at[0])
    third.start()
    third.wait()


def prepared(keys, values):
    return pl.pallas_call(
        prepare_kernel,
        out_shape=pltpu.HBM((2 * TOK, 2 * DH), jnp.bfloat16),
        in_specs=[HBM] * 2,
        out_specs=HBM,
        scratch_shapes=[
            pltpu.VMEM((TOK, 2 * DH), jnp.bfloat16),
            pltpu.VMEM((2 * TOK, 2 * DH), jnp.bfloat16),
            pltpu.SemaphoreType.DMA((2,)),
        ],
    )(in_hbm(keys), in_hbm(values))


def attention_kernel(count_ref, *refs, nq, nk, nx):
    refs = list(refs)

    def take(size):
        taken = refs[:size]
        del refs[:size]
        return taken

    q_refs, kv_refs = take(nq), take(nk)
    weight_hbm = take(1 + nx)[0]
    chunk_refs = take(nq)
    qs, ks, vs, scores, sems, acc_ref, top_ref, denom, weight_ref = refs

    sem = iter(range(64))

    def copied(source, target):
        copy = pltpu.make_async_copy(source, target, sems.at[next(sem)])
        copy.start()
        return copy

    arriving = []
    for b in range(nk):
        keys, values = kv_refs[b].at[pl.ds(0, TOK)], kv_refs[b].at[pl.ds(TOK, TOK)]
        group = [copied(keys, ks.at[b])]
        for half in range(2):
            for h in range(2):
                group.append(
                    copied(
                        values.at[pl.ds(half * 2 * DH + h * DH, DH)],
                        vs.at[b, h, pl.ds(0, DH), pl.ds(half * 2 * DH, 2 * DH)],
                    )
                )
        if b == 0:
            group += [copied(q_refs[j], qs.at[j]) for j in range(nq)]
        arriving.append(group)
    arriving[0].append(copied(weight_hbm, weight_ref))
    top_ref[...] = jnp.full((nq, 2, TOK), NEG_FILL, jnp.float32)
    denom[...] = jnp.zeros((nq, 2, TOK), jnp.float32)
    acc_ref[...] = jnp.zeros((nq, 2, DH, TOK), jnp.float32)
    for b in range(nk):
        for h in range(2):
            vs[b, h, DH:] = jnp.ones((16, TOK), jnp.bfloat16)
    for copy in arriving[0]:
        copy.wait()

    def scored(j, b, h):
        return lax.dot_general(
            ks[b, :, h * DH : (h + 1) * DH],
            qs[j, :, h * DH : (h + 1) * DH],
            (((1,), (1,)), ((), ())),
            preferred_element_type=jnp.float32,
        )

    def folded(j, b, h, score, masked):
        if masked:
            valid = lax.broadcasted_iota(jnp.int32, (TOK, TOK), 0) < count_ref[b]
            score = jnp.where(valid, score, NEG_FILL)
        old = top_ref[j, h : h + 1]
        new = jnp.maximum(old, jnp.max(score, axis=0, keepdims=True))
        weights = jnp.exp2((score - new) * LOG2_SCALE)
        if masked:
            weights = jnp.where(valid, weights, 0.0)
        factor = jnp.exp2((old - new) * LOG2_SCALE)
        top_ref[j, h : h + 1] = new
        mixed = jnp.dot(vs[b, h], weights.astype(jnp.bfloat16), preferred_element_type=jnp.float32)
        denom[j, h : h + 1] = denom[j, h : h + 1] * factor + mixed[DH : DH + 1]
        acc_ref[j, h] = acc_ref[j, h] * factor + mixed[:DH]

    total = nq * nk

    def step(t, _):
        j, b = lax.div(t, nk), lax.rem(t, nk)
        later = jnp.minimum(t + 1, total - 1)
        next_j, next_b = lax.div(later, nk), lax.rem(later, nk)
        count = count_ref[b]
        for needed in range(1, nk):

            @pl.when(t == needed - 1)
            def _():
                for copy in arriving[needed]:
                    copy.wait()

        def update(masked):
            scores[1] = scored(j, b, 1)
            folded(j, b, 0, scores[0], masked)
            scores[0] = scored(next_j, next_b, 0)
            folded(j, b, 1, scores[1], masked)

        @pl.when(count >= TOK)
        def _():
            update(False)

        @pl.when((count > 0) & (count < TOK))
        def _():
            update(True)

        @pl.when(count <= 0)
        def _():
            scores[0] = scored(next_j, next_b, 0)

        return 0

    scores[0] = scored(0, 0, 0)
    lax.fori_loop(0, total, step, 0)
    for j in range(nq):
        parts, rows = [], []
        for h in range(2):
            mixed = (acc_ref[j, h] * (1.0 / denom[j, h : h + 1])).astype(jnp.bfloat16)
            parts.append(jnp.dot(weight_ref[h], mixed, preferred_element_type=jnp.float32))
            stat = top_ref[j, h : h + 1] * LOG2_SCALE + jnp.log2(denom[j, h : h + 1])
            for _ in range(3):
                piece = stat.astype(jnp.bfloat16).astype(jnp.float32)
                rows.append(piece)
                stat = stat - piece
        blank = jnp.zeros((CHUNK - 2 * PATCH - 6, TOK), jnp.float32)
        chunk_refs[j][...] = jnp.concatenate(parts + rows + [blank], 0).astype(jnp.bfloat16)


def attend(counts, queries, blocks, weight, extras=()):
    f32, bf16 = jnp.float32, jnp.bfloat16
    nq, nk = len(queries), len(blocks)
    work = nq * nk * 2 * TOK * TOK
    return pl.pallas_call(
        functools.partial(attention_kernel, nq=nq, nk=nk, nx=len(extras)),
        out_shape=(jax.ShapeDtypeStruct((CHUNK, TOK), bf16),) * nq,
        in_specs=[SMEM] + [ANY] * (nq + nk + 1 + len(extras)),
        out_specs=(VMEM,) * nq,
        scratch_shapes=[
            pltpu.VMEM((nq, TOK, 2 * DH), bf16),
            pltpu.VMEM((nk, TOK, 2 * DH), bf16),
            pltpu.VMEM((nk, 2, DH + 16, TOK), bf16),
            pltpu.VMEM((2, TOK, TOK), f32),
            pltpu.SemaphoreType.DMA((5 * nk + nq + 1,)),
            pltpu.VMEM((nq, 2, DH, TOK), f32),
            pltpu.VMEM((nq, 2, TOK), f32),
            pltpu.VMEM((nq, 2, TOK), f32),
            pltpu.VMEM((2, PATCH, DH), bf16),
        ],
        compiler_params=pltpu.CompilerParams(vmem_limit_bytes=24 * 2**20),
        cost_estimate=pl.CostEstimate(
            flops=work * DH * 4, transcendentals=work, bytes_accessed=(nq + 2 * nk) * TOK * 4 * DH
        ),
    )(counts, *queries, *blocks, weight, *extras)


def combine_kernel(scale_ref, place_ref, *refs):
    chunk_refs, (latent_ref, out_ref) = refs[:4], refs[4:]
    stats = []
    for h in range(2):
        base = 2 * PATCH + 3 * h
        pieces = [ref[2 * PATCH :].astype(jnp.float32) for ref in chunk_refs]
        at = base - 2 * PATCH
        stats.append([x[at : at + 1] + x[at + 1 : at + 2] + x[at + 2 : at + 3] for x in pieces])
    values = jnp.zeros((PATCH, TOK), jnp.float32)
    for h in range(2):
        peak = jnp.maximum(
            jnp.maximum(stats[h][0], stats[h][1]), jnp.maximum(stats[h][2], stats[h][3])
        )
        shares = [jnp.exp2(stat - peak) for stat in stats[h]]
        norm = scale_ref[0] / (shares[0] + shares[1] + shares[2] + shares[3])
        for ref, share in zip(chunk_refs, shares):
            values += ref[h * PATCH : (h + 1) * PATCH].astype(jnp.float32) * (share * norm)
    values = jnp.transpose(jnp.concatenate([values[32:], values, values[:32]], 0))
    values = values.reshape(ROWS, TCOLS, 128)
    lane = lax.broadcasted_iota(jnp.int32, (ROWS, TCOLS, 128), 2)
    blank = jnp.zeros((1, TCOLS, 128), jnp.float32)
    above = jnp.concatenate([blank, values[:-1]], 0)
    below = jnp.concatenate([values[1:], blank], 0)
    window = jnp.where(lane < 32, above, jnp.where(lane < 96, values, below))
    for row in range(ROWS):
        out_ref[row] = window[row].astype(jnp.bfloat16)
    band = place_ref[0]
    edge = pltpu.roll(latent_ref[...], 64, 1) * scale_ref[1]
    lane = lax.broadcasted_iota(jnp.int32, (TCOLS, 128), 1)
    for target, part in ((band + 1, lane < 32), (band - 1, lane >= 96)):

        @pl.when((target >= 0) & (target < ROWS))
        def _():
            sent = jnp.where(part, edge, 0.0)
            out_ref[target] = (out_ref[target].astype(jnp.float32) + sent).astype(jnp.bfloat16)


def combine(scale, place, chunks, latent):
    return pl.pallas_call(
        combine_kernel,
        out_shape=jax.ShapeDtypeStruct((ROWS, TCOLS, 128), jnp.bfloat16),
        in_specs=[SMEM, SMEM] + [VMEM] * 5,
        out_specs=VMEM,
        compiler_params=pltpu.CompilerParams(vmem_limit_bytes=16 * 2**20),
    )(scale, place, *chunks, latent)


def laid_kernel(taps_hbm, bias_hbm, gain_hbm, _, even_ref, odd_ref, bias_ref, gain_ref, taps_ref, sems):
    copies = [
        pltpu.make_async_copy(taps_hbm, taps_ref, sems.at[0]),
        pltpu.make_async_copy(bias_hbm, bias_ref.at[0], sems.at[1]),
        pltpu.make_async_copy(gain_hbm, gain_ref.at[0], sems.at[2]),
    ]
    for copy in copies:
        copy.start()
    even_ref[...] = jnp.zeros(even_ref.shape, jnp.bfloat16)
    odd_ref[...] = jnp.zeros(odd_ref.shape, jnp.bfloat16)
    for copy in copies:
        copy.wait()
    for a in range(3):
        for u in range(3):
            for v in range(3):
                tap = taps_ref[a * 9 + u * 3 + v]
                for ref, place in ((even_ref, v + 1), (odd_ref, v)):
                    at = a * 256 + place // 2 * 128 + u * 32 + place % 2 * 16
                    ref[at : at + 16] = tap


def laid(taps, bias, gain, after):
    chans = taps.shape[-1]
    matrix = jax.ShapeDtypeStruct((768, chans), jnp.bfloat16)
    row = jax.ShapeDtypeStruct((1, chans), jnp.float32)
    return pl.pallas_call(
        laid_kernel,
        out_shape=(matrix, matrix, row, row),
        in_specs=[HBM] * 3 + [ANY],
        out_specs=(VMEM,) * 4,
        scratch_shapes=[pltpu.VMEM(taps.shape, taps.dtype), pltpu.SemaphoreType.DMA((3,))],
        compiler_params=pltpu.CompilerParams(vmem_limit_bytes=16 * 2**20),
    )(in_hbm(taps), in_hbm(bias), in_hbm(gain), after)


def decode_kernel(half_ref, own_ref, last_ref, older_ref, even_ref, odd_ref, bias_ref, gain_ref, out_ref):
    left = half_ref[0] == 0
    blank = jnp.zeros((1, 128), jnp.float32)
    even, odd = [], []
    for ref in (older_ref, last_ref, own_ref):
        block = ref[...].astype(jnp.float32)
        here = jnp.where(left, block[0:16], block[16:32])
        before = jnp.where(left, jnp.concatenate([blank, block[0:15]], 0), block[15:31])
        after = jnp.where(left, block[1:17], jnp.concatenate([block[17:32], blank], 0))
        rows = [
            jnp.concatenate([x, pltpu.roll(x, 96, 1)], 0).astype(jnp.bfloat16)
            for x in (before, here, after)
        ]
        even += rows[0:2]
        odd += rows[1:3]
    finished = []
    for parts, weight_ref in ((even, even_ref), (odd, odd_ref)):
        features = (
            jnp.dot(
                jnp.concatenate(parts, 1), weight_ref[...], preferred_element_type=jnp.float32
            )
            + bias_ref[...]
        )
        power = jnp.mean(features * features, axis=1, keepdims=True)
        scaled = features * lax.rsqrt(power + EPSILON) * gain_ref[...]
        finished.append((scaled / (1.0 + jnp.exp(-scaled))).astype(jnp.bfloat16))
    target = lax.broadcasted_iota(jnp.int32, (32, 32), 0)
    source = lax.broadcasted_iota(jnp.int32, (32, 32), 1)
    order = ((target & 1) * 16 + (target >> 1) == source).astype(jnp.float32).astype(jnp.bfloat16)
    for row in range(2):
        both = jnp.concatenate([x[row * 16 : row * 16 + 16] for x in finished], 0)
        out_ref[row] = jnp.dot(order, both, preferred_element_type=jnp.float32).astype(jnp.bfloat16)


def decode(half, own, last, older, even, odd, bias, gain):
    chans = bias.shape[1]
    return pl.pallas_call(
        decode_kernel,
        out_shape=jax.ShapeDtypeStruct((2, 32, chans), jnp.bfloat16),
        in_specs=[SMEM] + [VMEM] * 7,
        out_specs=VMEM,
        compiler_params=pltpu.CompilerParams(vmem_limit_bytes=32 * 2**20),
    )(half, own, last, older, even, odd, bias, gain)


def local(
    query, keys, values, lengths, timestep, latent, head_weight, conv_weight, conv_bias, gain
):
    cfg, zh, x = lax.axis_index("cfg"), lax.axis_index("zh"), lax.axis_index("x")
    y, zl = lax.axis_index("y"), lax.axis_index("zl")
    seq = ("y", "zl")

    own = prepared(keys[0], values[0])
    blocks = [own] + [lax.ppermute(own, "y", ring(d)) for d in (1, 3, 2)]
    queries = [query[0]] + [lax.ppermute(query[0], "zl", crossed(m)) for m in (1, 2, 3)]
    block = jnp.stack([((y - d) % SIDE) * SIDE + zl for d in (0, 1, 3, 2)])
    counts = jnp.clip(lengths[0] - block * TOK, 0, TOK).astype(jnp.int32)

    rows = latent[0].reshape(2, TCOLS, 32)
    blank = jnp.zeros((TCOLS, 32), jnp.float32)
    grid = jnp.concatenate([blank, rows[0], rows[1], blank], 1)
    part = lax.dynamic_slice_in_dim(head_weight, (zh * SIDE + x) * 2 * DH, 2 * DH, 0)
    weight = part.T.reshape(PATCH, 2, DH).transpose(1, 0, 2)
    sigma = noise_level(timestep[0], STEPS)
    scale = jnp.stack(
        [
            jnp.where(cfg == 0, GUIDE, 1.0 - GUIDE).astype(jnp.float32),
            jnp.where(cfg == 0, -1.0 / sigma, 0.0),
            sigma,
        ]
    )
    place = (zh * SIDE + x).astype(jnp.int32).reshape(1)

    third, second, first = attend(counts, queries[3:0:-1], blocks, weight)
    (mine,) = attend(counts, queries[:1], blocks, weight, extras=(third,))
    chunks = [mine] + [
        lax.ppermute(chunk, "zl", crossed(m)) for m, chunk in ((3, third), (2, second), (1, first))
    ]
    shares = combine(scale, place, chunks, grid)
    shares = lax.all_to_all(shares, ("zh", "x"), 0, 0, tiled=True)
    window = lax.psum(jnp.sum(shares.astype(jnp.float32), 0), "cfg")

    current = (grid - sigma * window).astype(jnp.bfloat16)
    last = lax.ppermute(current, seq, moved(1))
    older = lax.ppermute(current, seq, moved(2))
    cells = lax.dynamic_slice_in_dim(window, cfg * (TCOLS // 2), TCOLS // 2, 0)[:, 32:96]
    velocity = cells.reshape(TCOLS // 2, 2, 2, -1).transpose(1, 0, 2, 3).reshape(1, 2, TCOLS, -1)
    decoded = decode(
        cfg.astype(jnp.int32).reshape(1),
        current,
        last,
        older,
        *laid(conv_weight.reshape(27, *conv_weight.shape[3:]), conv_bias, gain, current),
    )
    return (velocity, decoded[None])


def solution(mesh):
    split = Mesh(
        mesh.devices.reshape(2, SIDE, SIDE, SIDE, SIDE), ("cfg", "zh", "x", "y", "zl")
    )
    seq, band = ("y", "zl"), ("zh", "x")
    tokens = P("cfg", seq, band)
    return jax.shard_map(
        local,
        mesh=split,
        in_specs=(
            tokens,
            tokens,
            tokens,
            P(),
            P(),
            P(seq, band, None, None),
            P(),
            P(),
            P(),
            P(),
        ),
        out_specs=(P(seq, band, "cfg", None), P(seq, band, "cfg", None)),
        check_vma=False,
    )
```

```python
import functools
import math

import jax
import jax.numpy as jnp
from jax import lax
from jax.experimental import pallas as pl
from jax.experimental.pallas import tpu as pltpu
from jax.sharding import Mesh
from jax.sharding import PartitionSpec as P

DH = 128
STEPS = 50
GUIDE = 5.0
SHIFT_FACTOR = 5.0
NEG_FILL = -1e30
EPSILON = 1e-06
SIDE = 4
TOK = 512
ROWS, TCOLS = 16, 32
PATCH = 64
CHUNK = 2 * PATCH + 16
LOG2_SCALE = math.log2(math.e) / math.sqrt(DH)

VMEM = pl.BlockSpec(memory_space=pltpu.VMEM)
SMEM = pl.BlockSpec(memory_space=pltpu.SMEM)
HBM = pl.BlockSpec(memory_space=pltpu.HBM)
ANY = pl.BlockSpec(memory_space=pl.ANY)


def in_hbm(value):
    return pltpu.with_memory_space_constraint(value, pltpu.HBM)


def noise_level(timestep, total_steps):
    frac = 1.0 - timestep.astype(jnp.float32) / total_steps
    return SHIFT_FACTOR * frac / (1.0 + (SHIFT_FACTOR - 1.0) * frac)


def ring(steps):
    return [(i, (i + steps) % SIDE) for i in range(SIDE)]


def crossed(mask):
    return [(i, i ^ mask) for i in range(SIDE)]


def moved(steps):
    count = SIDE * SIDE
    return [(i, i + steps) for i in range(count) if 0 <= i + steps < count]


def prepare_kernel(keys_ref, values_ref, out_ref, values, both, sems):
    first = pltpu.make_async_copy(keys_ref, both.at[pl.ds(0, TOK)], sems.at[0])
    second = pltpu.make_async_copy(values_ref, values, sems.at[1])
    first.start()
    second.start()
    second.wait()
    for half in range(2):
        at = half * 2 * DH
        both[TOK + at : TOK + at + 2 * DH] = jnp.transpose(values[at : at + 2 * DH])
    first.wait()
    third = pltpu.make_async_copy(both, out_ref, sems.at[0])
    third.start()
    third.wait()


def prepared(keys, values):
    return pl.pallas_call(
        prepare_kernel,
        out_shape=pltpu.HBM((2 * TOK, 2 * DH), jnp.bfloat16),
        in_specs=[HBM] * 2,
        out_specs=HBM,
        scratch_shapes=[
            pltpu.VMEM((TOK, 2 * DH), jnp.bfloat16),
            pltpu.VMEM((2 * TOK, 2 * DH), jnp.bfloat16),
            pltpu.SemaphoreType.DMA((2,)),
        ],
    )(in_hbm(keys), in_hbm(values))


def attention_kernel(count_ref, *refs, nq, nk, nx, parts, skip, last):
    refs = list(refs)

    def take(size):
        taken = refs[:size]
        del refs[:size]
        return taken

    q_refs, kv_refs = take(nq), take(nk)
    weight_hbm = take(1)[0] if last else None
    if parts:
        top_in, denom_in, acc_in = take(3)
    take(nx)
    if last:
        chunk_refs = take(nq)
        qs, ks, vs, scores, sems, acc_ref, top_ref, denom, weight_ref = refs
    else:
        top_ref, denom, acc_out = take(3)
        qs, ks, vs, scores, sems, acc_ref = refs

    sem = iter(range(64))

    def copied(source, target):
        copy = pltpu.make_async_copy(source, target, sems.at[next(sem)])
        copy.start()
        return copy

    arriving = []
    for b in range(nk):
        keys, values = kv_refs[b].at[pl.ds(0, TOK)], kv_refs[b].at[pl.ds(TOK, TOK)]
        group = [copied(keys, ks.at[b])]
        for half in range(2):
            for h in range(2):
                group.append(
                    copied(
                        values.at[pl.ds(half * 2 * DH + h * DH, DH)],
                        vs.at[b, h, pl.ds(0, DH), pl.ds(half * 2 * DH, 2 * DH)],
                    )
                )
        if b == 0:
            group += [copied(q_refs[j], qs.at[j]) for j in range(nq)]
        arriving.append(group)
    if last:
        arriving[0].append(copied(weight_hbm, weight_ref))
    if parts:
        arriving[0].append(copied(acc_in, acc_ref.at[pl.ds(0, parts)]))
        top_ref[:parts] = top_in[...]
        denom[:parts] = denom_in[...]
        arriving = [[copy for group in arriving for copy in group]] + [[]] * (nk - 1)
    fresh = nq - parts
    top_ref[parts:] = jnp.full((fresh, 2, TOK), NEG_FILL, jnp.float32)
    denom[parts:] = jnp.zeros((fresh, 2, TOK), jnp.float32)
    acc_ref[parts:] = jnp.zeros((fresh, 2, DH, TOK), jnp.float32)
    for b in range(nk):
        for h in range(2):
            vs[b, h, DH:] = jnp.ones((16, TOK), jnp.bfloat16)
    for copy in arriving[0]:
        copy.wait()

    def scored(j, b, h):
        return lax.dot_general(
            ks[b, :, h * DH : (h + 1) * DH],
            qs[j, :, h * DH : (h + 1) * DH],
            (((1,), (1,)), ((), ())),
            preferred_element_type=jnp.float32,
        )

    def folded(j, b, h, score, masked):
        if masked:
            valid = lax.broadcasted_iota(jnp.int32, (TOK, TOK), 0) < count_ref[b]
            score = jnp.where(valid, score, NEG_FILL)
        old = top_ref[j, h : h + 1]
        new = jnp.maximum(old, jnp.max(score, axis=0, keepdims=True))
        weights = jnp.exp2((score - new) * LOG2_SCALE)
        if masked:
            weights = jnp.where(valid, weights, 0.0)
        factor = jnp.exp2((old - new) * LOG2_SCALE)
        top_ref[j, h : h + 1] = new
        mixed = jnp.dot(vs[b, h], weights.astype(jnp.bfloat16), preferred_element_type=jnp.float32)
        denom[j, h : h + 1] = denom[j, h : h + 1] * factor + mixed[DH : DH + 1]
        acc_ref[j, h] = acc_ref[j, h] * factor + mixed[:DH]

    total = nq * nk - parts * skip

    def tile(t):
        if not parts:
            return lax.div(t, nk), lax.rem(t, nk)
        rest = nk - skip
        past = t - parts * rest
        j = jnp.where(past >= 0, parts + lax.div(past, nk), lax.div(t, rest))
        b = jnp.where(past >= 0, lax.rem(past, nk), skip + lax.rem(t, rest))
        return j, b

    def step(t, _):
        j, b = tile(t)
        next_j, next_b = tile(jnp.minimum(t + 1, total - 1))
        count = count_ref[b]
        for needed in range(1, nk if not parts else 1):

            @pl.when(t == needed - 1)
            def _():
                for copy in arriving[needed]:
                    copy.wait()

        def update(masked):
            scores[1] = scored(j, b, 1)
            folded(j, b, 0, scores[0], masked)
            scores[0] = scored(next_j, next_b, 0)
            folded(j, b, 1, scores[1], masked)

        @pl.when(count >= TOK)
        def _():
            update(False)

        @pl.when((count > 0) & (count < TOK))
        def _():
            update(True)

        @pl.when(count <= 0)
        def _():
            scores[0] = scored(next_j, next_b, 0)

        return 0

    scores[0] = scored(0, skip, 0)
    lax.fori_loop(0, total, step, 0)
    if not last:
        copy = pltpu.make_async_copy(acc_ref, acc_out, sems.at[0])
        copy.start()
        copy.wait()
        return
    for j in range(nq):
        parts, rows = [], []
        for h in range(2):
            mixed = (acc_ref[j, h] * (1.0 / denom[j, h : h + 1])).astype(jnp.bfloat16)
            parts.append(jnp.dot(weight_ref[h], mixed, preferred_element_type=jnp.float32))
            stat = top_ref[j, h : h + 1] * LOG2_SCALE + jnp.log2(denom[j, h : h + 1])
            for _ in range(3):
                piece = stat.astype(jnp.bfloat16).astype(jnp.float32)
                rows.append(piece)
                stat = stat - piece
        blank = jnp.zeros((CHUNK - 2 * PATCH - 6, TOK), jnp.float32)
        chunk_refs[j][...] = jnp.concatenate(parts + rows + [blank], 0).astype(jnp.bfloat16)


def attend(counts, queries, blocks, weight=None, extras=(), state=(), skip=0):
    f32, bf16 = jnp.float32, jnp.bfloat16
    nq, nk, last = len(queries), len(blocks), weight is not None
    parts = state[0].shape[0] if state else 0
    work = (nq * nk - parts * skip) * 2 * TOK * TOK
    stat = jax.ShapeDtypeStruct((nq, 2, TOK), f32)
    chunk = jax.ShapeDtypeStruct((CHUNK, TOK), bf16)
    ended = [
        pltpu.VMEM((nq, 2, TOK), f32),
        pltpu.VMEM((nq, 2, TOK), f32),
        pltpu.VMEM((2, PATCH, DH), bf16),
    ]
    return pl.pallas_call(
        functools.partial(
            attention_kernel, nq=nq, nk=nk, nx=len(extras), parts=parts, skip=skip, last=last
        ),
        out_shape=(chunk,) * nq if last else (stat, stat, pltpu.HBM((nq, 2, DH, TOK), f32)),
        in_specs=[SMEM]
        + [ANY] * (nq + nk + last)
        + ([VMEM, VMEM, HBM] if state else [])
        + [ANY] * len(extras),
        out_specs=(VMEM,) * nq if last else (VMEM, VMEM, HBM),
        scratch_shapes=[
            pltpu.VMEM((nq, TOK, 2 * DH), bf16),
            pltpu.VMEM((nk, TOK, 2 * DH), bf16),
            pltpu.VMEM((nk, 2, DH + 16, TOK), bf16),
            pltpu.VMEM((2, TOK, TOK), f32),
            pltpu.SemaphoreType.DMA((5 * nk + nq + 2,)),
            pltpu.VMEM((nq, 2, DH, TOK), f32),
        ]
        + (ended if last else []),
        compiler_params=pltpu.CompilerParams(vmem_limit_bytes=24 * 2**20),
        cost_estimate=pl.CostEstimate(
            flops=work * DH * 4, transcendentals=work, bytes_accessed=(nq + 2 * nk) * TOK * 4 * DH
        ),
    )(
        counts,
        *queries,
        *blocks,
        *((weight,) if last else ()),
        *(in_hbm(x) if x.ndim == 4 else x for x in state),
        *extras,
    )


def combine_kernel(scale_ref, place_ref, *refs):
    chunk_refs, (latent_ref, out_ref) = refs[:4], refs[4:]
    stats = []
    for h in range(2):
        base = 2 * PATCH + 3 * h
        pieces = [ref[2 * PATCH :].astype(jnp.float32) for ref in chunk_refs]
        at = base - 2 * PATCH
        stats.append([x[at : at + 1] + x[at + 1 : at + 2] + x[at + 2 : at + 3] for x in pieces])
    values = jnp.zeros((PATCH, TOK), jnp.float32)
    for h in range(2):
        peak = jnp.maximum(
            jnp.maximum(stats[h][0], stats[h][1]), jnp.maximum(stats[h][2], stats[h][3])
        )
        shares = [jnp.exp2(stat - peak) for stat in stats[h]]
        norm = scale_ref[0] / (shares[0] + shares[1] + shares[2] + shares[3])
        for ref, share in zip(chunk_refs, shares):
            values += ref[h * PATCH : (h + 1) * PATCH].astype(jnp.float32) * (share * norm)
    values = jnp.transpose(jnp.concatenate([values[32:], values, values[:32]], 0))
    values = values.reshape(ROWS, TCOLS, 128)
    lane = lax.broadcasted_iota(jnp.int32, (ROWS, TCOLS, 128), 2)
    blank = jnp.zeros((1, TCOLS, 128), jnp.float32)
    above = jnp.concatenate([blank, values[:-1]], 0)
    below = jnp.concatenate([values[1:], blank], 0)
    window = jnp.where(lane < 32, above, jnp.where(lane < 96, values, below))
    for row in range(ROWS):
        out_ref[row] = window[row].astype(jnp.bfloat16)
    band = place_ref[0]
    edge = pltpu.roll(latent_ref[...], 64, 1) * scale_ref[1]
    lane = lax.broadcasted_iota(jnp.int32, (TCOLS, 128), 1)
    for target, part in ((band + 1, lane < 32), (band - 1, lane >= 96)):

        @pl.when((target >= 0) & (target < ROWS))
        def _():
            sent = jnp.where(part, edge, 0.0)
            out_ref[target] = (out_ref[target].astype(jnp.float32) + sent).astype(jnp.bfloat16)


def combine(scale, place, chunks, latent):
    return pl.pallas_call(
        combine_kernel,
        out_shape=jax.ShapeDtypeStruct((ROWS, TCOLS, 128), jnp.bfloat16),
        in_specs=[SMEM, SMEM] + [VMEM] * 5,
        out_specs=VMEM,
        compiler_params=pltpu.CompilerParams(vmem_limit_bytes=16 * 2**20),
    )(scale, place, *chunks, latent)


def laid_kernel(taps_hbm, bias_hbm, gain_hbm, _, even_ref, odd_ref, bias_ref, gain_ref, taps_ref, sems):
    copies = [
        pltpu.make_async_copy(taps_hbm, taps_ref, sems.at[0]),
        pltpu.make_async_copy(bias_hbm, bias_ref.at[0], sems.at[1]),
        pltpu.make_async_copy(gain_hbm, gain_ref.at[0], sems.at[2]),
    ]
    for copy in copies:
        copy.start()
    even_ref[...] = jnp.zeros(even_ref.shape, jnp.bfloat16)
    odd_ref[...] = jnp.zeros(odd_ref.shape, jnp.bfloat16)
    for copy in copies:
        copy.wait()
    for a in range(3):
        for u in range(3):
            for v in range(3):
                tap = taps_ref[a * 9 + u * 3 + v]
                for ref, place in ((even_ref, v + 1), (odd_ref, v)):
                    at = a * 256 + place // 2 * 128 + u * 32 + place % 2 * 16
                    ref[at : at + 16] = tap


def laid(taps, bias, gain, after):
    chans = taps.shape[-1]
    matrix = jax.ShapeDtypeStruct((768, chans), jnp.bfloat16)
    row = jax.ShapeDtypeStruct((1, chans), jnp.float32)
    return pl.pallas_call(
        laid_kernel,
        out_shape=(matrix, matrix, row, row),
        in_specs=[HBM] * 3 + [ANY],
        out_specs=(VMEM,) * 4,
        scratch_shapes=[pltpu.VMEM(taps.shape, taps.dtype), pltpu.SemaphoreType.DMA((3,))],
        compiler_params=pltpu.CompilerParams(vmem_limit_bytes=16 * 2**20),
    )(in_hbm(taps), in_hbm(bias), in_hbm(gain), after)


def decode_kernel(half_ref, own_ref, last_ref, older_ref, even_ref, odd_ref, bias_ref, gain_ref, out_ref):
    left = half_ref[0] == 0
    blank = jnp.zeros((1, 128), jnp.float32)
    even, odd = [], []
    for ref in (older_ref, last_ref, own_ref):
        block = ref[...].astype(jnp.float32)
        here = jnp.where(left, block[0:16], block[16:32])
        before = jnp.where(left, jnp.concatenate([blank, block[0:15]], 0), block[15:31])
        after = jnp.where(left, block[1:17], jnp.concatenate([block[17:32], blank], 0))
        rows = [
            jnp.concatenate([x, pltpu.roll(x, 96, 1)], 0).astype(jnp.bfloat16)
            for x in (before, here, after)
        ]
        even += rows[0:2]
        odd += rows[1:3]
    finished = []
    for parts, weight_ref in ((even, even_ref), (odd, odd_ref)):
        features = (
            jnp.dot(
                jnp.concatenate(parts, 1), weight_ref[...], preferred_element_type=jnp.float32
            )
            + bias_ref[...]
        )
        power = jnp.mean(features * features, axis=1, keepdims=True)
        scaled = features * lax.rsqrt(power + EPSILON) * gain_ref[...]
        finished.append((scaled / (1.0 + jnp.exp(-scaled))).astype(jnp.bfloat16))
    target = lax.broadcasted_iota(jnp.int32, (32, 32), 0)
    source = lax.broadcasted_iota(jnp.int32, (32, 32), 1)
    order = ((target & 1) * 16 + (target >> 1) == source).astype(jnp.float32).astype(jnp.bfloat16)
    for row in range(2):
        both = jnp.concatenate([x[row * 16 : row * 16 + 16] for x in finished], 0)
        out_ref[row] = jnp.dot(order, both, preferred_element_type=jnp.float32).astype(jnp.bfloat16)


def decode(half, own, last, older, even, odd, bias, gain):
    chans = bias.shape[1]
    return pl.pallas_call(
        decode_kernel,
        out_shape=jax.ShapeDtypeStruct((2, 32, chans), jnp.bfloat16),
        in_specs=[SMEM] + [VMEM] * 7,
        out_specs=VMEM,
        compiler_params=pltpu.CompilerParams(vmem_limit_bytes=32 * 2**20),
    )(half, own, last, older, even, odd, bias, gain)


def local(
    query, keys, values, lengths, timestep, latent, head_weight, conv_weight, conv_bias, gain
):
    cfg, zh, x = lax.axis_index("cfg"), lax.axis_index("zh"), lax.axis_index("x")
    y, zl = lax.axis_index("y"), lax.axis_index("zl")
    seq = ("y", "zl")

    own = prepared(keys[0], values[0])
    blocks = [own] + [lax.ppermute(own, "y", ring(d)) for d in (1, 3, 2)]
    queries = [query[0]] + [lax.ppermute(query[0], "zl", crossed(m)) for m in (1, 2, 3)]
    block = jnp.stack([((y - d) % SIDE) * SIDE + zl for d in (0, 1, 3, 2)])
    counts = jnp.clip(lengths[0] - block * TOK, 0, TOK).astype(jnp.int32)

    rows = latent[0].reshape(2, TCOLS, 32)
    blank = jnp.zeros((TCOLS, 32), jnp.float32)
    grid = jnp.concatenate([blank, rows[0], rows[1], blank], 1)
    part = lax.dynamic_slice_in_dim(head_weight, (zh * SIDE + x) * 2 * DH, 2 * DH, 0)
    weight = part.T.reshape(PATCH, 2, DH).transpose(1, 0, 2)
    sigma = noise_level(timestep[0], STEPS)
    scale = jnp.stack(
        [
            jnp.where(cfg == 0, GUIDE, 1.0 - GUIDE).astype(jnp.float32),
            jnp.where(cfg == 0, -1.0 / sigma, 0.0),
            sigma,
        ]
    )
    place = (zh * SIDE + x).astype(jnp.int32).reshape(1)

    early = attend(counts, queries[3:1:-1], blocks[:2])
    third, second, first = attend(
        counts, queries[3:0:-1], blocks, weight, state=early, skip=2
    )
    (mine,) = attend(counts, queries[:1], blocks, weight, extras=(third,))
    chunks = [mine] + [
        lax.ppermute(chunk, "zl", crossed(m)) for m, chunk in ((3, third), (2, second), (1, first))
    ]
    shares = combine(scale, place, chunks, grid)
    shares = lax.all_to_all(shares, ("zh", "x"), 0, 0, tiled=True)
    window = lax.psum(jnp.sum(shares.astype(jnp.float32), 0), "cfg")

    current = (grid - sigma * window).astype(jnp.bfloat16)
    last = lax.ppermute(current, seq, moved(1))
    older = lax.ppermute(current, seq, moved(2))
    cells = lax.dynamic_slice_in_dim(window, cfg * (TCOLS // 2), TCOLS // 2, 0)[:, 32:96]
    velocity = cells.reshape(TCOLS // 2, 2, 2, -1).transpose(1, 0, 2, 3).reshape(1, 2, TCOLS, -1)
    decoded = decode(
        cfg.astype(jnp.int32).reshape(1),
        current,
        last,
        older,
        *laid(conv_weight.reshape(27, *conv_weight.shape[3:]), conv_bias, gain, current),
    )
    return (velocity, decoded[None])


def solution(mesh):
    split = Mesh(
        mesh.devices.reshape(2, SIDE, SIDE, SIDE, SIDE), ("cfg", "zh", "x", "y", "zl")
    )
    seq, band = ("y", "zl"), ("zh", "x")
    tokens = P("cfg", seq, band)
    return jax.shard_map(
        local,
        mesh=split,
        in_specs=(
            tokens,
            tokens,
            tokens,
            P(),
            P(),
            P(seq, band, None, None),
            P(),
            P(),
            P(),
            P(),
        ),
        out_specs=(P(seq, band, "cfg", None), P(seq, band, "cfg", None)),
        check_vma=False,
    )
```

```python
import functools
import math

import jax
import jax.numpy as jnp
from jax import lax
from jax.experimental import pallas as pl
from jax.experimental.pallas import tpu as pltpu
from jax.sharding import Mesh
from jax.sharding import PartitionSpec as P

DH = 128
STEPS = 50
GUIDE = 5.0
SHIFT_FACTOR = 5.0
NEG_FILL = -1e30
EPSILON = 1e-06
SIDE = 4
TOK = 512
ROWS, TCOLS = 16, 32
PATCH = 64
CHUNK = 2 * PATCH + 16
LOG2_SCALE = math.log2(math.e) / math.sqrt(DH)

VMEM = pl.BlockSpec(memory_space=pltpu.VMEM)
SMEM = pl.BlockSpec(memory_space=pltpu.SMEM)
HBM = pl.BlockSpec(memory_space=pltpu.HBM)
ANY = pl.BlockSpec(memory_space=pl.ANY)


def in_hbm(value):
    return pltpu.with_memory_space_constraint(value, pltpu.HBM)


def noise_level(timestep, total_steps):
    frac = 1.0 - timestep.astype(jnp.float32) / total_steps
    return SHIFT_FACTOR * frac / (1.0 + (SHIFT_FACTOR - 1.0) * frac)


def ring(steps):
    return [(i, (i + steps) % SIDE) for i in range(SIDE)]


def crossed(mask):
    return [(i, i ^ mask) for i in range(SIDE)]


def moved(steps):
    count = SIDE * SIDE
    return [(i, i + steps) for i in range(count) if 0 <= i + steps < count]


def prepare_kernel(keys_ref, values_ref, out_ref, values, both, sems):
    first = pltpu.make_async_copy(keys_ref, both.at[pl.ds(0, TOK)], sems.at[0])
    second = pltpu.make_async_copy(values_ref, values, sems.at[1])
    first.start()
    second.start()
    second.wait()
    for half in range(2):
        at = half * 2 * DH
        both[TOK + at : TOK + at + 2 * DH] = jnp.transpose(values[at : at + 2 * DH])
    first.wait()
    third = pltpu.make_async_copy(both, out_ref, sems.at[0])
    third.start()
    third.wait()


def prepared(keys, values):
    return pl.pallas_call(
        prepare_kernel,
        out_shape=pltpu.HBM((2 * TOK, 2 * DH), jnp.bfloat16),
        in_specs=[HBM] * 2,
        out_specs=HBM,
        scratch_shapes=[
            pltpu.VMEM((TOK, 2 * DH), jnp.bfloat16),
            pltpu.VMEM((2 * TOK, 2 * DH), jnp.bfloat16),
            pltpu.SemaphoreType.DMA((2,)),
        ],
    )(in_hbm(keys), in_hbm(values))


def attention_kernel(count_ref, *refs, nq, nk, nx):
    refs = list(refs)

    def take(size):
        taken = refs[:size]
        del refs[:size]
        return taken

    q_refs, kv_refs = take(nq), take(nk)
    weight_hbm = take(1 + nx)[0]
    chunk_refs = take(nq)
    qs, ks, vs, scores, sems, acc_ref, top_ref, denom, weight_ref = refs

    sem = iter(range(64))

    def copied(source, target):
        copy = pltpu.make_async_copy(source, target, sems.at[next(sem)])
        copy.start()
        return copy

    arriving = []
    for b in range(nk):
        keys, values = kv_refs[b].at[pl.ds(0, TOK)], kv_refs[b].at[pl.ds(TOK, TOK)]
        group = [copied(keys, ks.at[b])]
        for half in range(2):
            for h in range(2):
                group.append(
                    copied(
                        values.at[pl.ds(half * 2 * DH + h * DH, DH)],
                        vs.at[b, h, pl.ds(0, DH), pl.ds(half * 2 * DH, 2 * DH)],
                    )
                )
        if b == 0:
            group += [copied(q_refs[j], qs.at[j]) for j in range(nq)]
        arriving.append(group)
    arriving[0].append(copied(weight_hbm, weight_ref))
    top_ref[...] = jnp.full((nq, 2, TOK), NEG_FILL, jnp.float32)
    denom[...] = jnp.zeros((nq, 2, TOK), jnp.float32)
    acc_ref[...] = jnp.zeros((nq, 2, DH, TOK), jnp.float32)
    for b in range(nk):
        for h in range(2):
            vs[b, h, DH:] = jnp.ones((16, TOK), jnp.bfloat16)
    for copy in arriving[0]:
        copy.wait()

    def scored(j, b, h):
        return lax.dot_general(
            ks[b, :, h * DH : (h + 1) * DH],
            qs[j, :, h * DH : (h + 1) * DH],
            (((1,), (1,)), ((), ())),
            preferred_element_type=jnp.float32,
        )

    def folded(j, b, h, score, masked):
        if masked:
            valid = lax.broadcasted_iota(jnp.int32, (TOK, TOK), 0) < count_ref[b]
            score = jnp.where(valid, score, NEG_FILL)
        old = top_ref[j, h : h + 1]
        new = jnp.maximum(old, jnp.max(score, axis=0, keepdims=True))
        weights = jnp.exp2((score - new) * LOG2_SCALE)
        if masked:
            weights = jnp.where(valid, weights, 0.0)
        factor = jnp.exp2((old - new) * LOG2_SCALE)
        top_ref[j, h : h + 1] = new
        mixed = jnp.dot(vs[b, h], weights.astype(jnp.bfloat16), preferred_element_type=jnp.float32)
        denom[j, h : h + 1] = denom[j, h : h + 1] * factor + mixed[DH : DH + 1]
        acc_ref[j, h] = acc_ref[j, h] * factor + mixed[:DH]

    total = nq * nk

    def step(t, _):
        j, b = lax.div(t, nk), lax.rem(t, nk)
        later = jnp.minimum(t + 1, total - 1)
        next_j, next_b = lax.div(later, nk), lax.rem(later, nk)
        count = count_ref[b]
        for needed in range(1, nk):

            @pl.when(t == needed - 1)
            def _():
                for copy in arriving[needed]:
                    copy.wait()

        def update(masked):
            scores[1] = scored(j, b, 1)
            folded(j, b, 0, scores[0], masked)
            scores[0] = scored(next_j, next_b, 0)
            folded(j, b, 1, scores[1], masked)

        @pl.when(count >= TOK)
        def _():
            update(False)

        @pl.when((count > 0) & (count < TOK))
        def _():
            update(True)

        @pl.when(count <= 0)
        def _():
            scores[0] = scored(next_j, next_b, 0)

        return 0

    scores[0] = scored(0, 0, 0)
    lax.fori_loop(0, total, step, 0)
    for j in range(nq):
        parts, rows = [], []
        for h in range(2):
            mixed = (acc_ref[j, h] * (1.0 / denom[j, h : h + 1])).astype(jnp.bfloat16)
            parts.append(jnp.dot(weight_ref[h], mixed, preferred_element_type=jnp.float32))
            stat = top_ref[j, h : h + 1] * LOG2_SCALE + jnp.log2(denom[j, h : h + 1])
            for _ in range(3):
                piece = stat.astype(jnp.bfloat16).astype(jnp.float32)
                rows.append(piece)
                stat = stat - piece
        blank = jnp.zeros((CHUNK - 2 * PATCH - 6, TOK), jnp.float32)
        chunk_refs[j][...] = jnp.concatenate(parts + rows + [blank], 0).astype(jnp.bfloat16)


def attend(counts, queries, blocks, weight, extras=()):
    f32, bf16 = jnp.float32, jnp.bfloat16
    nq, nk = len(queries), len(blocks)
    work = nq * nk * 2 * TOK * TOK
    return pl.pallas_call(
        functools.partial(attention_kernel, nq=nq, nk=nk, nx=len(extras)),
        out_shape=(jax.ShapeDtypeStruct((CHUNK, TOK), bf16),) * nq,
        in_specs=[SMEM] + [ANY] * (nq + nk + 1 + len(extras)),
        out_specs=(VMEM,) * nq,
        scratch_shapes=[
            pltpu.VMEM((nq, TOK, 2 * DH), bf16),
            pltpu.VMEM((nk, TOK, 2 * DH), bf16),
            pltpu.VMEM((nk, 2, DH + 16, TOK), bf16),
            pltpu.VMEM((2, TOK, TOK), f32),
            pltpu.SemaphoreType.DMA((5 * nk + nq + 1,)),
            pltpu.VMEM((nq, 2, DH, TOK), f32),
            pltpu.VMEM((nq, 2, TOK), f32),
            pltpu.VMEM((nq, 2, TOK), f32),
            pltpu.VMEM((2, PATCH, DH), bf16),
        ],
        compiler_params=pltpu.CompilerParams(vmem_limit_bytes=24 * 2**20),
        cost_estimate=pl.CostEstimate(
            flops=work * DH * 4, transcendentals=work, bytes_accessed=(nq + 2 * nk) * TOK * 4 * DH
        ),
    )(counts, *queries, *blocks, weight, *extras)


def combine_kernel(scale_ref, place_ref, *refs):
    chunk_refs, (latent_ref, out_ref) = refs[:4], refs[4:]
    stats = []
    for h in range(2):
        base = 2 * PATCH + 3 * h
        pieces = [ref[2 * PATCH :].astype(jnp.float32) for ref in chunk_refs]
        at = base - 2 * PATCH
        stats.append([x[at : at + 1] + x[at + 1 : at + 2] + x[at + 2 : at + 3] for x in pieces])
    values = jnp.zeros((PATCH, TOK), jnp.float32)
    for h in range(2):
        peak = jnp.maximum(
            jnp.maximum(stats[h][0], stats[h][1]), jnp.maximum(stats[h][2], stats[h][3])
        )
        shares = [jnp.exp2(stat - peak) for stat in stats[h]]
        norm = scale_ref[0] / (shares[0] + shares[1] + shares[2] + shares[3])
        for ref, share in zip(chunk_refs, shares):
            values += ref[h * PATCH : (h + 1) * PATCH].astype(jnp.float32) * (share * norm)
    values = jnp.transpose(jnp.concatenate([values[32:], values, values[:32]], 0))
    values = values.reshape(ROWS, TCOLS, 128)
    lane = lax.broadcasted_iota(jnp.int32, (ROWS, TCOLS, 128), 2)
    blank = jnp.zeros((1, TCOLS, 128), jnp.float32)
    above = jnp.concatenate([blank, values[:-1]], 0)
    below = jnp.concatenate([values[1:], blank], 0)
    window = jnp.where(lane < 32, above, jnp.where(lane < 96, values, below))
    for row in range(ROWS):
        out_ref[row] = window[row].astype(jnp.bfloat16)
    band = place_ref[0]
    edge = pltpu.roll(latent_ref[...], 64, 1) * scale_ref[1]
    lane = lax.broadcasted_iota(jnp.int32, (TCOLS, 128), 1)
    for target, part in ((band + 1, lane < 32), (band - 1, lane >= 96)):

        @pl.when((target >= 0) & (target < ROWS))
        def _():
            sent = jnp.where(part, edge, 0.0)
            out_ref[target] = (out_ref[target].astype(jnp.float32) + sent).astype(jnp.bfloat16)


def combine(scale, place, chunks, latent):
    return pl.pallas_call(
        combine_kernel,
        out_shape=jax.ShapeDtypeStruct((ROWS, TCOLS, 128), jnp.bfloat16),
        in_specs=[SMEM, SMEM] + [VMEM] * 5,
        out_specs=VMEM,
        compiler_params=pltpu.CompilerParams(vmem_limit_bytes=16 * 2**20),
    )(scale, place, *chunks, latent)


def laid_kernel(taps_hbm, bias_hbm, gain_hbm, _, even_ref, odd_ref, bias_ref, gain_ref, taps_ref, sems):
    copies = [
        pltpu.make_async_copy(taps_hbm, taps_ref, sems.at[0]),
        pltpu.make_async_copy(bias_hbm, bias_ref.at[0], sems.at[1]),
        pltpu.make_async_copy(gain_hbm, gain_ref.at[0], sems.at[2]),
    ]
    for copy in copies:
        copy.start()
    even_ref[...] = jnp.zeros(even_ref.shape, jnp.bfloat16)
    odd_ref[...] = jnp.zeros(odd_ref.shape, jnp.bfloat16)
    for copy in copies:
        copy.wait()
    for a in range(3):
        for u in range(3):
            for v in range(3):
                tap = taps_ref[a * 9 + u * 3 + v]
                for ref, place in ((even_ref, v + 1), (odd_ref, v)):
                    at = a * 256 + place // 2 * 128 + u * 32 + place % 2 * 16
                    ref[at : at + 16] = tap


def laid(taps, bias, gain, after):
    chans = taps.shape[-1]
    matrix = jax.ShapeDtypeStruct((768, chans), jnp.bfloat16)
    row = jax.ShapeDtypeStruct((1, chans), jnp.float32)
    return pl.pallas_call(
        laid_kernel,
        out_shape=(matrix, matrix, row, row),
        in_specs=[HBM] * 3 + [ANY],
        out_specs=(VMEM,) * 4,
        scratch_shapes=[pltpu.VMEM(taps.shape, taps.dtype), pltpu.SemaphoreType.DMA((3,))],
        compiler_params=pltpu.CompilerParams(vmem_limit_bytes=16 * 2**20),
    )(in_hbm(taps), in_hbm(bias), in_hbm(gain), after)


def decode_kernel(half_ref, own_ref, last_ref, older_ref, even_ref, odd_ref, bias_ref, gain_ref, out_ref):
    left = half_ref[0] == 0
    blank = jnp.zeros((1, 128), jnp.float32)
    even, odd = [], []
    for ref in (older_ref, last_ref, own_ref):
        block = ref[...].astype(jnp.float32)
        here = jnp.where(left, block[0:16], block[16:32])
        before = jnp.where(left, jnp.concatenate([blank, block[0:15]], 0), block[15:31])
        after = jnp.where(left, block[1:17], jnp.concatenate([block[17:32], blank], 0))
        rows = [
            jnp.concatenate([x, pltpu.roll(x, 96, 1)], 0).astype(jnp.bfloat16)
            for x in (before, here, after)
        ]
        even += rows[0:2]
        odd += rows[1:3]
    finished = []
    for parts, weight_ref in ((even, even_ref), (odd, odd_ref)):
        features = (
            jnp.dot(
                jnp.concatenate(parts, 1), weight_ref[...], preferred_element_type=jnp.float32
            )
            + bias_ref[...]
        )
        power = jnp.mean(features * features, axis=1, keepdims=True)
        scaled = features * lax.rsqrt(power + EPSILON) * gain_ref[...]
        finished.append((scaled / (1.0 + jnp.exp(-scaled))).astype(jnp.bfloat16))
    target = lax.broadcasted_iota(jnp.int32, (32, 32), 0)
    source = lax.broadcasted_iota(jnp.int32, (32, 32), 1)
    order = ((target & 1) * 16 + (target >> 1) == source).astype(jnp.float32).astype(jnp.bfloat16)
    for row in range(2):
        both = jnp.concatenate([x[row * 16 : row * 16 + 16] for x in finished], 0)
        out_ref[row] = jnp.dot(order, both, preferred_element_type=jnp.float32).astype(jnp.bfloat16)


def decode(half, own, last, older, even, odd, bias, gain):
    chans = bias.shape[1]
    return pl.pallas_call(
        decode_kernel,
        out_shape=jax.ShapeDtypeStruct((2, 32, chans), jnp.bfloat16),
        in_specs=[SMEM] + [VMEM] * 7,
        out_specs=VMEM,
        compiler_params=pltpu.CompilerParams(vmem_limit_bytes=32 * 2**20),
    )(half, own, last, older, even, odd, bias, gain)


def local(
    query, keys, values, lengths, timestep, latent, head_weight, conv_weight, conv_bias, gain
):
    cfg, zh, x = lax.axis_index("cfg"), lax.axis_index("zh"), lax.axis_index("x")
    y, zl = lax.axis_index("y"), lax.axis_index("zl")
    seq = ("y", "zl")

    own = prepared(keys[0], values[0])
    blocks = [own] + [lax.ppermute(own, "y", ring(d)) for d in (1, 3, 2)]
    queries = [query[0]] + [lax.ppermute(query[0], "zl", crossed(m)) for m in (1, 2, 3)]
    block = jnp.stack([((y - d) % SIDE) * SIDE + zl for d in (0, 1, 3, 2)])
    counts = jnp.clip(lengths[0] - block * TOK, 0, TOK).astype(jnp.int32)

    rows = latent[0].reshape(2, TCOLS, 32)
    blank = jnp.zeros((TCOLS, 32), jnp.float32)
    grid = jnp.concatenate([blank, rows[0], rows[1], blank], 1)
    part = lax.dynamic_slice_in_dim(head_weight, (zh * SIDE + x) * 2 * DH, 2 * DH, 0)
    weight = part.T.reshape(PATCH, 2, DH).transpose(1, 0, 2)
    sigma = noise_level(timestep[0], STEPS)
    scale = jnp.stack(
        [
            jnp.where(cfg == 0, GUIDE, 1.0 - GUIDE).astype(jnp.float32),
            jnp.where(cfg == 0, -1.0 / sigma, 0.0),
            sigma,
        ]
    )
    place = (zh * SIDE + x).astype(jnp.int32).reshape(1)

    third, second, first = attend(counts, queries[3:0:-1], blocks, weight)
    (mine,) = attend(counts, queries[:1], blocks, weight, extras=(third,))
    chunks = [mine] + [
        lax.ppermute(chunk, "zl", crossed(m)) for m, chunk in ((3, third), (2, second), (1, first))
    ]
    shares = combine(scale, place, chunks, grid)
    shares = lax.all_to_all(shares, ("zh", "x"), 0, 0, tiled=True)
    window = jnp.sum(shares.astype(jnp.float32), 0)
    window += lax.ppermute(window, "cfg", [(0, 1), (1, 0)])

    current = (grid - sigma * window).astype(jnp.bfloat16)
    last = lax.ppermute(current, seq, moved(1))
    older = lax.ppermute(current, seq, moved(2))
    cells = lax.dynamic_slice_in_dim(window, cfg * (TCOLS // 2), TCOLS // 2, 0)[:, 32:96]
    velocity = cells.reshape(TCOLS // 2, 2, 2, -1).transpose(1, 0, 2, 3).reshape(1, 2, TCOLS, -1)
    decoded = decode(
        cfg.astype(jnp.int32).reshape(1),
        current,
        last,
        older,
        *laid(conv_weight.reshape(27, *conv_weight.shape[3:]), conv_bias, gain, current),
    )
    return (velocity, decoded[None])


def solution(mesh):
    split = Mesh(
        mesh.devices.reshape(2, SIDE, SIDE, SIDE, SIDE), ("cfg", "zh", "x", "y", "zl")
    )
    seq, band = ("y", "zl"), ("zh", "x")
    tokens = P("cfg", seq, band)
    return jax.shard_map(
        local,
        mesh=split,
        in_specs=(
            tokens,
            tokens,
            tokens,
            P(),
            P(),
            P(seq, band, None, None),
            P(),
            P(),
            P(),
            P(),
        ),
        out_specs=(P(seq, band, "cfg", None), P(seq, band, "cfg", None)),
        check_vma=False,
    )
```
